32 devices in a mesh: pipe: 2 (over core), dp: 4 (over z), expert: 4 (over y, x).
Axes of the slice: x: 2, y: 2, z: 4, core: 2. Of those that a mesh axis runs over, the one named last changes fastest.
Arguments:
- section_input: bfloat16 [2, 2, 16, 64, 1536], P('pipe', None, ('dp', 'expert')), may hold values from -6 to 6
- out_grad: bfloat16 [2, 2, 16, 64, 1536], P('pipe', None, ('dp', 'expert')), may hold values from -6 to 6
- routes: int32 [2, 2, 16, 64, 2], P('pipe', None, ('dp', 'expert')), may hold values from 0 to 3, all different within a row; in each aligned block of 64 rows (0 to 63, 64 to 127, ..., all dimensions but the last counted through in order) at most 36 rows name the same one
- combine: float32 [2, 2, 16, 64, 2], P('pipe', None, ('dp', 'expert')), may hold values from 0.2 to 1
- kernel: float32 [2, 31, 1536], P('pipe'), may hold values from -1 to 1
- norm_gain: float32 [2, 1536], P('pipe'), may hold values from 0.5 to 1.5
- up_weight: bfloat16 [2, 4, 1536, 6144], P('pipe', 'expert', None, 'dp'), may hold values from -0.15625 to 0.15625
- down_weight: bfloat16 [2, 4, 6144, 1536], P('pipe', 'expert', 'dp'), may hold values from -0.078125 to 0.078125
Outputs:
- prev_grad: bfloat16 [2, 2, 16, 64, 1536], P('pipe', None, ('dp', 'expert'))
- kernel_grad: float32 [2, 31, 1536], P('pipe')
- gain_grad: float32 [2, 1536], P('pipe')
- up_grad: bfloat16 [2, 4, 1536, 6144], P('pipe', 'expert', None, 'dp')
- down_grad: bfloat16 [2, 4, 6144, 1536], P('pipe', 'expert', 'dp')
The draws below stay inside these ranges and needn't reach their ends.
Inputs may be any that keep to these rules, and one draw needn't show every extreme that they name: `routes`: within each sequence of one micro-batch of one section, no expert is named by more than 36 choices, a bound that some block reaches there in every draw; the 2 experts of a frame differ.
All inputs are finite; a program needn't handle non-finite values.
Results may differ from the reference program's by a relative error of at most 0.0066.
Values may be sent and summed in bfloat16 or wider, within the bound.
No kernel may reach another device: no remote copies, remote signals or barrier semaphores. Data moves between devices by JAX's collectives and lax.ppermute only.
A program may use at most 128 MiB of HBM per device.

```python
import math
from functools import partial
import jax
import jax.numpy as jnp
import numpy as np
from jax import lax

D = 1536
H = 6144
KW = 31
TOPK = 2
MB = 2
FRAMES = 64
SECTIONS = 2
SEQS = 16
EXPERTS = 4
CAP = 36


def shard_levels(key, shape, cuts, least, high):
    loudness = 1.0
    for dim, blocks in cuts:
        steps = jax.random.uniform(jax.random.fold_in(jax.random.fold_in(key, 6), dim), (blocks,), jnp.float32, least / len(cuts), high / len(cuts))
        loudness = loudness * jnp.repeat(jnp.exp(steps), shape[dim] // blocks).reshape((-1,) + (1,) * (len(shape) - 1 - dim))
    return loudness


def assign_block(rng, own, number, rows, amount, top, reach, slope):
    sequence = jax.random.permutation(rng, amount)
    crowded, common = portions_of(amount, rows * top, reach, slope, True), portions_of(amount, rows * top, reach, slope, False)
    places = jnp.arange(amount)

    def named(lengths, turn):
        used = int((lengths > 0).sum())
        fixed = max(1, used // 4)
        moved = fixed + (places - fixed + turn * (used - fixed)) % max(1, amount - fixed)
        return jnp.zeros((amount,), jnp.int32).at[sequence[jnp.where(places < fixed, places, moved)]].set(jnp.asarray(lengths, jnp.int32))

    lengths = jnp.where(number % 4 == 0, named(crowded, number // 4), named(common, number - number // 4 - 1))
    mixed = jax.random.permutation(jax.random.fold_in(own, 3), amount)
    donor, sink = mixed[0:amount // 2 * 2:2], mixed[1:amount // 2 * 2:2]
    slack = jnp.minimum(lengths[donor] - 1, reach - lengths[sink]) // 2
    slack = jnp.where((donor == sequence[0]) | (sink == sequence[0]) | (lengths[sink] == 0), 0, jnp.maximum(slack, 0))
    moved = jax.random.randint(jax.random.fold_in(own, 4), (amount // 2,), 0, 1 << 20) % (slack + 1)
    lengths = lengths.at[donor].add(-moved).at[sink].add(moved)
    labels = jnp.searchsorted(jnp.cumsum(lengths), jnp.arange(rows * top), side="right").astype(jnp.int32)
    listing = labels.reshape(top, rows).T
    listing = listing[jax.random.permutation(jax.random.fold_in(own, 1), rows)]
    turn = jax.random.randint(jax.random.fold_in(own, 2), (rows, 1), 0, top)
    return jnp.take_along_axis(listing, (jnp.arange(top)[None, :] + turn) % top, axis=1)


def portions_of(number_of, total, most, lean, full):
    portions = [(1 << 20) // math.isqrt(standing ** lean) + 1 for standing in range(1, number_of + 1)]
    largest = most if full else min(most, max(-(-total // number_of), total * portions[0] // sum(portions)))
    least = 1 if total - largest >= number_of - 1 else 0
    given, surplus = [largest] + [least] * (number_of - 1), total - largest - least * (number_of - 1)
    while surplus > 0:
        candidates = [i for i in range(1, number_of) if given[i] < largest] or [i for i in range(1, number_of) if given[i] < most]
        pool, budget = sum([portions[i] for i in candidates]), surplus
        for i in candidates:
            more = min(most - given[i], max(1, budget * portions[i] // pool), surplus)
            given[i] = given[i] + more
            surplus = surplus - more
    return np.array(given)


def normal_values(key, dims, scale, bound, shards=(), kind=jnp.bfloat16):
    factor_of = shard_levels(key, dims, shards, -0.22, 0.18) if shards else 1.0
    values = jax.random.normal(key, dims, jnp.float32) * scale * factor_of
    return jnp.minimum(jnp.maximum(values, -bound), bound).astype(kind)


def setup_inputs(seed: int = 0) -> dict:
    arg_keys = jax.random.split(jax.random.key(seed), 9)
    section_input = normal_values(arg_keys[0], (SECTIONS, MB, SEQS, FRAMES, D), 1.0, 6.0, ((0, 2), (2, 16)))
    out_grad = normal_values(arg_keys[1], (SECTIONS, MB, SEQS, FRAMES, D), 1.0, 6.0, ((0, 2), (2, 16)))
    routes_keys = jax.random.split(jax.random.fold_in(arg_keys[2], 1), SECTIONS * MB * SEQS * FRAMES // FRAMES)
    routes_turns = jax.random.permutation(jax.random.fold_in(arg_keys[2], 3), SECTIONS * MB * SEQS * FRAMES // FRAMES)
    routes = jax.vmap(lambda own, number: assign_block(jax.random.fold_in(arg_keys[2], 2), own, number, FRAMES, EXPERTS, TOPK, CAP, 2))(routes_keys, routes_turns).reshape((SECTIONS, MB, SEQS, FRAMES, TOPK))
    combine = jnp.clip(0.2 + 0.8 * jax.random.uniform(arg_keys[3], (SECTIONS, MB, SEQS, FRAMES, TOPK), jnp.float32) ** shard_levels(arg_keys[3], (SECTIONS, MB, SEQS, FRAMES, TOPK), ((0, 2), (2, 16)), -0.2, 0.2), 0.2, 1.0)
    kernel = normal_values(arg_keys[4], (SECTIONS, KW, D), KW ** -0.5, 1.0, ((0, 2),), jnp.float32)
    norm_gain = jnp.clip(1.0 + 0.1 * jax.random.normal(arg_keys[5], (SECTIONS, D), jnp.float32), 0.5, 1.5)
    up_weight = normal_values(arg_keys[6], (SECTIONS, EXPERTS, D, H), D ** -0.5, 0.15625, ((0, 2), (1, 4), (3, 4)))
    down_weight = normal_values(arg_keys[7], (SECTIONS, EXPERTS, H, D), H ** -0.5, 0.078125, ((0, 2), (1, 4), (2, 4)))
    return dict(section_input=section_input, out_grad=out_grad, routes=routes, combine=combine, kernel=kernel, norm_gain=norm_gain, up_weight=up_weight, down_weight=down_weight)


EPSILON = 1e-06

def silu_slope(values):
    gate_sig = jax.nn.sigmoid(values)
    return gate_sig * (1.0 + values * (1.0 - gate_sig))

def pad_frames(frames, margin):
    widths = [(0, 0)] * (frames.ndim - 2) + [(margin, margin), (0, 0)]
    return jnp.pad(frames, widths)

def depthwise(frames, conv_taps):
    tap_count = conv_taps.shape[0]
    margin = tap_count // 2
    length = frames.shape[-2]
    padded = pad_frames(frames, margin)
    result = jnp.zeros(frames.shape, jnp.float32)
    for offset in range(tap_count):
        result = result + conv_taps[offset] * lax.slice_in_dim(padded, offset, offset + length, axis=frames.ndim - 2)
    return result

def depthwise_transpose(grad_rows, conv_taps):
    tap_count = conv_taps.shape[0]
    margin = tap_count // 2
    length = grad_rows.shape[-2]
    padded = pad_frames(grad_rows, margin)
    result = jnp.zeros(grad_rows.shape, jnp.float32)
    for offset in range(tap_count):
        first = 2 * margin - offset
        result = result + conv_taps[offset] * lax.slice_in_dim(padded, first, first + length, axis=grad_rows.ndim - 2)
    return result

def depthwise_taps_grad(grad_rows, frames, tap_count):
    margin = tap_count // 2
    length = frames.shape[-2]
    padded = pad_frames(frames, margin)
    tap_rows = []
    for offset in range(tap_count):
        shifted = lax.slice_in_dim(padded, offset, offset + length, axis=frames.ndim - 2)
        tap_rows.append(lax.optimization_barrier(jnp.sum(grad_rows * shifted, axis=tuple(range(frames.ndim - 1)))))
    return jnp.stack(tap_rows)

def slot_targets(route_rows, experts, capacity):
    flat_ids = route_rows.reshape(-1).astype(jnp.int32)
    onehot = (flat_ids[:, None] == jnp.arange(experts, dtype=jnp.int32)[None, :]).astype(jnp.int32)
    rank_run = jnp.cumsum(onehot, axis=0) - 1
    slot_index = lax.optimization_barrier(jnp.sum(onehot * rank_run, axis=1))
    return (flat_ids * capacity + slot_index).astype(jnp.int32)

def expert_terms(operands):
    rows_in, rows_grad, up_mat, down_mat = operands
    pre_act = jnp.dot(rows_in, up_mat, preferred_element_type=jnp.float32)
    activated = jax.nn.silu(pre_act).astype(jnp.bfloat16)
    down_term = jnp.dot(activated.T, rows_grad, preferred_element_type=jnp.float32)
    act_grad = jnp.dot(rows_grad, down_mat.T, preferred_element_type=jnp.float32)
    pre_grad = (act_grad * silu_slope(pre_act)).astype(jnp.bfloat16)
    up_term = jnp.dot(rows_in.T, pre_grad, preferred_element_type=jnp.float32)
    slot_grad = jnp.dot(pre_grad, up_mat.T, preferred_element_type=jnp.float32).astype(jnp.bfloat16)
    return (up_term, down_term, slot_grad)

def reference(section_input, out_grad, routes, combine, kernel, norm_gain, up_weight, down_weight):
    total_slots = EXPERTS * CAP
    previous = [None] * SECTIONS
    kernel_list = []
    gain_list = []
    up_list = []
    down_list = []
    targeting = jax.vmap(partial(slot_targets, experts=EXPERTS, capacity=CAP))
    for section_index in range(SECTIONS):
        conv_taps = kernel[section_index]
        gain_vec = norm_gain[section_index]
        taps_sum = jnp.zeros((KW, D), jnp.float32)
        gain_sum = jnp.zeros((D,), jnp.float32)
        up_sum = jnp.zeros((EXPERTS, D, H), jnp.float32)
        down_sum = jnp.zeros((EXPERTS, H, D), jnp.float32)
        handed = []
        for micro_step in range(MB):
            inputs = section_input[section_index, micro_step].astype(jnp.float32)
            conv_out = depthwise(inputs, conv_taps)
            mixed = inputs + jax.nn.silu(conv_out)
            scale_inv = lax.rsqrt(lax.optimization_barrier(jnp.mean(mixed * mixed, axis=-1, keepdims=True)) + EPSILON)
            normed = (mixed * scale_inv * gain_vec).astype(jnp.bfloat16)
            upstream = out_grad[section_index, micro_step].astype(jnp.float32)
            weighted = (combine[section_index, micro_step][..., None] * upstream[:, :, None, :]).astype(jnp.bfloat16)
            copies = jnp.broadcast_to(normed[:, :, None, :], weighted.shape).reshape(SEQS, FRAMES * TOPK, D)
            weighted = weighted.reshape(SEQS, FRAMES * TOPK, D)
            targets = targeting(routes[section_index, micro_step])
            placing = (jnp.arange(total_slots, dtype=jnp.int32)[None, :, None] == targets[:, None, :]).astype(jnp.float32)
            send_in = jnp.einsum('sra,sad->srd', placing, copies.astype(jnp.float32)).astype(jnp.bfloat16)
            send_grad = jnp.einsum('sra,sad->srd', placing, weighted.astype(jnp.float32)).astype(jnp.bfloat16)
            rows_in = send_in.reshape(SEQS, EXPERTS, CAP, D).transpose(1, 0, 2, 3).reshape(EXPERTS, SEQS * CAP, D)
            rows_grad = send_grad.reshape(SEQS, EXPERTS, CAP, D).transpose(1, 0, 2, 3).reshape(EXPERTS, SEQS * CAP, D)
            up_term, down_term, slot_grad = lax.map(expert_terms, (rows_in, rows_grad, up_weight[section_index], down_weight[section_index]))
            up_sum = up_sum + up_term
            down_sum = down_sum + down_term
            back_rows = slot_grad.reshape(EXPERTS, SEQS, CAP, D).transpose(1, 0, 2, 3).reshape(SEQS, total_slots, D)
            gathered = jnp.einsum('sra,srd->sad', placing, back_rows.astype(jnp.float32))
            norm_grad = lax.optimization_barrier(jnp.sum(gathered.reshape(SEQS, FRAMES, TOPK, D), axis=2))
            gain_sum = gain_sum + lax.optimization_barrier(jnp.sum(norm_grad * mixed * scale_inv, axis=(0, 1)))
            scaled = norm_grad * gain_vec
            mixed_grad = upstream + scale_inv * scaled - mixed * scale_inv ** 3 * lax.optimization_barrier(jnp.mean(scaled * mixed, axis=-1, keepdims=True))
            conv_grad = mixed_grad * silu_slope(conv_out)
            taps_sum = taps_sum + depthwise_taps_grad(conv_grad, inputs, KW)
            handed.append((mixed_grad + depthwise_transpose(conv_grad, conv_taps)).astype(jnp.bfloat16))
        previous[(section_index - 1) % SECTIONS] = jnp.stack(handed)
        kernel_list.append(taps_sum)
        gain_list.append(gain_sum)
        up_list.append(up_sum.astype(jnp.bfloat16))
        down_list.append(down_sum.astype(jnp.bfloat16))
    return (jnp.stack(previous), jnp.stack(kernel_list), jnp.stack(gain_list), jnp.stack(up_list), jnp.stack(down_list))
```

```python
import functools

import jax
import jax.numpy as jnp
from jax import lax
from jax.experimental import pallas as pl
from jax.experimental.pallas import tpu as pltpu
from jax.sharding import PartitionSpec as P

MB = 2
EPSILON = 1e-06
LANES = 128
TILE = 256
VMEM_LIMIT = 60 * 1024 * 1024
bf16 = jnp.bfloat16
f32 = jnp.float32


def round_up(value, step):
    return -(-value // step) * step


def params():
    return pltpu.CompilerParams(vmem_limit_bytes=VMEM_LIMIT)


def whole(count):
    return [pl.BlockSpec(memory_space=pltpu.VMEM)] * count


def sigmoid(values):
    return 1.0 / (1.0 + jnp.exp(-values))


def silu_slope(values):
    gate_sig = sigmoid(values)
    return gate_sig * (1.0 + values * (1.0 - gate_sig))


def prologue_body(x_ref, taps_ref, gain_ref, normed_ref, conv_ref, mixed_ref, scale_ref, pad):
    frames, features = x_ref.shape
    tap_count = taps_ref.shape[0]
    margin = tap_count // 2
    lead = round_up(margin, 8)
    pad[...] = jnp.zeros(pad.shape, f32)

    def chunk(c, squares):
        cols = pl.ds(pl.multiple_of(c * LANES, LANES), LANES)
        xs = x_ref[:, cols].astype(f32)
        pad[lead : lead + frames, :] = xs
        acc = jnp.zeros((frames, LANES), f32)
        for j in range(tap_count):
            first = lead + j - margin
            acc = acc + taps_ref[j : j + 1, cols] * pad[first : first + frames, :]
        mixed = xs + acc * sigmoid(acc)
        conv_ref[:, cols] = acc
        mixed_ref[:, cols] = mixed
        return squares + mixed * mixed

    squares = lax.fori_loop(0, features // LANES, chunk, jnp.zeros((frames, LANES), f32))
    scale = lax.rsqrt(jnp.sum(squares, axis=1, keepdims=True) / features + EPSILON)
    scale_ref[...] = scale
    normed_ref[...] = (mixed_ref[...] * scale * gain_ref[...]).astype(bf16)


def prologue(x, taps, gain):
    frames, features = x.shape
    lead = round_up(taps.shape[0] // 2, 8)
    return pl.pallas_call(
        prologue_body,
        out_shape=(
            jax.ShapeDtypeStruct((frames, features), bf16),
            jax.ShapeDtypeStruct((frames, features), f32),
            jax.ShapeDtypeStruct((frames, features), f32),
            jax.ShapeDtypeStruct((frames, 1), f32),
        ),
        in_specs=whole(3),
        out_specs=tuple(whole(4)),
        scratch_shapes=[pltpu.VMEM((frames + 2 * lead, LANES), f32)],
        compiler_params=params(),
        cost_estimate=pl.CostEstimate(flops=4000000, bytes_accessed=2000000, transcendentals=0),
        name="conv_norm",
    )(x, taps, gain)


def slot_rows_body(experts, capacity, frames, weigh, meta_ref, *refs):
    seqs = (len(refs) - experts - 1)
    frame_refs, out_refs, joined = refs[:seqs], refs[seqs : seqs + experts], refs[-1]
    for k in range(seqs):
        joined[k * frames : (k + 1) * frames, :] = frame_refs[k][...]
    total = seqs * frames
    padded = round_up(experts, 16)
    named = lax.broadcasted_iota(jnp.int32, (padded, total), 0).astype(f32)
    first, second = meta_ref[0:1, :] == named, meta_ref[1:2, :] == named
    member = (first | second)
    earlier = lax.broadcasted_iota(jnp.int32, (total, total), 0)
    later = lax.broadcasted_iota(jnp.int32, (total, total), 1)
    before = (earlier < later) & (earlier // frames == later // frames)
    rank = jnp.dot(
        member.astype(f32).astype(bf16),
        before.astype(f32).astype(bf16),
        preferred_element_type=f32,
    )
    seq_of = (lax.broadcasted_iota(jnp.int32, (padded, total), 1) // frames).astype(f32)
    slot = jnp.where(member, rank + seq_of * capacity, -1.0)
    weight = jnp.where(first, meta_ref[2:3, :], 0.0) + jnp.where(second, meta_ref[3:4, :], 0.0)
    rows = out_refs[0].shape[0]
    row_ids = lax.broadcasted_iota(jnp.int32, (rows, total), 0).astype(f32)
    for e in range(experts):
        chosen = row_ids == slot[e : e + 1, :]
        placing = chosen.astype(f32).astype(bf16)
        if weigh:
            amount = jnp.sum(jnp.where(chosen, weight[e : e + 1, :], 0.0), axis=1, keepdims=True)
        for first_col in range(0, joined.shape[1], 512):
            cols = slice(first_col, min(first_col + 512, joined.shape[1]))
            picked = jnp.dot(placing, joined[:, cols], preferred_element_type=f32)
            if weigh:
                picked = picked * amount
            out_refs[e][:, cols] = picked.astype(bf16)


def slot_rows(meta, blocks, experts, capacity, weigh):
    frames, features = blocks[0].shape
    rows = round_up(len(blocks) * capacity, 16)
    return pl.pallas_call(
        functools.partial(slot_rows_body, experts, capacity, frames, weigh),
        out_shape=tuple(jax.ShapeDtypeStruct((rows, features), bf16) for _ in range(experts)),
        in_specs=whole(1 + len(blocks)),
        out_specs=tuple(whole(experts)),
        scratch_shapes=[pltpu.VMEM((len(blocks) * frames, features), bf16)],
        compiler_params=params(),
        cost_estimate=pl.CostEstimate(flops=450000000, bytes_accessed=3000000, transcendentals=0),
        name="slot_rows",
    )(meta, *blocks)


def expert_body(parts, *refs):
    in_refs, grad_refs = refs[:parts], refs[parts : 2 * parts]
    up_ref, down_ref = refs[2 * parts : 2 * parts + 2]
    slot_refs = refs[2 * parts + 2 : 3 * parts + 2]
    rows_in, rows_grad, acted, pre_grad = refs[3 * parts + 2 :]
    rows = in_refs[0].shape[0]
    for j in range(parts):
        rows_in[j * rows : (j + 1) * rows, :] = in_refs[j][...]
        rows_grad[j * rows : (j + 1) * rows, :] = grad_refs[j][...]
    width = up_ref.shape[1]

    def hidden(h, carry):
        cols = pl.ds(pl.multiple_of(h * TILE, TILE), TILE)
        pre_act = jnp.dot(rows_in[...], up_ref[:, cols], preferred_element_type=f32)
        act_grad = lax.dot_general(
            rows_grad[...],
            down_ref[cols, :],
            (((1,), (1,)), ((), ())),
            preferred_element_type=f32,
        )
        gate_sig = sigmoid(pre_act)
        acted[:, cols] = (pre_act * gate_sig).astype(bf16)
        slope = gate_sig * (1.0 + pre_act * (1.0 - gate_sig))
        pre_grad[:, cols] = (act_grad * slope).astype(bf16)
        return carry

    lax.fori_loop(0, width // TILE, hidden, 0)

    def feature(d, carry):
        cols = pl.ds(pl.multiple_of(d * TILE, TILE), TILE)
        term = lax.dot_general(
            pre_grad[...],
            up_ref[cols, :],
            (((1,), (1,)), ((), ())),
            preferred_element_type=f32,
        )
        for j in range(parts):
            slot_refs[j][:, cols] = term[j * rows : (j + 1) * rows, :].astype(bf16)
        return carry

    lax.fori_loop(0, up_ref.shape[0] // TILE, feature, 0)


def expert_products(in_blocks, grad_blocks, up_mat, down_mat):
    parts = len(in_blocks)
    rows, features = in_blocks[0].shape
    hidden = up_mat.shape[1]
    total = parts * rows
    out = pl.pallas_call(
        functools.partial(expert_body, parts),
        out_shape=tuple(jax.ShapeDtypeStruct((rows, features), bf16) for _ in range(parts))
        + (
            jax.ShapeDtypeStruct((total, features), bf16),
            jax.ShapeDtypeStruct((total, features), bf16),
            jax.ShapeDtypeStruct((total, hidden), bf16),
            jax.ShapeDtypeStruct((total, hidden), bf16),
        ),
        in_specs=whole(2 * parts + 2),
        out_specs=tuple(whole(parts + 4)),
        compiler_params=params(),
        cost_estimate=pl.CostEstimate(
            flops=6 * total * features * hidden, bytes_accessed=20000000, transcendentals=total * hidden
        ),
        name="expert_products",
    )(*in_blocks, *grad_blocks, up_mat, down_mat)
    return out[:parts], out[parts:]


def frame_sums_body(experts, seqs, capacity, frames, meta_ref, *refs):
    slot_refs, out_refs, picking = refs[:experts], refs[experts : experts + seqs], refs[-1]
    total = seqs * frames
    padded = round_up(experts, 128)
    named = lax.broadcasted_iota(jnp.int32, (total, padded), 1).astype(f32)
    member = (meta_ref[:, 0:1] == named) | (meta_ref[:, 1:2] == named)
    later = lax.broadcasted_iota(jnp.int32, (total, total), 0)
    earlier = lax.broadcasted_iota(jnp.int32, (total, total), 1)
    before = (earlier < later) & (earlier // frames == later // frames)
    rank = jnp.dot(
        before.astype(f32).astype(bf16),
        member.astype(f32).astype(bf16),
        preferred_element_type=f32,
    )
    seq_of = (lax.broadcasted_iota(jnp.int32, (total, padded), 0) // frames).astype(f32)
    slot = jnp.where(member, rank + seq_of * capacity, -1.0)
    rows = slot_refs[0].shape[0]
    col_ids = lax.broadcasted_iota(jnp.int32, (total, rows), 1).astype(f32)
    for e in range(experts):
        picking[e] = (col_ids == slot[:, e : e + 1]).astype(f32).astype(bf16)

    def feature(d, carry):
        cols = pl.ds(pl.multiple_of(d * TILE, TILE), TILE)
        acc = jnp.zeros((total, TILE), f32)
        for e in range(experts):
            acc = acc + jnp.dot(picking[e], slot_refs[e][:, cols], preferred_element_type=f32)
        for k in range(seqs):
            out_refs[k][:, cols] = acc[k * frames : (k + 1) * frames, :].astype(out_refs[k].dtype)
        return carry

    lax.fori_loop(0, slot_refs[0].shape[1] // TILE, feature, 0)


def frame_sums(meta, blocks, seqs, capacity):
    rows, features = blocks[0].shape
    frames = meta.shape[0] // seqs
    return pl.pallas_call(
        functools.partial(frame_sums_body, len(blocks), seqs, capacity, frames),
        out_shape=tuple(
            jax.ShapeDtypeStruct((frames, features), f32 if k == 0 else bf16) for k in range(seqs)
        ),
        in_specs=whole(1 + len(blocks)),
        out_specs=tuple(whole(seqs)),
        scratch_shapes=[pltpu.VMEM((len(blocks), seqs * frames, rows), bf16)],
        compiler_params=params(),
        cost_estimate=pl.CostEstimate(flops=450000000, bytes_accessed=3000000, transcendentals=0),
        name="frame_sums",
    )(meta, *blocks)


def epilogue_body(seqs, *refs):
    norm_refs = refs[:seqs]
    (x_ref, up_ref, conv_ref, mixed_ref, scale_ref, taps_ref, gain_ref, sums_ref) = refs[seqs : seqs + 8]
    prev_ref, term_ref, norm_grad, pad_x, pad_g = refs[seqs + 8 :]
    frames, features = x_ref.shape
    tap_count = taps_ref.shape[0]
    margin = tap_count // 2
    lead = round_up(margin, 8)
    pad_x[...] = jnp.zeros(pad_x.shape, f32)
    pad_g[...] = jnp.zeros(pad_g.shape, f32)
    scale = scale_ref[...]

    def gather(c, inner):
        cols = pl.ds(pl.multiple_of(c * LANES, LANES), LANES)
        grad = norm_refs[0][:, cols].astype(f32)
        for k in range(1, seqs):
            grad = grad + norm_refs[k][:, cols].astype(f32)
        norm_grad[:, cols] = grad
        weighed = grad * mixed_ref[:, cols]
        term_ref[tap_count : tap_count + 1, cols] = sums_ref[
            tap_count : tap_count + 1, cols
        ] + jnp.sum(weighed * scale, axis=0, keepdims=True)
        return inner + weighed * gain_ref[:, cols]

    inner = lax.fori_loop(0, features // LANES, gather, jnp.zeros((frames, LANES), f32))
    pull = scale * scale * scale * (jnp.sum(inner, axis=1, keepdims=True) / features)

    def chunk(c, carry):
        cols = pl.ds(pl.multiple_of(c * LANES, LANES), LANES)
        mixed_grad = (
            up_ref[:, cols].astype(f32)
            + scale * (norm_grad[:, cols] * gain_ref[:, cols])
            - mixed_ref[:, cols] * pull
        )
        conv_grad = mixed_grad * silu_slope(conv_ref[:, cols])
        pad_x[lead : lead + frames, :] = x_ref[:, cols].astype(f32)
        pad_g[lead : lead + frames, :] = conv_grad
        acc = mixed_grad
        for j in range(tap_count):
            first = lead + j - margin
            term_ref[j : j + 1, cols] = sums_ref[j : j + 1, cols] + jnp.sum(
                conv_grad * pad_x[first : first + frames, :], axis=0, keepdims=True
            )
            first = lead + margin - j
            acc = acc + taps_ref[j : j + 1, cols] * pad_g[first : first + frames, :]
        prev_ref[:, cols] = acc.astype(bf16)
        return carry

    lax.fori_loop(0, features // LANES, chunk, 0)


def epilogue(norm_blocks, x, upstream, conv, mixed, scale, taps, gain, sums):
    frames, features = x.shape
    seqs = len(norm_blocks)
    lead = round_up(taps.shape[0] // 2, 8)
    return pl.pallas_call(
        functools.partial(epilogue_body, seqs),
        out_shape=(
            jax.ShapeDtypeStruct((frames, features), bf16),
            jax.ShapeDtypeStruct((taps.shape[0] + 1, features), f32),
        ),
        in_specs=whole(seqs + 8),
        out_specs=tuple(whole(2)),
        scratch_shapes=[
            pltpu.VMEM((frames, features), f32),
            pltpu.VMEM((frames + 2 * lead, LANES), f32),
            pltpu.VMEM((frames + 2 * lead, LANES), f32),
        ],
        compiler_params=params(),
        cost_estimate=pl.CostEstimate(flops=8000000, bytes_accessed=3000000, transcendentals=0),
        name="norm_conv_back",
    )(*norm_blocks, x, upstream, conv, mixed, scale, taps, gain, sums)


def to_partner(array, axis, k):
    return lax.ppermute(array, axis, [(i, i ^ k) for i in range(lax.axis_size(axis))])


def from_all(array, axis):
    return [array] + [to_partner(array, axis, k) for k in range(1, lax.axis_size(axis))]


def exchanged(blocks, axis):
    return [blocks[0]] + [to_partner(blocks[k], axis, k) for k in range(1, len(blocks))]


def tree_sum(terms):
    while len(terms) > 1:
        terms = [terms[i] + terms[i + 1] for i in range(0, len(terms), 2)]
    return terms[0]


def local(section_input, out_grad, routes, combine, kernel, norm_gain, up_weight, down_weight):
    experts = lax.axis_size("expert")
    seqs = lax.axis_size("dp")
    frames, features = section_input.shape[3:]
    top_count = routes.shape[4]
    capacity = 9 * frames * top_count // (8 * experts)
    taps = kernel[0]
    gain = norm_gain
    up_mat, down_mat = up_weight[0, 0], down_weight[0, 0]
    own = lax.axis_index("expert").astype(jnp.int32)

    relative = (routes[0, :, 0] ^ own).astype(f32)
    meta = jnp.concatenate([relative, combine[0, :, 0]], axis=2)
    metas = jnp.concatenate(from_all(meta, "dp"), axis=1)
    metas_wide = metas.transpose(0, 2, 1)

    xs = [section_input[0, m, 0] for m in range(MB)]
    ups = [out_grad[0, m, 0] for m in range(MB)]
    saved, rows_in, rows_grad = [], [], []
    for m in range(MB):
        normed, *rest = prologue(xs[m], taps, gain)
        saved.append(rest)
        rows_in.append(from_all(normed, "dp"))
        rows_grad.append(from_all(ups[m], "dp"))
    kept, back = [], []
    for m in range(MB):
        in_blocks = exchanged(slot_rows(metas_wide[m], rows_in[m], experts, capacity, False), "expert")
        grad_blocks = exchanged(slot_rows(metas_wide[m], rows_grad[m], experts, capacity, True), "expert")
        slots, rest = expert_products(in_blocks, grad_blocks, up_mat, down_mat)
        kept.append(rest)
        back.append(exchanged(slots, "expert"))
    handed = []
    sums = jnp.zeros((taps.shape[0] + 1, features), f32)
    for m in range(MB):
        norm_blocks = exchanged(frame_sums(metas[m], back[m], seqs, capacity), "dp")
        conv, mixed, scale = saved[m]
        prev, sums = epilogue(norm_blocks, xs[m], ups[m], conv, mixed, scale, taps, gain, sums)
        handed.append(
            lax.ppermute(prev, "pipe", [(i, (i - 1) % lax.axis_size("pipe")) for i in range(lax.axis_size("pipe"))])
        )
    all_in, all_grad, all_acted, all_pre = [jnp.concatenate(a, axis=0) for a in zip(*kept)]
    over_rows = (((0,), (0,)), ((), ()))
    up_grad = lax.dot_general(all_in, all_pre, over_rows, preferred_element_type=f32).astype(bf16)
    down_grad = lax.dot_general(all_acted, all_grad, over_rows, preferred_element_type=f32).astype(bf16)
    for axis in ("expert", "dp"):
        sums = tree_sum(from_all(sums, axis))
    return (
        jnp.stack(handed)[None, :, None],
        sums[:-1][None],
        sums[-1][None],
        up_grad[None, None],
        down_grad[None, None],
    )


def solution(mesh):
    split = P("pipe", None, ("dp", "expert"), None, None)
    up_split = P("pipe", "expert", None, "dp")
    down_split = P("pipe", "expert", "dp", None)
    return jax.shard_map(
        local,
        mesh=mesh,
        in_specs=(split, split, split, split, P("pipe", None, None), P("pipe", None), up_split, down_split),
        out_specs=(split, P("pipe", None, None), P("pipe", None), up_split, down_split),
        check_vma=False,
    )
```

```python
import functools

import jax
import jax.numpy as jnp
from jax import lax
from jax.experimental import pallas as pl
from jax.experimental.pallas import tpu as pltpu
from jax.sharding import PartitionSpec as P

MB = 2
EPSILON = 1e-06
LANES = 128
TILE = 512
PART = 256
GATE = -1
MIB = 1024 * 1024
SMALL = pl.CostEstimate(flops=1, bytes_accessed=1, transcendentals=0)
bf16 = jnp.bfloat16
f32 = jnp.float32


def round_up(value, step):
    return -(-value // step) * step


def params(mib):
    return pltpu.CompilerParams(vmem_limit_bytes=mib * MIB)


def whole(count):
    return [pl.BlockSpec(memory_space=pltpu.VMEM)] * count


def after(count):
    return [pl.BlockSpec(memory_space=pl.ANY)] * count


def far(count):
    return [pl.BlockSpec(memory_space=pltpu.HBM)] * count


def fetched(m, sources, targets, sems):
    copies = [
        pltpu.make_async_copy(source.at[m], target, sems.at[i])
        for i, (source, target) in enumerate(zip(sources, targets))
    ]
    for copy in copies:
        copy.start()
    for copy in copies:
        copy.wait()


def fetch_scratch(frames, features):
    return [
        pltpu.VMEM((frames, features), bf16),
        pltpu.VMEM((frames, features), bf16),
        pltpu.SemaphoreType.DMA((2,)),
    ]


def sigmoid(values):
    return 1.0 / (1.0 + jnp.exp(-values))


def silu_slope(values):
    gate_sig = sigmoid(values)
    return gate_sig * (1.0 + values * (1.0 - gate_sig))


def mixed_frames(x_ref, taps_ref, pad, conv_ref, mixed_ref):
    frames, features = x_ref.shape
    tap_count = taps_ref.shape[0]
    margin = tap_count // 2
    lead = round_up(margin, 8)
    pad[...] = jnp.zeros(pad.shape, f32)

    def chunk(c, squares):
        cols = pl.ds(pl.multiple_of(c * LANES, LANES), LANES)
        xs = x_ref[:, cols].astype(f32)
        pad[lead : lead + frames, :] = xs
        acc = jnp.zeros((frames, LANES), f32)
        for j in range(tap_count):
            first = lead + j - margin
            acc = acc + taps_ref[j, :, cols] * pad[first : first + frames, :]
        mixed = xs + acc * sigmoid(acc)
        if conv_ref is not None:
            conv_ref[:, cols] = acc
        mixed_ref[:, cols] = mixed
        return squares + mixed * mixed

    squares = lax.fori_loop(0, features // LANES, chunk, jnp.zeros((frames, LANES), f32))
    return lax.rsqrt(jnp.sum(squares, axis=1, keepdims=True) / features + EPSILON)


def meta_rows(routes_ref, combine_ref, m):
    own = lax.axis_index("expert").astype(jnp.int32)
    rows = [(routes_ref[m] ^ own).astype(f32)]
    left = combine_ref[m]
    for _ in range(3):
        rows.append(left.astype(bf16).astype(f32))
        left = left - rows[-1]
    return jnp.concatenate(rows, axis=0)


def first_send_body(x_all, up_all, routes_ref, combine_ref, taps_ref, gain_ref, send_ref, mixed, pad, x_ref, sems):
    frames = x_ref.shape[0]
    fetched(0, (x_all, up_all), (x_ref, send_ref.at[frames : 2 * frames]), sems)
    scale = mixed_frames(x_ref, taps_ref, pad, None, mixed)
    send_ref[:frames, :] = (mixed[...] * scale * gain_ref[...]).astype(bf16)
    meta = jnp.concatenate([meta_rows(routes_ref, combine_ref, m) for m in range(MB)], axis=0)
    send_ref[2 * frames :, :frames] = meta.astype(bf16)


def first_send(x, upstream, routes, combine, taps, gain):
    _, frames, features = x.shape
    lead = round_up(taps.shape[0] // 2, 8)
    return pl.pallas_call(
        first_send_body,
        out_shape=jax.ShapeDtypeStruct((2 * frames + 8 * MB, features), bf16),
        in_specs=far(2) + whole(4),
        out_specs=whole(1)[0],
        scratch_shapes=[
            pltpu.VMEM((frames, features), f32),
            pltpu.VMEM((frames + 2 * lead, LANES), f32),
            pltpu.VMEM((frames, features), bf16),
            pltpu.SemaphoreType.DMA((2,)),
        ],
        compiler_params=params(16),
        cost_estimate=SMALL,
        name="first_send",
    )(x, upstream, routes, combine, taps, gain)


def second_send_body(experts, capacity, x_all, up_all, routes_ref, combine_ref, taps_ref, gain_ref, _, *refs):
    outs, (mixed, pad, x_ref, joined, sems) = refs[:experts], refs[experts:]
    frames, features = x_ref.shape
    fetched(1, (x_all, up_all), (x_ref, joined.at[frames:]), sems)
    scale = mixed_frames(x_ref, taps_ref, pad, None, mixed)
    joined[:frames, :] = (mixed[...] * scale * gain_ref[...]).astype(bf16)
    slot, weight = slot_map(experts, capacity, frames, meta_rows(routes_ref, combine_ref, 1))
    rows = outs[0].shape[0]
    row_ids = lax.broadcasted_iota(jnp.int32, (rows, frames), 0).astype(f32)
    for e in range(experts):
        normed_row = (row_ids == slot[e : e + 1, :]).astype(f32).astype(bf16)
        chosen = (row_ids - capacity == slot[e : e + 1, :]) & (row_ids >= capacity)
        amount = jnp.sum(jnp.where(chosen, weight[e : e + 1, :], 0.0), axis=1, keepdims=True)
        grad_row = chosen.astype(f32).astype(bf16)
        for first_col in range(0, features, 512):
            cols = slice(first_col, min(first_col + 512, features))
            picked = jnp.dot(grad_row, joined[frames:, cols], preferred_element_type=f32) * amount
            picked = picked + jnp.dot(normed_row, joined[:frames, cols], preferred_element_type=f32)
            outs[e][:, cols] = picked.astype(bf16)


def second_send(x, upstream, routes, combine, taps, gain, experts, capacity, earlier):
    _, frames, features = x.shape
    lead = round_up(taps.shape[0] // 2, 8)
    rows = round_up(2 * capacity, 8)
    return pl.pallas_call(
        functools.partial(second_send_body, experts, capacity),
        out_shape=(jax.ShapeDtypeStruct((rows, features), bf16),) * experts,
        in_specs=far(2) + whole(4) + after(1),
        out_specs=tuple(whole(experts)),
        scratch_shapes=[
            pltpu.VMEM((frames, features), f32),
            pltpu.VMEM((frames + 2 * lead, LANES), f32),
            pltpu.VMEM((frames, features), bf16),
            pltpu.VMEM((2 * frames, features), bf16),
            pltpu.SemaphoreType.DMA((2,)),
        ],
        compiler_params=params(16),
        cost_estimate=SMALL,
        name="second_send",
    )(x, upstream, routes, combine, taps, gain, earlier)


def saved_body(x_ref, taps_ref, _, conv_ref, mixed_ref, scale_ref, pad):
    for m in range(MB):
        scale_ref[m] = mixed_frames(x_ref.at[m], taps_ref, pad, conv_ref.at[m], mixed_ref.at[m])


def saved_frames(x, taps, earlier):
    lead = round_up(taps.shape[0] // 2, 8)
    return pl.pallas_call(
        saved_body,
        out_shape=(
            jax.ShapeDtypeStruct(x.shape, f32),
            jax.ShapeDtypeStruct(x.shape, f32),
            jax.ShapeDtypeStruct(x.shape[:2] + (1,), f32),
        ),
        in_specs=whole(2) + after(1),
        out_specs=tuple(whole(3)),
        scratch_shapes=[pltpu.VMEM((x.shape[1] + 2 * lead, LANES), f32)],
        compiler_params=params(16),
        cost_estimate=SMALL,
        name="saved_frames",
    )(x, taps, earlier)


def stacked_body(*refs):
    for i, ref in enumerate(refs[:-2]):
        refs[-1][i] = ref[...]


def stacked(blocks, earlier):
    return pl.pallas_call(
        stacked_body,
        out_shape=jax.ShapeDtypeStruct((len(blocks),) + blocks[0].shape, blocks[0].dtype),
        in_specs=whole(len(blocks)) + after(1),
        out_specs=whole(1)[0],
        compiler_params=params(16),
        cost_estimate=SMALL,
        name="stacked",
    )(*blocks, earlier)


def slot_map(experts, capacity, frames, meta):
    total = meta.shape[1]
    padded = round_up(experts, 16)
    named = lax.broadcasted_iota(jnp.int32, (padded, total), 0).astype(f32)
    first, second = meta[0:1, :] == named, meta[1:2, :] == named
    member = first | second
    earlier = lax.broadcasted_iota(jnp.int32, (total, total), 0)
    later = lax.broadcasted_iota(jnp.int32, (total, total), 1)
    before = (earlier < later) & (earlier // frames == later // frames)
    rank = jnp.dot(
        member.astype(f32).astype(bf16),
        before.astype(f32).astype(bf16),
        preferred_element_type=f32,
    )
    seq_of = lax.broadcasted_iota(jnp.int32, (padded, total), 1) // frames
    slot = jnp.where(member, rank + (seq_of * capacity).astype(f32), -1.0)
    first_weight = meta[2:3, :] + meta[4:5, :] + meta[6:7, :]
    second_weight = meta[3:4, :] + meta[5:6, :] + meta[7:8, :]
    weight = jnp.where(first, first_weight, 0.0) + jnp.where(second, second_weight, 0.0)
    return slot, weight


def place(slot, weight, joined, out_ref, first_row, rows):
    row_ids = lax.broadcasted_iota(jnp.int32, (rows, slot.shape[1]), 0).astype(f32)
    chosen = row_ids == slot
    placing = chosen.astype(f32).astype(bf16)
    if weight is not None:
        amount = jnp.sum(jnp.where(chosen, weight, 0.0), axis=1, keepdims=True)
    for first_col in range(0, joined.shape[1], 512):
        cols = slice(first_col, min(first_col + 512, joined.shape[1]))
        picked = jnp.dot(placing, joined[:, cols], preferred_element_type=f32)
        if weight is not None:
            picked = picked * amount
        out_ref[first_row : first_row + rows, cols] = picked.astype(bf16)


def slots_body(experts, capacity, frames, *refs):
    seqs = len(refs) - experts - 3
    block_refs, out_refs = refs[:seqs], refs[seqs : seqs + experts]
    slot_ref, joined, meta = refs[seqs + experts :]
    total = seqs * frames
    for k in range(seqs):
        here = slice(k * frames, (k + 1) * frames)
        joined[here, :] = block_refs[k][:frames, :]
        joined[total + k * frames : total + (k + 1) * frames, :] = block_refs[k][frames : 2 * frames, :]
        meta[:, here] = block_refs[k][2 * frames :, :frames].astype(f32)
    slot, weight = slot_map(experts, capacity, frames, meta[:8, :])
    slot_ref[0] = slot
    slot_ref[1] = slot_map(experts, capacity, frames, meta[8:, :])[0]
    rows = out_refs[0].shape[0] // 2
    for e in range(experts):
        place(slot[e : e + 1, :], None, joined.at[:total], out_refs[e], 0, rows)
        place(slot[e : e + 1, :], weight[e : e + 1, :], joined.at[total:], out_refs[e], rows, rows)


def slots(blocks, experts, capacity, frames):
    features = blocks[0].shape[1]
    seqs = len(blocks)
    rows = round_up(seqs * capacity, 16)
    total = seqs * frames
    out = pl.pallas_call(
        functools.partial(slots_body, experts, capacity, frames),
        out_shape=tuple(jax.ShapeDtypeStruct((2 * rows, features), bf16) for _ in range(experts))
        + (jax.ShapeDtypeStruct((MB, round_up(experts, 16), total), f32),),
        in_specs=whole(seqs),
        out_specs=tuple(whole(experts + 1)),
        scratch_shapes=[pltpu.VMEM((2 * total, features), bf16), pltpu.VMEM((8 * MB, total), f32)],
        compiler_params=params(16),
        cost_estimate=SMALL,
        name="slots",
    )(*blocks)
    return out[:experts], out[experts]


def expert_body(parts, rows, capacity, count, *refs):
    in_refs, (up_far, down_far) = refs[:count], refs[count : count + 2]
    slot_refs, far_outs = refs[count + 2 : count + 2 + parts], refs[count + 2 + parts : count + 6 + parts]
    up_mat, down_mat, rows_in, rows_grad, acted, kept, get_sems, put_sems = refs[count + 6 + parts :]
    features, hidden = up_mat.shape
    steps = hidden // TILE

    def hidden_cols(h):
        return pl.ds(pl.multiple_of(h * TILE, TILE), TILE)

    def getting(h):
        cols = hidden_cols(h)
        return (
            pltpu.make_async_copy(up_far.at[:, cols], up_mat.at[:, cols], get_sems.at[0, h]),
            pltpu.make_async_copy(down_far.at[cols, :], down_mat.at[cols, :], get_sems.at[1, h]),
        )

    def putting(h):
        cols = hidden_cols(h)
        return (
            pltpu.make_async_copy(acted.at[:, cols], far_outs[2].at[:, cols], put_sems.at[0, h]),
            pltpu.make_async_copy(kept.at[:, cols], far_outs[3].at[:, cols], put_sems.at[1, h]),
        )

    row_puts = [
        pltpu.make_async_copy(rows_in, far_outs[0], put_sems.at[2, 0]),
        pltpu.make_async_copy(rows_grad, far_outs[1], put_sems.at[2, 1]),
    ]
    for h in range(steps):
        for copy in getting(h):
            copy.start()
    for j in range(parts):
        here = slice(j * rows, (j + 1) * rows)
        if capacity is None:
            rows_in[here, :] = in_refs[j][:rows, :]
            rows_grad[here, :] = in_refs[j][rows:, :]
            continue
        seqs, size = len(in_refs), in_refs[0].shape[1]
        pieces = jnp.concatenate([ref[j] for ref in in_refs], axis=0)
        row = lax.broadcasted_iota(jnp.int32, (rows, seqs * size), 0)
        source = lax.broadcasted_iota(jnp.int32, (rows, seqs * size), 1)
        wanted = (row // capacity) * size + row % capacity
        wanted = jnp.where(row < seqs * capacity, wanted, -size)
        for target, first in ((rows_in, 0), (rows_grad, capacity)):
            moving = (source == wanted + first).astype(f32).astype(bf16)
            target[here, :] = jnp.dot(moving, pieces, preferred_element_type=f32).astype(bf16)
    for copy in row_puts:
        copy.start()

    def forward(h, carry):
        for copy in getting(h):
            copy.wait()
        for first in range(0, TILE, PART):
            cols = pl.ds(pl.multiple_of(h * TILE + first, PART), PART)
            pre_act = jnp.dot(rows_in[...], up_mat[:, cols], preferred_element_type=f32)
            act_grad = lax.dot_general(
                rows_grad[...], down_mat[cols, :], (((1,), (1,)), ((), ())), preferred_element_type=f32
            )
            gate_sig = sigmoid(pre_act)
            acted[:, cols] = (pre_act * gate_sig).astype(bf16)
            slope = gate_sig * (1.0 + pre_act * (1.0 - gate_sig))
            kept[:, cols] = (act_grad * slope).astype(bf16)
        for copy in putting(h):
            copy.start()
        return carry

    lax.fori_loop(0, steps, forward, 0)

    def backward(d, carry):
        for first in range(0, TILE, PART):
            cols = pl.ds(pl.multiple_of(d * TILE + first, PART), PART)
            term = lax.dot_general(
                kept[...], up_mat[cols, :], (((1,), (1,)), ((), ())), preferred_element_type=f32
            )
            for j in range(parts):
                slot_refs[j][:, cols] = term[j * rows : (j + 1) * rows, :].astype(bf16)
        return carry

    lax.fori_loop(0, features // TILE, backward, 0)
    for copy in row_puts:
        copy.wait()
    for h in range(steps):
        for copy in putting(h):
            copy.wait()


def expert_products(blocks, parts, seqs, capacity, up_mat, down_mat):
    features, hidden = up_mat.shape
    rows = round_up(seqs * capacity, 16)
    total = parts * rows
    steps = hidden // TILE
    out = pl.pallas_call(
        functools.partial(
            expert_body, parts, rows, capacity if blocks[0].ndim == 3 else None, len(blocks)
        ),
        out_shape=tuple(jax.ShapeDtypeStruct((rows, features), bf16) for _ in range(parts))
        + (
            pltpu.HBM((total, features), bf16),
            pltpu.HBM((total, features), bf16),
            pltpu.HBM((total, hidden), bf16),
            pltpu.HBM((total, hidden), bf16),
        ),
        in_specs=whole(len(blocks)) + far(2),
        out_specs=tuple(whole(parts) + far(4)),
        scratch_shapes=[
            pltpu.VMEM((features, hidden), bf16),
            pltpu.VMEM((hidden, features), bf16),
            pltpu.VMEM((total, features), bf16),
            pltpu.VMEM((total, features), bf16),
            pltpu.VMEM((total, hidden), bf16),
            pltpu.VMEM((total, hidden), bf16),
            pltpu.SemaphoreType.DMA((2, steps)),
            pltpu.SemaphoreType.DMA((3, max(2, steps))),
        ],
        compiler_params=params(54),
        cost_estimate=SMALL,
        name="expert_products",
    )(*blocks, up_mat, down_mat)
    return out[:parts], out[parts:]


def frame_sums_body(m, experts, seqs, frames, slot_ref, *refs):
    slot_refs, out_refs, picking = refs[:experts], refs[-1 - seqs : -1], refs[-1]
    total = seqs * frames
    rows = slot_refs[0].shape[0]
    same = lax.broadcasted_iota(jnp.int32, (total, total), 0) == lax.broadcasted_iota(
        jnp.int32, (total, total), 1
    )
    columns = lax.dot_general(
        same.astype(f32).astype(bf16),
        slot_ref[m].astype(bf16),
        (((1,), (1,)), ((), ())),
        preferred_element_type=f32,
    )
    col_ids = lax.broadcasted_iota(jnp.int32, (total, rows), 1).astype(f32)
    for e in range(experts):
        picking[e] = (col_ids == columns[:, e : e + 1]).astype(f32).astype(bf16)

    def feature(d, carry):
        cols = pl.ds(pl.multiple_of(d * PART, PART), PART)
        acc = jnp.zeros((total, PART), f32)
        for e in range(experts):
            acc = acc + jnp.dot(picking[e], slot_refs[e][:, cols], preferred_element_type=f32)
        for k in range(seqs):
            out_refs[k][:, cols] = acc[k * frames : (k + 1) * frames, :].astype(out_refs[k].dtype)
        return carry

    lax.fori_loop(0, slot_refs[0].shape[1] // PART, feature, 0)


def frame_sums(m, slot, blocks, seqs, earlier, handed=()):
    rows, features = blocks[0].shape
    frames = slot.shape[2] // seqs
    first = 1 + len(blocks) + len(earlier)
    out = pl.pallas_call(
        functools.partial(frame_sums_body, m, len(blocks), seqs, frames),
        out_shape=tuple(pltpu.HBM(h.shape, h.dtype) for h in handed)
        + tuple(
            jax.ShapeDtypeStruct((frames, features), f32 if k == 0 else bf16) for k in range(seqs)
        ),
        in_specs=whole(1 + len(blocks)) + after(len(earlier)) + far(len(handed)),
        out_specs=tuple(far(len(handed)) + whole(seqs)),
        input_output_aliases={first + i: i for i in range(len(handed))},
        scratch_shapes=[pltpu.VMEM((len(blocks), seqs * frames, rows), bf16)],
        compiler_params=params(16),
        cost_estimate=SMALL,
        name="frame_sums",
    )(slot, *blocks, *earlier, *handed)
    return out[: len(handed)], out[len(handed) :]


def epilogue_body(m, seqs, last, *refs):
    norm_refs = refs[:seqs]
    (x_all, up_all, conv_ref, mixed_ref, scale_ref, taps_ref, gain_ref) = refs[seqs : seqs + 7]
    if last:
        sums_ref, other_ref, prev_ref, term_ref, norm_grad, pad_x, pad_g, x_ref, up_ref, sems = refs[seqs + 7 :]
        prev_ref[0] = other_ref[...]
        prev_ref = prev_ref.at[1]
    else:
        prev_ref, term_ref, norm_grad, pad_x, pad_g, x_ref, up_ref, sems = refs[seqs + 7 :]
    fetched(m, (x_all, up_all), (x_ref, up_ref), sems)
    conv_ref, mixed_ref, scale_ref = conv_ref.at[m], mixed_ref.at[m], scale_ref.at[m]
    frames, features = x_ref.shape
    tap_count = taps_ref.shape[0]
    margin = tap_count // 2
    lead = round_up(margin, 8)
    pad_x[...] = jnp.zeros(pad_x.shape, f32)
    pad_g[...] = jnp.zeros(pad_g.shape, f32)
    scale = scale_ref[...]

    def put(row, cols, value):
        if last:
            value = value + sums_ref[row : row + 1, cols]
        term_ref[row : row + 1, cols] = value.astype(term_ref.dtype)

    def gather(c, inner):
        cols = pl.ds(pl.multiple_of(c * LANES, LANES), LANES)
        grad = norm_refs[0][:, cols].astype(f32)
        for k in range(1, seqs):
            grad = grad + norm_refs[k][:, cols].astype(f32)
        norm_grad[:, cols] = grad
        weighed = grad * mixed_ref[:, cols]
        put(tap_count, cols, jnp.sum(weighed * scale, axis=0, keepdims=True))
        return inner + weighed * gain_ref[:, cols]

    inner = lax.fori_loop(0, features // LANES, gather, jnp.zeros((frames, LANES), f32))
    pull = scale * scale * scale * (jnp.sum(inner, axis=1, keepdims=True) / features)

    def chunk(c, carry):
        cols = pl.ds(pl.multiple_of(c * LANES, LANES), LANES)
        mixed_grad = (
            up_ref[:, cols].astype(f32)
            + scale * (norm_grad[:, cols] * gain_ref[:, cols])
            - mixed_ref[:, cols] * pull
        )
        conv_grad = mixed_grad * silu_slope(conv_ref[:, cols])
        pad_x[lead : lead + frames, :] = x_ref[:, cols].astype(f32)
        pad_g[lead : lead + frames, :] = conv_grad
        acc = mixed_grad
        for j in range(tap_count):
            first = lead + j - margin
            put(j, cols, jnp.sum(conv_grad * pad_x[first : first + frames, :], axis=0, keepdims=True))
            first = lead + margin - j
            acc = acc + taps_ref[j, :, cols] * pad_g[first : first + frames, :]
        prev_ref[:, cols] = acc.astype(bf16)
        return carry

    lax.fori_loop(0, features // LANES, chunk, 0)


def epilogue(m, norm_blocks, x, upstream, saved, taps, gain, *before):
    _, frames, features = x.shape
    seqs = len(norm_blocks)
    lead = round_up(taps.shape[0] // 2, 8)
    last = bool(before)
    return pl.pallas_call(
        functools.partial(epilogue_body, m, seqs, last),
        out_shape=(
            jax.ShapeDtypeStruct(x.shape if last else (frames, features), bf16),
            jax.ShapeDtypeStruct((taps.shape[0] + 1, features), bf16 if last else f32),
        ),
        in_specs=whole(seqs) + far(2) + whole(5 + len(before)),
        out_specs=tuple(whole(2)),
        scratch_shapes=[
            pltpu.VMEM((frames, features), f32),
            pltpu.VMEM((frames + 2 * lead, LANES), f32),
            pltpu.VMEM((frames + 2 * lead, LANES), f32),
        ]
        + fetch_scratch(frames, features),
        compiler_params=params(16),
        cost_estimate=SMALL,
        name="norm_conv_back",
    )(*norm_blocks, x, upstream, *saved, taps, gain, *before)


def tree_sum(terms):
    while len(terms) > 1:
        terms = [terms[i] + terms[i + 1] for i in range(0, len(terms), 2)]
    return terms[0]


def last_sum_body(*refs):
    term_refs, taps_ref, gain_ref = refs[:-2], refs[-2], refs[-1]
    tap_count = taps_ref.shape[0]
    total = tree_sum([ref[...].astype(f32) for ref in term_refs])
    for j in range(tap_count):
        taps_ref[j] = total[j : j + 1, :]
    gain_ref[...] = total[tap_count:, :]


def last_sum(terms):
    rows, features = terms[0].shape
    return pl.pallas_call(
        last_sum_body,
        out_shape=(
            jax.ShapeDtypeStruct((rows - 1, 1, features), f32),
            jax.ShapeDtypeStruct((1, features), f32),
        ),
        in_specs=whole(len(terms)),
        out_specs=tuple(whole(2)),
        compiler_params=params(16),
        cost_estimate=SMALL,
        name="last_sum",
    )(*terms)


def to_partner(array, axis, k):
    return lax.ppermute(array, axis, [(i, i ^ k) for i in range(lax.axis_size(axis))])


def from_all(array, axis):
    held = [array]
    for k in range(1, lax.axis_size(axis)):
        low = k & -k
        held.append(to_partner(held[k - low], axis, low))
    return held


def exchanged(blocks, axis):
    return [blocks[0]] + [to_partner(blocks[k], axis, k) for k in range(1, len(blocks))]


def local(section_input, out_grad, routes, combine, kernel, norm_gain, up_weight, down_weight):
    experts = lax.axis_size("expert")
    seqs = lax.axis_size("dp")
    frames, features = section_input.shape[3:]
    top_count = routes.shape[4]
    capacity = 9 * frames * top_count // (8 * experts)
    taps = kernel.transpose(1, 0, 2)
    up_mat, down_mat = up_weight[0, 0], down_weight[0, 0]
    routes = routes[0, :, 0].transpose(0, 2, 1)
    combine = combine[0, :, 0].transpose(0, 2, 1)
    xs = section_input.reshape(MB, frames, features)
    ups = out_grad.reshape(MB, frames, features)

    first = from_all(first_send(xs, ups, routes, combine, taps, norm_gain), "dp")
    pieces = second_send(xs, ups, routes, combine, taps, norm_gain, experts, capacity, first[1])
    saved = saved_frames(xs, taps, pieces[0])
    pieces = from_all(stacked(exchanged(pieces, "expert"), first[GATE]), "dp")
    blocks, slot = slots(first, experts, capacity, frames)
    blocks = exchanged(blocks, "expert")
    back, first_kept = expert_products(blocks, experts, seqs, capacity, up_mat, down_mat)
    first_back = exchanged(back, "expert")
    back, second_kept = expert_products(pieces, experts, seqs, capacity, up_mat, down_mat)
    second_back = exchanged(back, "expert")

    second_kept, sent = frame_sums(0, slot, first_back, seqs, [back[0]], second_kept)
    first_norm = exchanged(sent, "dp")
    all_in, all_grad, all_acted, all_pre = [
        jnp.concatenate(a, axis=0) for a in zip(first_kept, second_kept)
    ]
    over_rows = (((0,), (0,)), ((), ()))
    up_grad = lax.dot_general(all_in, all_pre, over_rows, preferred_element_type=f32).astype(bf16)
    down_grad = lax.dot_general(all_acted, all_grad, over_rows, preferred_element_type=f32).astype(bf16)
    _, sent = frame_sums(1, slot, second_back, seqs, [up_grad, down_grad])
    second_norm = exchanged(sent, "dp")
    before = epilogue(0, first_norm, xs, ups, saved, taps, norm_gain)
    prev, sums = epilogue(1, second_norm, xs, ups, saved, taps, norm_gain, before[1], before[0])
    peers = lax.axis_size("pipe")
    handed = lax.ppermute(prev, "pipe", [(i, (i - 1) % peers) for i in range(peers)])
    sums = tree_sum([term.astype(f32) for term in from_all(sums, "expert")]).astype(bf16)
    taps_grad, gain_grad = last_sum(from_all(sums, "dp"))
    return (
        handed[None, :, None],
        taps_grad.transpose(1, 0, 2),
        gain_grad,
        up_grad[None, None],
        down_grad[None, None],
    )


def solution(mesh):
    split = P("pipe", None, ("dp", "expert"), None, None)
    up_split = P("pipe", "expert", None, "dp")
    down_split = P("pipe", "expert", "dp", None)
    return jax.shard_map(
        local,
        mesh=mesh,
        in_specs=(split, split, split, split, P("pipe", None, None), P("pipe", None), up_split, down_split),
        out_specs=(split, P("pipe", None, None), P("pipe", None), up_split, down_split),
        check_vma=False,
    )
```

```python
import functools

import jax
import jax.numpy as jnp
from jax import lax
from jax.experimental import pallas as pl
from jax.experimental.pallas import tpu as pltpu
from jax.sharding import PartitionSpec as P

MB = 2
EPSILON = 1e-06
LANES = 128
TILE = 512
PART = 256
SEND_MIB = 60
EXPERT_MIB = 24
NOWHERE = -512.0
COSTS = (0, 0, 0, 0, 12, 0, 0, 0, 0, 2, 0, 0, 0, 0, 12)
MIB = 1024 * 1024
SMALL = pl.CostEstimate(flops=1, bytes_accessed=1, transcendentals=0)
bf16 = jnp.bfloat16
f32 = jnp.float32


def round_up(value, step):
    return -(-value // step) * step


def params(mib):
    return pltpu.CompilerParams(vmem_limit_bytes=mib * MIB)


def cost(amount):
    return pl.CostEstimate(flops=int(amount * 1.15e9) + 1, bytes_accessed=1, transcendentals=0)


def whole(count):
    return [pl.BlockSpec(memory_space=pltpu.VMEM)] * count


def after(count):
    return [pl.BlockSpec(memory_space=pl.ANY)] * count


def far(count):
    return [pl.BlockSpec(memory_space=pltpu.HBM)] * count


def fetching(sources, targets, sems):
    copies = [
        pltpu.make_async_copy(source, target, sems.at[i])
        for i, (source, target) in enumerate(zip(sources, targets))
    ]
    for copy in copies:
        copy.start()
    return copies


def fetched(sources, targets, sems):
    for copy in fetching(sources, targets, sems):
        copy.wait()


def sigmoid(values):
    return 1.0 / (1.0 + jnp.exp(-values))


def silu_slope(values):
    gate_sig = sigmoid(values)
    return gate_sig * (1.0 + values * (1.0 - gate_sig))


def shifted(pad, starts, frames):
    for residue in range(8):
        group = [(i, start // 8) for i, start in enumerate(starts) if start % 8 == residue]
        if not group:
            continue
        low, high = min(t for _, t in group), max(t for _, t in group)
        first = 8 * low + residue
        block = pad[first : first + 8 * (high - low) + frames, :]
        for i, tile in group:
            yield i, block[8 * (tile - low) : 8 * (tile - low) + frames, :]


def mixed_frames(x_ref, taps_ref, pad, conv_ref, mixed_ref):
    frames, features = x_ref.shape
    tap_count = taps_ref.shape[0]
    margin = tap_count // 2
    lead = round_up(margin, 8)
    pad[...] = jnp.zeros(pad.shape, f32)

    def chunk(c, squares):
        cols = pl.ds(pl.multiple_of(c * LANES, LANES), LANES)
        xs = x_ref[:, cols].astype(f32)
        pad[lead : lead + frames, :] = xs
        acc = jnp.zeros((frames, LANES), f32)
        for j, rows in shifted(pad, [lead + j - margin for j in range(tap_count)], frames):
            acc = acc + taps_ref[j, :, cols] * rows
        mixed = xs + acc * sigmoid(acc)
        if conv_ref is not None:
            conv_ref[:, cols] = acc
        mixed_ref[:, cols] = mixed
        return squares + mixed * mixed

    squares = lax.fori_loop(0, features // LANES, chunk, jnp.zeros((frames, LANES), f32))
    return lax.rsqrt(jnp.sum(squares, axis=1, keepdims=True) / features + EPSILON)


def meta_rows(routes_ref, combine_ref, m):
    own = lax.axis_index("expert").astype(jnp.int32)
    rows = [(routes_ref[m] ^ own).astype(f32)]
    left = combine_ref[m]
    for _ in range(3):
        rows.append(left.astype(bf16).astype(f32))
        left = left - rows[-1]
    return jnp.concatenate(rows, axis=0)


def first_send_body(
    x_all, up_all, routes_all, combine_all, taps_all, gain_all, send_ref, mixed, pad, x_ref, routes_ref,
    combine_ref, taps_ref, gain_ref, sems
):
    frames = x_ref.shape[0]
    fetched(
        (x_all.at[0], up_all.at[0], routes_all, combine_all, taps_all, gain_all),
        (x_ref, send_ref.at[frames : 2 * frames], routes_ref, combine_ref, taps_ref, gain_ref),
        sems,
    )
    scale = mixed_frames(x_ref, taps_ref, pad, None, mixed)
    send_ref[:frames, :] = (mixed[...] * scale * gain_ref[...]).astype(bf16)
    metas = [meta_rows(routes_ref, combine_ref, m) for m in range(MB)]
    send_ref[2 * frames :, :frames] = jnp.concatenate(metas, axis=0).astype(bf16)


def send_scratch(x, routes, combine, taps, gain):
    _, frames, features = x.shape
    return [
        pltpu.VMEM((frames, features), f32),
        pltpu.VMEM((frames + 2 * round_up(taps.shape[0] // 2, 8), LANES), f32),
        pltpu.VMEM((frames, features), bf16),
        pltpu.VMEM(routes.shape, routes.dtype),
        pltpu.VMEM(combine.shape, f32),
        pltpu.VMEM(taps.shape, f32),
        pltpu.VMEM(gain.shape, f32),
        pltpu.SemaphoreType.DMA((6,)),
    ]


def first_send(x, upstream, routes, combine, taps, gain):
    _, frames, features = x.shape
    return pl.pallas_call(
        first_send_body,
        out_shape=jax.ShapeDtypeStruct((2 * frames + 8 * MB, features), bf16),
        in_specs=far(6),
        out_specs=whole(1)[0],
        scratch_shapes=send_scratch(x, routes, combine, taps, gain),
        compiler_params=params(SEND_MIB),
        cost_estimate=cost(COSTS[0]),
        name="first_send",
    )(x, upstream, routes, combine, taps, gain)


def second_send_body(
    experts, capacity, x_all, up_all, routes_all, combine_all, taps_all, gain_all, _, *refs
):
    outs, (mixed, pad, x_ref, routes_ref, combine_ref, taps_ref, gain_ref, sems, joined) = (
        refs[:experts],
        refs[experts:],
    )
    frames, features = x_ref.shape
    fetched(
        (x_all.at[1], up_all.at[1], routes_all, combine_all, taps_all, gain_all),
        (x_ref, joined.at[frames:], routes_ref, combine_ref, taps_ref, gain_ref),
        sems,
    )
    scale = mixed_frames(x_ref, taps_ref, pad, None, mixed)
    joined[:frames, :] = (mixed[...] * scale * gain_ref[...]).astype(bf16)
    slot, weight = slot_map(experts, frames, meta_rows(routes_ref, combine_ref, 1), (0,))
    rows = outs[0].shape[0]
    row_ids = lax.broadcasted_iota(jnp.int32, (rows, frames), 0).astype(f32)
    for e in range(experts):
        normed_row = (row_ids == slot[e : e + 1, :]).astype(f32).astype(bf16)
        chosen = (row_ids - capacity == slot[e : e + 1, :]) & (row_ids >= capacity)
        amount = jnp.sum(jnp.where(chosen, weight[e : e + 1, :], 0.0), axis=1, keepdims=True)
        grad_row = chosen.astype(f32).astype(bf16)
        for first_col in range(0, features, 512):
            cols = slice(first_col, min(first_col + 512, features))
            picked = jnp.dot(grad_row, joined[frames:, cols], preferred_element_type=f32) * amount
            picked = picked + jnp.dot(normed_row, joined[:frames, cols], preferred_element_type=f32)
            outs[e][:, cols] = picked.astype(bf16)


def second_send(x, upstream, routes, combine, taps, gain, experts, capacity, earlier):
    _, frames, features = x.shape
    rows = round_up(2 * capacity, 8)
    return pl.pallas_call(
        functools.partial(second_send_body, experts, capacity),
        out_shape=(jax.ShapeDtypeStruct((rows, features), bf16),) * experts,
        in_specs=far(6) + after(1),
        out_specs=tuple(whole(experts)),
        scratch_shapes=send_scratch(x, routes, combine, taps, gain) + [pltpu.VMEM((2 * frames, features), bf16)],
        compiler_params=params(SEND_MIB),
        cost_estimate=cost(COSTS[14]),
        name="second_send",
    )(x, upstream, routes, combine, taps, gain, earlier)


def saved_body(x_ref, taps_ref, _, conv_ref, mixed_ref, scale_ref, pad):
    for m in range(MB):
        scale_ref[m] = mixed_frames(x_ref.at[m], taps_ref, pad, conv_ref.at[m], mixed_ref.at[m])


def saved_frames(x, taps, earlier):
    lead = round_up(taps.shape[0] // 2, 8)
    return pl.pallas_call(
        saved_body,
        out_shape=(
            jax.ShapeDtypeStruct(x.shape, f32),
            jax.ShapeDtypeStruct(x.shape, f32),
            jax.ShapeDtypeStruct(x.shape[:2] + (1,), f32),
        ),
        in_specs=whole(2) + after(1),
        out_specs=tuple(whole(3)),
        scratch_shapes=[pltpu.VMEM((x.shape[1] + 2 * lead, LANES), f32)],
        compiler_params=params(16),
        cost_estimate=cost(COSTS[1]),
        name="saved_frames",
    )(x, taps, earlier)


def passed_body(*refs):
    pass


def passed(array, earlier):
    return pl.pallas_call(
        passed_body,
        out_shape=jax.ShapeDtypeStruct(array.shape, array.dtype),
        in_specs=after(2),
        out_specs=after(1)[0],
        input_output_aliases={0: 0},
        compiler_params=params(16),
        cost_estimate=SMALL,
        name="passed",
    )(array, earlier)


def slot_map(experts, frames, meta, places):
    total = meta.shape[1]
    padded = round_up(experts, 16)
    named = lax.broadcasted_iota(jnp.int32, (padded, total), 0).astype(f32)
    first, second = meta[0:1, :] == named, meta[1:2, :] == named
    member = first | second
    earlier = lax.broadcasted_iota(jnp.int32, (total, total), 0)
    later = lax.broadcasted_iota(jnp.int32, (total, total), 1)
    before = (earlier < later) & (earlier // frames == later // frames)
    rank = jnp.dot(
        member.astype(f32).astype(bf16),
        before.astype(f32).astype(bf16),
        preferred_element_type=f32,
    )
    seq_of = lax.broadcasted_iota(jnp.int32, (padded, total), 1) // frames
    for k, first_row in enumerate(places):
        rank = jnp.where(seq_of == k, rank + first_row, rank)
    slot = jnp.where(member, rank, NOWHERE)
    first_weight = meta[2:3, :] + meta[4:5, :] + meta[6:7, :]
    second_weight = meta[3:4, :] + meta[5:6, :] + meta[7:8, :]
    weight = jnp.where(first, first_weight, 0.0) + jnp.where(second, second_weight, 0.0)
    return slot, weight


def place(slot, weight, joined, out_ref, first_row, rows):
    row_ids = lax.broadcasted_iota(jnp.int32, (rows, slot.shape[1]), 0).astype(f32)
    chosen = row_ids == slot
    placing = chosen.astype(f32).astype(bf16)
    if weight is not None:
        amount = jnp.sum(jnp.where(chosen, weight, 0.0), axis=1, keepdims=True)
    for first_col in range(0, joined.shape[1], 512):
        cols = slice(first_col, min(first_col + 512, joined.shape[1]))
        picked = jnp.dot(placing, joined[:, cols], preferred_element_type=f32)
        if weight is not None:
            picked = picked * amount
        out_ref[first_row : first_row + rows, cols] = picked.astype(bf16)


def slots_body(experts, frames, places, seqs, waits, *refs):
    block_refs, refs = refs[:seqs], refs[seqs + waits :]
    piece_refs, refs = refs[: len(refs) - experts - 3], refs[len(refs) - experts - 3 :]
    if piece_refs:
        piece_refs, stacked, refs = piece_refs[:-1], piece_refs[-1], refs
        for i, ref in enumerate(piece_refs):
            stacked[i] = ref[...]
    out_refs, (slot_ref, joined, meta) = refs[:experts], refs[experts:]
    total = seqs * frames
    for k in range(seqs):
        here = slice(k * frames, (k + 1) * frames)
        joined[here, :] = block_refs[k][:frames, :]
        joined[total + k * frames : total + (k + 1) * frames, :] = block_refs[k][frames : 2 * frames, :]
        meta[:, here] = block_refs[k][2 * frames :, :frames].astype(f32)
    slot, weight = slot_map(experts, frames, meta[:8, :], places[0])
    slot_ref[0] = slot
    slot_ref[1] = slot_map(experts, frames, meta[8:, :], places[1])[0]
    rows = out_refs[0].shape[0] // 2
    for e in range(experts):
        place(slot[e : e + 1, :], None, joined.at[:total], out_refs[e], 0, rows)
        place(slot[e : e + 1, :], weight[e : e + 1, :], joined.at[total:], out_refs[e], rows, rows)


def slots(blocks, experts, capacity, frames, places, pieces=(), earlier=()):
    features = blocks[0].shape[1]
    seqs = len(blocks)
    rows = round_up(seqs * capacity, 8)
    total = seqs * frames
    together = tuple(jax.ShapeDtypeStruct((len(pieces),) + p.shape, bf16) for p in pieces[:1])
    out = pl.pallas_call(
        functools.partial(slots_body, experts, frames, places, seqs, len(earlier)),
        out_shape=together
        + tuple(jax.ShapeDtypeStruct((2 * rows, features), bf16) for _ in range(experts))
        + (jax.ShapeDtypeStruct((MB, round_up(experts, 16), total), f32),),
        in_specs=whole(seqs) + after(len(earlier)) + whole(len(pieces)),
        out_specs=tuple(whole(len(together) + experts + 1)),
        scratch_shapes=[pltpu.VMEM((2 * total, features), bf16), pltpu.VMEM((8 * MB, total), f32)],
        compiler_params=params(16),
        cost_estimate=cost(COSTS[2 + (not pieces)]),
        name="slots",
    )(*blocks, *earlier, *pieces)
    return out[-1 - experts : -1], out[-1], out[0]


def expert_body(parts, rows, capacity, first_row, counts, *refs):
    cuts = [sum(counts[:i]) for i in range(len(counts) + 1)]
    in_refs, (up_mat, down_mat), before_refs, _, _, slot_refs, kept_far, scratch = (
        refs[cuts[i] : cuts[i + 1]] for i in range(len(counts))
    )
    rows_in, rows_grad, acted, kept, put_sems = scratch
    features, hidden = up_mat.shape
    steps = hidden // TILE
    far_outs = [ref.at[first_row : first_row + parts * rows, :] for ref in kept_far]

    def putting(h):
        cols = pl.ds(pl.multiple_of(h * TILE, TILE), TILE)
        return (
            pltpu.make_async_copy(acted.at[:, cols], far_outs[2].at[:, cols], put_sems.at[0, h]),
            pltpu.make_async_copy(kept.at[:, cols], far_outs[3].at[:, cols], put_sems.at[1, h]),
        )

    row_puts = [
        pltpu.make_async_copy(rows_in, far_outs[0], put_sems.at[2, 0]),
        pltpu.make_async_copy(rows_grad, far_outs[1], put_sems.at[2, 1]),
    ]
    for j in range(parts):
        here = slice(j * rows, (j + 1) * rows)
        if capacity is None:
            rows_in[here, :] = in_refs[j][:rows, :]
            rows_grad[here, :] = in_refs[j][rows:, :]
            continue
        seqs, size = len(in_refs), in_refs[0].shape[1]
        pieces = jnp.concatenate([ref[j] for ref in in_refs], axis=0)
        row = lax.broadcasted_iota(jnp.int32, (rows, seqs * size), 0)
        source = lax.broadcasted_iota(jnp.int32, (rows, seqs * size), 1)
        wanted = (row // capacity) * size + row % capacity
        wanted = jnp.where(row < seqs * capacity, wanted, -2 * size)
        for target, first in ((rows_in, 0), (rows_grad, capacity)):
            moving = (source == wanted + first).astype(f32).astype(bf16)
            target[here, :] = jnp.dot(moving, pieces, preferred_element_type=f32).astype(bf16)
    for copy in row_puts:
        copy.start()

    def forward(h, carry):
        for first in range(0, TILE, PART):
            cols = pl.ds(pl.multiple_of(h * TILE + first, PART), PART)
            pre_act = jnp.dot(rows_in[...], up_mat[:, cols], preferred_element_type=f32)
            act_grad = lax.dot_general(
                rows_grad[...], down_mat[cols, :], (((1,), (1,)), ((), ())), preferred_element_type=f32
            )
            gate_sig = sigmoid(pre_act)
            acted[:, cols] = (pre_act * gate_sig).astype(bf16)
            slope = gate_sig * (1.0 + pre_act * (1.0 - gate_sig))
            kept[:, cols] = (act_grad * slope).astype(bf16)
        for copy in putting(h):
            copy.start()
        return carry

    lax.fori_loop(0, steps, forward, 0)
    own_row = slot_refs[0].shape[0] - rows
    if before_refs:
        for j in range(parts):
            slot_refs[j][:own_row, :] = before_refs[j][...]

    def backward(d, carry):
        for first in range(0, TILE, PART):
            cols = pl.ds(pl.multiple_of(d * TILE + first, PART), PART)
            term = lax.dot_general(
                kept[...], up_mat[cols, :], (((1,), (1,)), ((), ())), preferred_element_type=f32
            )
            for j in range(parts):
                slot_refs[j][own_row:, cols] = term[j * rows : (j + 1) * rows, :].astype(bf16)
        return carry

    lax.fori_loop(0, features // TILE, backward, 0)
    for copy in row_puts:
        copy.wait()
    for h in range(steps):
        for copy in putting(h):
            copy.wait()


def expert_products(blocks, parts, capacity, up_mat, down_mat, rows, total, first_row, before, kept, earlier=(), stage=4):
    features, hidden = up_mat.shape
    steps = hidden // TILE
    mine = parts * rows
    slot_rows = rows + (before[0].shape[0] if before else 0)
    counts = (len(blocks), 2, len(before), len(earlier), len(kept), parts, 4, 5)
    first_kept = sum(counts[:4])
    out = pl.pallas_call(
        functools.partial(
            expert_body, parts, rows, capacity if blocks[0].ndim == 3 else None, first_row, counts
        ),
        out_shape=tuple(jax.ShapeDtypeStruct((slot_rows, features), bf16) for _ in range(parts))
        + (
            pltpu.HBM((total, features), bf16),
            pltpu.HBM((total, features), bf16),
            pltpu.HBM((total, hidden), bf16),
            pltpu.HBM((total, hidden), bf16),
        ),
        in_specs=whole(len(blocks) + 2 + len(before)) + after(len(earlier)) + far(len(kept)),
        out_specs=tuple(whole(parts) + far(4)),
        input_output_aliases={first_kept + i: parts + i for i in range(len(kept))},
        scratch_shapes=[
            pltpu.VMEM((mine, features), bf16),
            pltpu.VMEM((mine, features), bf16),
            pltpu.VMEM((mine, hidden), bf16),
            pltpu.VMEM((mine, hidden), bf16),
            pltpu.SemaphoreType.DMA((3, max(2, steps))),
        ],
        compiler_params=params(EXPERT_MIB),
        cost_estimate=cost(COSTS[stage]),
        name="expert_products",
    )(*blocks, up_mat, down_mat, *before, *earlier, *kept)
    return out[:parts], out[parts:]


def frame_sums_body(m, experts, frames, pieces, *refs):
    map_refs, slot_refs, out_refs, picking = refs[:2], refs[2 : 2 + experts], refs[-1 - len(pieces) : -1], refs[-1]
    total = len(pieces) * frames
    rows = slot_refs[0].shape[0]
    same = lax.broadcasted_iota(jnp.int32, (frames, frames), 0) == lax.broadcasted_iota(
        jnp.int32, (frames, frames), 1
    )
    same = same.astype(f32).astype(bf16)
    col_ids = lax.broadcasted_iota(jnp.int32, (frames, rows), 1)
    for i, (half, k, first_row) in enumerate(pieces):
        columns = lax.dot_general(
            same,
            map_refs[half][m, :, k * frames : (k + 1) * frames].astype(bf16),
            (((1,), (1,)), ((), ())),
            preferred_element_type=f32,
        )
        here = (col_ids - first_row).astype(f32)
        for e in range(experts):
            picking[e, i * frames : (i + 1) * frames, :] = (
                (here == columns[:, e : e + 1]).astype(f32).astype(bf16)
            )

    def feature(d, carry):
        cols = pl.ds(pl.multiple_of(d * PART, PART), PART)
        acc = jnp.zeros((total, PART), f32)
        for e in range(experts):
            acc = acc + jnp.dot(picking[e], slot_refs[e][:, cols], preferred_element_type=f32)
        for i, out_ref in enumerate(out_refs):
            out_ref[:, cols] = acc[i * frames : (i + 1) * frames, :].astype(out_ref.dtype)
        return carry

    lax.fori_loop(0, slot_refs[0].shape[1] // PART, feature, 0)


def frame_sums(m, maps, blocks, frames, pieces, earlier, handed=()):
    rows, features = blocks[0].shape
    first = 2 + len(blocks) + len(earlier)
    out = pl.pallas_call(
        functools.partial(frame_sums_body, m, len(blocks), frames, pieces),
        out_shape=tuple(pltpu.HBM(h.shape, h.dtype) for h in handed)
        + tuple(
            jax.ShapeDtypeStruct((frames, features), f32 if piece[:2] == (0, 0) else bf16)
            for piece in pieces
        ),
        in_specs=whole(2 + len(blocks)) + after(len(earlier)) + far(len(handed)),
        out_specs=tuple(far(len(handed)) + whole(len(pieces))),
        input_output_aliases={first + i: i for i in range(len(handed))},
        scratch_shapes=[pltpu.VMEM((len(blocks), len(pieces) * frames, rows), bf16)],
        compiler_params=params(16),
        cost_estimate=cost(COSTS[8 + m + (len(pieces) == 1)]),
        name="frame_sums",
    )(*maps, *blocks, *earlier, *handed)
    return out[: len(handed)], out[len(handed) :]


def epilogue_body(m, seqs, last, waits, *refs):
    norm_refs = refs[:seqs]
    (x_all, up_all, conv_ref, mixed_ref, scale_ref, taps_ref, gain_ref) = refs[seqs : seqs + 7]
    before, refs = refs[seqs + 7 : seqs + 7 + 2 * last], refs[seqs + 7 + 2 * last + waits :]
    if last:
        sums_ref, other_ref = before
    prev_ref, term_ref, norm_grad, pad_x, pad_g, x_ref, up_ref, sems = refs
    if last:
        prev_ref[0] = other_ref[...]
        prev_ref = prev_ref.at[1]
    copies = fetching((x_all.at[m], up_all.at[m]), (x_ref, up_ref), sems)
    conv_ref, mixed_ref, scale_ref = conv_ref.at[m], mixed_ref.at[m], scale_ref.at[m]
    frames, features = x_ref.shape
    tap_count = taps_ref.shape[0]
    margin = tap_count // 2
    lead = round_up(margin, 8)
    pad_x[...] = jnp.zeros(pad_x.shape, f32)
    pad_g[...] = jnp.zeros(pad_g.shape, f32)
    scale = scale_ref[...]

    def put(row, cols, value):
        if last:
            value = value + sums_ref[row : row + 1, cols]
        term_ref[row : row + 1, cols] = value.astype(term_ref.dtype)

    def gather(c, inner):
        cols = pl.ds(pl.multiple_of(c * LANES, LANES), LANES)
        grad = norm_refs[0][:, cols].astype(f32)
        for k in range(1, seqs):
            grad = grad + norm_refs[k][:, cols].astype(f32)
        norm_grad[:, cols] = grad
        weighed = grad * mixed_ref[:, cols]
        put(tap_count, cols, jnp.sum(weighed * scale, axis=0, keepdims=True))
        return inner + weighed * gain_ref[:, cols]

    inner = lax.fori_loop(0, features // LANES, gather, jnp.zeros((frames, LANES), f32))
    for copy in copies:
        copy.wait()
    pull = scale * scale * scale * (jnp.sum(inner, axis=1, keepdims=True) / features)

    def chunk(c, carry):
        cols = pl.ds(pl.multiple_of(c * LANES, LANES), LANES)
        mixed_grad = (
            up_ref[:, cols].astype(f32)
            + scale * (norm_grad[:, cols] * gain_ref[:, cols])
            - mixed_ref[:, cols] * pull
        )
        conv_grad = mixed_grad * silu_slope(conv_ref[:, cols])
        pad_x[lead : lead + frames, :] = x_ref[:, cols].astype(f32)
        pad_g[lead : lead + frames, :] = conv_grad
        acc = mixed_grad
        for j, rows in shifted(pad_x, [lead + j - margin for j in range(tap_count)], frames):
            put(j, cols, jnp.sum(conv_grad * rows, axis=0, keepdims=True))
        for j, rows in shifted(pad_g, [lead + margin - j for j in range(tap_count)], frames):
            acc = acc + taps_ref[j, :, cols] * rows
        prev_ref[:, cols] = acc.astype(bf16)
        return carry

    lax.fori_loop(0, features // LANES, chunk, 0)


def epilogue(m, norm_blocks, x, upstream, saved, taps, gain, before=(), earlier=()):
    _, frames, features = x.shape
    seqs = len(norm_blocks)
    lead = round_up(taps.shape[0] // 2, 8)
    last = bool(before)
    return pl.pallas_call(
        functools.partial(epilogue_body, m, seqs, last, len(earlier)),
        out_shape=(
            jax.ShapeDtypeStruct(x.shape if last else (frames, features), bf16),
            jax.ShapeDtypeStruct((taps.shape[0] + 1, features), bf16 if last else f32),
        ),
        in_specs=whole(seqs) + far(2) + whole(5 + len(before)) + after(len(earlier)),
        out_specs=tuple(whole(2)),
        scratch_shapes=[
            pltpu.VMEM((frames, features), f32),
            pltpu.VMEM((frames + 2 * lead, LANES), f32),
            pltpu.VMEM((frames + 2 * lead, LANES), f32),
        ]
        + [
            pltpu.VMEM((frames, features), bf16),
            pltpu.VMEM((frames, features), bf16),
            pltpu.SemaphoreType.DMA((2,)),
        ],
        compiler_params=params(16),
        cost_estimate=cost(COSTS[11 + m]),
        name="norm_conv_back",
    )(*norm_blocks, x, upstream, *saved, taps, gain, *before, *earlier)


def tree_sum(terms):
    while len(terms) > 1:
        terms = [terms[i] + terms[i + 1] for i in range(0, len(terms), 2)]
    return terms[0]


def last_sum_body(*refs):
    term_refs, taps_ref, gain_ref = refs[:-2], refs[-2], refs[-1]
    tap_count = taps_ref.shape[0]
    total = tree_sum([ref[...].astype(f32) for ref in term_refs])
    for j in range(tap_count):
        taps_ref[j] = total[j : j + 1, :]
    gain_ref[...] = total[tap_count:, :]


def last_sum(terms):
    rows, features = terms[0].shape
    return pl.pallas_call(
        last_sum_body,
        out_shape=(
            jax.ShapeDtypeStruct((rows - 1, 1, features), f32),
            jax.ShapeDtypeStruct((1, features), f32),
        ),
        in_specs=whole(len(terms)),
        out_specs=tuple(whole(2)),
        compiler_params=params(16),
        cost_estimate=cost(COSTS[13]),
        name="last_sum",
    )(*terms)


def to_partner(array, axis, k):
    return lax.ppermute(array, axis, [(i, i ^ k) for i in range(lax.axis_size(axis))])


def from_all(array, axis):
    return [array] + [to_partner(array, axis, k) for k in range(1, lax.axis_size(axis))]


def exchanged(blocks, axis):
    return [blocks[0]] + [to_partner(blocks[k], axis, k) for k in range(1, len(blocks))]


def local(section_input, out_grad, routes, combine, kernel, norm_gain, up_weight, down_weight):
    experts = lax.axis_size("expert")
    seqs = lax.axis_size("dp")
    frames, features = section_input.shape[3:]
    top_count = routes.shape[4]
    capacity = 9 * frames * top_count // (8 * experts)
    taps = kernel.transpose(1, 0, 2)
    up_mat, down_mat = up_weight[0, 0], down_weight[0, 0]
    routes = routes[0, :, 0].transpose(0, 2, 1)
    combine = combine[0, :, 0].transpose(0, 2, 1)
    xs = section_input.reshape(MB, frames, features)
    ups = out_grad.reshape(MB, frames, features)

    sent = first_send(xs, ups, routes, combine, taps, norm_gain)
    pieces = second_send(xs, ups, routes, combine, taps, norm_gain, experts, capacity, sent)
    half = round_up(seqs // 2 * capacity, 8)
    most, last = round_up((seqs - 1) * capacity, 16), round_up(capacity, 16)
    near_places = ((0, capacity), (0, capacity))
    wide_places = ((0, capacity), (2 * capacity, 0))

    first = [sent, to_partner(sent, "dp", 1)]
    near, near_map, pieces = slots(
        first, experts, capacity, frames, near_places, exchanged(pieces, "expert")
    )
    later = passed(to_partner(sent, "dp", 2), near[0])
    first += [later, to_partner(later, "dp", 1)]
    saved = saved_frames(xs, taps, first[1])
    near = exchanged(near, "expert")

    products = functools.partial(
        expert_products,
        parts=experts,
        capacity=capacity,
        up_mat=up_mat,
        down_mat=down_mat,
        total=experts * (2 * half + most + last),
    )
    at = experts * half
    back, kept = products(near, rows=half, first_row=0, before=(), kept=(), earlier=(saved[2],), stage=4)
    early = passed(pieces, later)
    pieces = passed(pieces, near[1])
    later = passed(to_partner(early, "dp", 2), back[0])
    second = [pieces, to_partner(pieces, "dp", 1), later, to_partner(later, "dp", 1)]
    wide, wide_map, _ = slots(first[2:], experts, capacity, frames, wide_places, earlier=tuple(near[1:]))
    maps = (near_map, wide_map)
    wide = exchanged(wide, "expert")
    back, kept = products(wide, rows=half, first_row=at, before=back, kept=kept, stage=5)
    first_back = exchanged(back, "expert")
    back, kept = products(second[:-1], rows=most, first_row=2 * at, before=(), kept=kept, stage=6)
    most_back = exchanged(back, "expert")
    back, kept = products(
        second[-1:], rows=last, first_row=2 * at + experts * most, before=(), kept=kept, stage=7
    )
    last_back = exchanged(back, "expert")

    _, sent = frame_sums(
        0, maps, first_back, frames, ((0, 0, 0), (0, 1, 0), (1, 0, half), (1, 1, half)), [back[0]]
    )
    first_norm = exchanged(sent, "dp")
    (all_in, all_grad, all_acted, all_pre), sent = frame_sums(
        1, maps, most_back, frames, ((0, 0, 0), (0, 1, 0), (1, 0, 0)), [], kept
    )
    second_norm = exchanged(sent, "dp")
    over_rows = (((0,), (0,)), ((), ()))
    up_grad = lax.dot_general(all_in, all_pre, over_rows, preferred_element_type=f32).astype(bf16)
    down_grad = lax.dot_general(all_acted, all_grad, over_rows, preferred_element_type=f32).astype(bf16)
    _, sent = frame_sums(1, maps, last_back, frames, ((1, 1, 0),), [])
    second_norm.append(to_partner(sent[0], "dp", seqs - 1))
    prev, sums = epilogue(0, first_norm, xs, ups, saved, taps, norm_gain, earlier=(up_grad,))
    prev, sums = epilogue(1, second_norm, xs, ups, saved, taps, norm_gain, before=(sums, prev))
    peers = lax.axis_size("pipe")
    handed = lax.ppermute(prev, "pipe", [(i, (i - 1) % peers) for i in range(peers)])
    sums = tree_sum([term.astype(f32) for term in from_all(sums, "expert")]).astype(bf16)
    taps_grad, gain_grad = last_sum(from_all(sums, "dp"))
    return (
        handed[None, :, None],
        taps_grad.transpose(1, 0, 2),
        gain_grad,
        up_grad[None, None],
        down_grad[None, None],
    )


def solution(mesh):
    split = P("pipe", None, ("dp", "expert"), None, None)
    up_split = P("pipe", "expert", None, "dp")
    down_split = P("pipe", "expert", "dp", None)
    return jax.shard_map(
        local,
        mesh=mesh,
        in_specs=(split, split, split, split, P("pipe", None, None), P("pipe", None), up_split, down_split),
        out_specs=(split, P("pipe", None, None), P("pipe", None), up_split, down_split),
        check_vma=False,
    )
```

```python
import functools

import jax
import jax.numpy as jnp
from jax import lax
from jax.experimental import pallas as pl
from jax.experimental.pallas import tpu as pltpu
from jax.sharding import PartitionSpec as P

MB = 2
EPSILON = 1e-06
LANES = 128
TILE = 512
PART = 256
SEND_MIB = 60
EXPERT_MIB = 24
NOWHERE = -512.0
COSTS = (0, 0, 0, 0, 12, 0, 10, 0, 0, 2, 0, 0, 0, 0, 12, 0)
MIB = 1024 * 1024
SMALL = pl.CostEstimate(flops=1, bytes_accessed=1, transcendentals=0)
bf16 = jnp.bfloat16
f32 = jnp.float32


def round_up(value, step):
    return -(-value // step) * step


def params(mib):
    return pltpu.CompilerParams(vmem_limit_bytes=mib * MIB)


def cost(amount):
    return pl.CostEstimate(flops=int(amount * 1.15e9) + 1, bytes_accessed=1, transcendentals=0)


def whole(count):
    return [pl.BlockSpec(memory_space=pltpu.VMEM)] * count


def after(count):
    return [pl.BlockSpec(memory_space=pl.ANY)] * count


def far(count):
    return [pl.BlockSpec(memory_space=pltpu.HBM)] * count


def fetching(sources, targets, sems):
    copies = [
        pltpu.make_async_copy(source, target, sems.at[i])
        for i, (source, target) in enumerate(zip(sources, targets))
    ]
    for copy in copies:
        copy.start()
    return copies


def fetched(sources, targets, sems):
    for copy in fetching(sources, targets, sems):
        copy.wait()


def sigmoid(values):
    return 1.0 / (1.0 + jnp.exp(-values))


def silu_slope(values):
    gate_sig = sigmoid(values)
    return gate_sig * (1.0 + values * (1.0 - gate_sig))


def shifted(pad, starts, frames):
    for residue in range(8):
        group = [(i, start // 8) for i, start in enumerate(starts) if start % 8 == residue]
        if not group:
            continue
        low, high = min(t for _, t in group), max(t for _, t in group)
        first = 8 * low + residue
        block = pad[first : first + 8 * (high - low) + frames, :]
        for i, tile in group:
            yield i, block[8 * (tile - low) : 8 * (tile - low) + frames, :]


def mixed_frames(x_ref, taps_ref, pad, conv_ref, mixed_ref):
    frames, features = x_ref.shape
    tap_count = taps_ref.shape[0]
    margin = tap_count // 2
    lead = round_up(margin, 8)
    pad[...] = jnp.zeros(pad.shape, f32)

    def chunk(c, squares):
        cols = pl.ds(pl.multiple_of(c * LANES, LANES), LANES)
        xs = x_ref[:, cols].astype(f32)
        pad[lead : lead + frames, :] = xs
        acc = jnp.zeros((frames, LANES), f32)
        for j, rows in shifted(pad, [lead + j - margin for j in range(tap_count)], frames):
            acc = acc + taps_ref[j, :, cols] * rows
        mixed = xs + acc * sigmoid(acc)
        if conv_ref is not None:
            conv_ref[:, cols] = acc
        mixed_ref[:, cols] = mixed
        return squares + mixed * mixed

    squares = lax.fori_loop(0, features // LANES, chunk, jnp.zeros((frames, LANES), f32))
    return lax.rsqrt(jnp.sum(squares, axis=1, keepdims=True) / features + EPSILON)


def meta_rows(routes_ref, combine_ref, m):
    own = lax.axis_index("expert").astype(jnp.int32)
    rows = [(routes_ref[m] ^ own).astype(f32)]
    left = combine_ref[m]
    for _ in range(3):
        rows.append(left.astype(bf16).astype(f32))
        left = left - rows[-1]
    return jnp.concatenate(rows, axis=0)


def first_send_body(
    x_all, up_all, routes_all, combine_all, taps_all, gain_all, send_ref, mixed, pad, x_ref, routes_ref,
    combine_ref, taps_ref, gain_ref, sems
):
    frames = x_ref.shape[0]
    fetched(
        (x_all.at[0], up_all.at[0], routes_all, combine_all, taps_all, gain_all),
        (x_ref, send_ref.at[frames : 2 * frames], routes_ref, combine_ref, taps_ref, gain_ref),
        sems,
    )
    scale = mixed_frames(x_ref, taps_ref, pad, None, mixed)
    send_ref[:frames, :] = (mixed[...] * scale * gain_ref[...]).astype(bf16)
    metas = [meta_rows(routes_ref, combine_ref, m) for m in range(MB)]
    send_ref[2 * frames :, :frames] = jnp.concatenate(metas, axis=0).astype(bf16)


def send_scratch(x, routes, combine, taps, gain):
    _, frames, features = x.shape
    return [
        pltpu.VMEM((frames, features), f32),
        pltpu.VMEM((frames + 2 * round_up(taps.shape[0] // 2, 8), LANES), f32),
        pltpu.VMEM((frames, features), bf16),
        pltpu.VMEM(routes.shape, routes.dtype),
        pltpu.VMEM(combine.shape, f32),
        pltpu.VMEM(taps.shape, f32),
        pltpu.VMEM(gain.shape, f32),
        pltpu.SemaphoreType.DMA((6,)),
    ]


def first_send(x, upstream, routes, combine, taps, gain):
    _, frames, features = x.shape
    return pl.pallas_call(
        first_send_body,
        out_shape=jax.ShapeDtypeStruct((2 * frames + 8 * MB, features), bf16),
        in_specs=far(6),
        out_specs=whole(1)[0],
        scratch_shapes=send_scratch(x, routes, combine, taps, gain),
        compiler_params=params(SEND_MIB),
        cost_estimate=cost(COSTS[0]),
        name="first_send",
    )(x, upstream, routes, combine, taps, gain)


def second_send_body(
    experts, capacity, x_all, up_all, routes_all, combine_all, taps_all, gain_all, _, *refs
):
    outs, (mixed, pad, x_ref, routes_ref, combine_ref, taps_ref, gain_ref, sems, joined) = (
        refs[:experts],
        refs[experts:],
    )
    frames, features = x_ref.shape
    fetched(
        (x_all.at[1], up_all.at[1], routes_all, combine_all, taps_all, gain_all),
        (x_ref, joined.at[frames:], routes_ref, combine_ref, taps_ref, gain_ref),
        sems,
    )
    scale = mixed_frames(x_ref, taps_ref, pad, None, mixed)
    joined[:frames, :] = (mixed[...] * scale * gain_ref[...]).astype(bf16)
    slot, weight = slot_map(experts, frames, meta_rows(routes_ref, combine_ref, 1), (0,))
    rows = outs[0].shape[0]
    row_ids = lax.broadcasted_iota(jnp.int32, (rows, frames), 0).astype(f32)
    for e in range(experts):
        normed_row = (row_ids == slot[e : e + 1, :]).astype(f32).astype(bf16)
        chosen = (row_ids - capacity == slot[e : e + 1, :]) & (row_ids >= capacity)
        amount = jnp.sum(jnp.where(chosen, weight[e : e + 1, :], 0.0), axis=1, keepdims=True)
        grad_row = chosen.astype(f32).astype(bf16)
        for first_col in range(0, features, 512):
            cols = slice(first_col, min(first_col + 512, features))
            picked = jnp.dot(grad_row, joined[frames:, cols], preferred_element_type=f32) * amount
            picked = picked + jnp.dot(normed_row, joined[:frames, cols], preferred_element_type=f32)
            outs[e][:, cols] = picked.astype(bf16)


def second_send(x, upstream, routes, combine, taps, gain, experts, capacity, earlier):
    _, frames, features = x.shape
    rows = round_up(2 * capacity, 8)
    return pl.pallas_call(
        functools.partial(second_send_body, experts, capacity),
        out_shape=(jax.ShapeDtypeStruct((rows, features), bf16),) * experts,
        in_specs=far(6) + after(1),
        out_specs=tuple(whole(experts)),
        scratch_shapes=send_scratch(x, routes, combine, taps, gain) + [pltpu.VMEM((2 * frames, features), bf16)],
        compiler_params=params(SEND_MIB),
        cost_estimate=cost(COSTS[14]),
        name="second_send",
    )(x, upstream, routes, combine, taps, gain, earlier)


def saved_body(x_ref, taps_ref, _, conv_ref, mixed_ref, scale_ref, pad):
    for m in range(MB):
        scale_ref[m] = mixed_frames(x_ref.at[m], taps_ref, pad, conv_ref.at[m], mixed_ref.at[m])


def saved_frames(x, taps, earlier):
    lead = round_up(taps.shape[0] // 2, 8)
    return pl.pallas_call(
        saved_body,
        out_shape=(
            jax.ShapeDtypeStruct(x.shape, f32),
            jax.ShapeDtypeStruct(x.shape, f32),
            jax.ShapeDtypeStruct(x.shape[:2] + (1,), f32),
        ),
        in_specs=whole(2) + after(1),
        out_specs=tuple(whole(3)),
        scratch_shapes=[pltpu.VMEM((x.shape[1] + 2 * lead, LANES), f32)],
        compiler_params=params(16),
        cost_estimate=cost(COSTS[1]),
        name="saved_frames",
    )(x, taps, earlier)


def passed_body(*refs):
    pass


def passed(array, earlier):
    return pl.pallas_call(
        passed_body,
        out_shape=jax.ShapeDtypeStruct(array.shape, array.dtype),
        in_specs=after(2),
        out_specs=after(1)[0],
        input_output_aliases={0: 0},
        compiler_params=params(16),
        cost_estimate=SMALL,
        name="passed",
    )(array, earlier)


def slot_map(experts, frames, meta, places):
    total = meta.shape[1]
    padded = round_up(experts, 16)
    named = lax.broadcasted_iota(jnp.int32, (padded, total), 0).astype(f32)
    first, second = meta[0:1, :] == named, meta[1:2, :] == named
    member = first | second
    earlier = lax.broadcasted_iota(jnp.int32, (total, total), 0)
    later = lax.broadcasted_iota(jnp.int32, (total, total), 1)
    before = (earlier < later) & (earlier // frames == later // frames)
    rank = jnp.dot(
        member.astype(f32).astype(bf16),
        before.astype(f32).astype(bf16),
        preferred_element_type=f32,
    )
    seq_of = lax.broadcasted_iota(jnp.int32, (padded, total), 1) // frames
    for k, first_row in enumerate(places):
        rank = jnp.where(seq_of == k, rank + first_row, rank)
    slot = jnp.where(member, rank, NOWHERE)
    first_weight = meta[2:3, :] + meta[4:5, :] + meta[6:7, :]
    second_weight = meta[3:4, :] + meta[5:6, :] + meta[7:8, :]
    weight = jnp.where(first, first_weight, 0.0) + jnp.where(second, second_weight, 0.0)
    return slot, weight


def place(slot, weight, joined, out_ref, first_row, rows):
    row_ids = lax.broadcasted_iota(jnp.int32, (rows, slot.shape[1]), 0).astype(f32)
    chosen = row_ids == slot
    placing = chosen.astype(f32).astype(bf16)
    if weight is not None:
        amount = jnp.sum(jnp.where(chosen, weight, 0.0), axis=1, keepdims=True)
    for first_col in range(0, joined.shape[1], 512):
        cols = slice(first_col, min(first_col + 512, joined.shape[1]))
        picked = jnp.dot(placing, joined[:, cols], preferred_element_type=f32)
        if weight is not None:
            picked = picked * amount
        out_ref[first_row : first_row + rows, cols] = picked.astype(bf16)


def slots_body(experts, frames, places, seqs, waits, *refs):
    block_refs, refs = refs[:seqs], refs[seqs + waits :]
    piece_refs, refs = refs[: len(refs) - experts - 3], refs[len(refs) - experts - 3 :]
    if piece_refs:
        piece_refs, stacked, refs = piece_refs[:-1], piece_refs[-1], refs
        for i, ref in enumerate(piece_refs):
            stacked[i] = ref[...]
    out_refs, (slot_ref, joined, meta) = refs[:experts], refs[experts:]
    total = seqs * frames
    for k in range(seqs):
        here = slice(k * frames, (k + 1) * frames)
        joined[here, :] = block_refs[k][:frames, :]
        joined[total + k * frames : total + (k + 1) * frames, :] = block_refs[k][frames : 2 * frames, :]
        meta[:, here] = block_refs[k][2 * frames :, :frames].astype(f32)
    slot, weight = slot_map(experts, frames, meta[:8, :], places[0])
    slot_ref[0] = slot
    slot_ref[1] = slot_map(experts, frames, meta[8:, :], places[1])[0]
    rows = out_refs[0].shape[0] // 2
    for e in range(experts):
        place(slot[e : e + 1, :], None, joined.at[:total], out_refs[e], 0, rows)
        place(slot[e : e + 1, :], weight[e : e + 1, :], joined.at[total:], out_refs[e], rows, rows)


def slots(blocks, experts, capacity, frames, places, pieces=(), earlier=()):
    features = blocks[0].shape[1]
    seqs = len(blocks)
    rows = round_up(seqs * capacity, 8)
    total = seqs * frames
    together = tuple(jax.ShapeDtypeStruct((len(pieces),) + p.shape, bf16) for p in pieces[:1])
    out = pl.pallas_call(
        functools.partial(slots_body, experts, frames, places, seqs, len(earlier)),
        out_shape=together
        + tuple(jax.ShapeDtypeStruct((2 * rows, features), bf16) for _ in range(experts))
        + (jax.ShapeDtypeStruct((MB, round_up(experts, 16), total), f32),),
        in_specs=whole(seqs) + after(len(earlier)) + whole(len(pieces)),
        out_specs=tuple(whole(len(together) + experts + 1)),
        scratch_shapes=[pltpu.VMEM((2 * total, features), bf16), pltpu.VMEM((8 * MB, total), f32)],
        compiler_params=params(16),
        cost_estimate=cost(COSTS[2 + (not pieces)]),
        name="slots",
    )(*blocks, *earlier, *pieces)
    return out[-1 - experts : -1], out[-1], out[0]


def expert_body(parts, rows, capacity, first_row, counts, *refs):
    cuts = [sum(counts[:i]) for i in range(len(counts) + 1)]
    in_refs, (up_mat, down_mat), before_refs, _, _, slot_refs, kept_far, scratch = (
        refs[cuts[i] : cuts[i + 1]] for i in range(len(counts))
    )
    rows_in, rows_grad, acted, kept, put_sems = scratch
    features, hidden = up_mat.shape
    steps = hidden // TILE
    far_outs = [ref.at[first_row : first_row + parts * rows, :] for ref in kept_far]

    def putting(h):
        cols = pl.ds(pl.multiple_of(h * TILE, TILE), TILE)
        return (
            pltpu.make_async_copy(acted.at[:, cols], far_outs[2].at[:, cols], put_sems.at[0, h]),
            pltpu.make_async_copy(kept.at[:, cols], far_outs[3].at[:, cols], put_sems.at[1, h]),
        )

    row_puts = [
        pltpu.make_async_copy(rows_in, far_outs[0], put_sems.at[2, 0]),
        pltpu.make_async_copy(rows_grad, far_outs[1], put_sems.at[2, 1]),
    ]
    for j in range(parts):
        here = slice(j * rows, (j + 1) * rows)
        if capacity is None:
            rows_in[here, :] = in_refs[j][:rows, :]
            rows_grad[here, :] = in_refs[j][rows:, :]
            continue
        seqs, size = len(in_refs), in_refs[0].shape[1]
        pieces = jnp.concatenate([ref[j] for ref in in_refs], axis=0)
        row = lax.broadcasted_iota(jnp.int32, (rows, seqs * size), 0)
        source = lax.broadcasted_iota(jnp.int32, (rows, seqs * size), 1)
        wanted = (row // capacity) * size + row % capacity
        wanted = jnp.where(row < seqs * capacity, wanted, -2 * size)
        for target, first in ((rows_in, 0), (rows_grad, capacity)):
            moving = (source == wanted + first).astype(f32).astype(bf16)
            target[here, :] = jnp.dot(moving, pieces, preferred_element_type=f32).astype(bf16)
    for copy in row_puts:
        copy.start()

    def forward(h, carry):
        for first in range(0, TILE, PART):
            cols = pl.ds(pl.multiple_of(h * TILE + first, PART), PART)
            pre_act = jnp.dot(rows_in[...], up_mat[:, cols], preferred_element_type=f32)
            act_grad = lax.dot_general(
                rows_grad[...], down_mat[cols, :], (((1,), (1,)), ((), ())), preferred_element_type=f32
            )
            gate_sig = sigmoid(pre_act)
            acted[:, cols] = (pre_act * gate_sig).astype(bf16)
            slope = gate_sig * (1.0 + pre_act * (1.0 - gate_sig))
            kept[:, cols] = (act_grad * slope).astype(bf16)
        for copy in putting(h):
            copy.start()
        return carry

    lax.fori_loop(0, steps, forward, 0)
    own_row = slot_refs[0].shape[0] - rows
    if before_refs:
        for j in range(parts):
            slot_refs[j][:own_row, :] = before_refs[j][...]

    def backward(d, carry):
        for first in range(0, TILE, PART):
            cols = pl.ds(pl.multiple_of(d * TILE + first, PART), PART)
            term = lax.dot_general(
                kept[...], up_mat[cols, :], (((1,), (1,)), ((), ())), preferred_element_type=f32
            )
            for j in range(parts):
                slot_refs[j][own_row:, cols] = term[j * rows : (j + 1) * rows, :].astype(bf16)
        return carry

    lax.fori_loop(0, features // TILE, backward, 0)
    for copy in row_puts:
        copy.wait()
    for h in range(steps):
        for copy in putting(h):
            copy.wait()


def expert_products(blocks, parts, capacity, up_mat, down_mat, rows, total, first_row, before, kept, earlier=(), stage=4):
    features, hidden = up_mat.shape
    steps = hidden // TILE
    mine = parts * rows
    slot_rows = rows + (before[0].shape[0] if before else 0)
    counts = (len(blocks), 2, len(before), len(earlier), len(kept), parts, 4, 5)
    first_kept = sum(counts[:4])
    out = pl.pallas_call(
        functools.partial(
            expert_body, parts, rows, capacity if blocks[0].ndim == 3 else None, first_row, counts
        ),
        out_shape=tuple(jax.ShapeDtypeStruct((slot_rows, features), bf16) for _ in range(parts))
        + (
            pltpu.HBM((total, features), bf16),
            pltpu.HBM((total, features), bf16),
            pltpu.HBM((total, hidden), bf16),
            pltpu.HBM((total, hidden), bf16),
        ),
        in_specs=whole(len(blocks) + 2 + len(before)) + after(len(earlier)) + far(len(kept)),
        out_specs=tuple(whole(parts) + far(4)),
        input_output_aliases={first_kept + i: parts + i for i in range(len(kept))},
        scratch_shapes=[
            pltpu.VMEM((mine, features), bf16),
            pltpu.VMEM((mine, features), bf16),
            pltpu.VMEM((mine, hidden), bf16),
            pltpu.VMEM((mine, hidden), bf16),
            pltpu.SemaphoreType.DMA((3, max(2, steps))),
        ],
        compiler_params=params(EXPERT_MIB),
        cost_estimate=cost(COSTS[stage]),
        name="expert_products",
    )(*blocks, up_mat, down_mat, *before, *earlier, *kept)
    return out[:parts], out[parts:]


def frame_sums_body(m, experts, frames, pieces, groups, *refs):
    map_refs, slot_refs, out_refs, picking = refs[:2], refs[2 : 2 + experts], refs[-1 - len(groups) : -1], refs[-1]
    total = len(pieces) * frames
    rows = slot_refs[0].shape[0]
    same = lax.broadcasted_iota(jnp.int32, (frames, frames), 0) == lax.broadcasted_iota(
        jnp.int32, (frames, frames), 1
    )
    same = same.astype(f32).astype(bf16)
    col_ids = lax.broadcasted_iota(jnp.int32, (frames, rows), 1)
    for i, (half, k, first_row) in enumerate(pieces):
        columns = lax.dot_general(
            same,
            map_refs[half][m, :, k * frames : (k + 1) * frames].astype(bf16),
            (((1,), (1,)), ((), ())),
            preferred_element_type=f32,
        )
        here = (col_ids - first_row).astype(f32)
        for e in range(experts):
            picking[e, i * frames : (i + 1) * frames, :] = (
                (here == columns[:, e : e + 1]).astype(f32).astype(bf16)
            )

    def feature(d, carry):
        cols = pl.ds(pl.multiple_of(d * PART, PART), PART)
        acc = jnp.zeros((total, PART), f32)
        for e in range(experts):
            acc = acc + jnp.dot(picking[e], slot_refs[e][:, cols], preferred_element_type=f32)
        for group, out_ref in zip(groups, out_refs):
            for place, i in enumerate(group):
                out_ref[place * frames : (place + 1) * frames, cols] = acc[
                    i * frames : (i + 1) * frames, :
                ].astype(out_ref.dtype)
        return carry

    lax.fori_loop(0, slot_refs[0].shape[1] // PART, feature, 0)


def frame_sums(m, maps, blocks, frames, pieces, groups, earlier, handed=()):
    rows, features = blocks[0].shape
    first = 2 + len(blocks) + len(earlier)
    out = pl.pallas_call(
        functools.partial(frame_sums_body, m, len(blocks), frames, pieces, tuple(g for g, _ in groups)),
        out_shape=tuple(pltpu.HBM(h.shape, h.dtype) for h in handed)
        + tuple(
            jax.ShapeDtypeStruct((len(group) * frames, features), kind) for group, kind in groups
        ),
        in_specs=whole(2 + len(blocks)) + after(len(earlier)) + far(len(handed)),
        out_specs=tuple(far(len(handed)) + whole(len(groups))),
        input_output_aliases={first + i: i for i in range(len(handed))},
        scratch_shapes=[pltpu.VMEM((len(blocks), len(pieces) * frames, rows), bf16)],
        compiler_params=params(16),
        cost_estimate=cost(COSTS[8 + m + (len(pieces) == 1)]),
        name="frame_sums",
    )(*maps, *blocks, *earlier, *handed)
    return out[: len(handed)], out[len(handed) :]


def pair_sum_body(own_ref, got_ref, out_ref):
    first = got_ref.shape[0] - own_ref.shape[0]
    out_ref[...] = (own_ref[...] + got_ref[first:, :].astype(f32)).astype(bf16)


def pair_sum(own, got):
    return pl.pallas_call(
        pair_sum_body,
        out_shape=jax.ShapeDtypeStruct(own.shape, bf16),
        in_specs=whole(2),
        out_specs=whole(1)[0],
        compiler_params=params(16),
        cost_estimate=cost(COSTS[15]),
        name="pair_sum",
    )(own, got)


def epilogue_body(m, seqs, last, waits, *refs):
    norm_refs = refs[:seqs]
    (x_all, up_all, conv_ref, mixed_ref, scale_ref, taps_ref, gain_ref) = refs[seqs : seqs + 7]
    before, refs = refs[seqs + 7 : seqs + 7 + 2 * last], refs[seqs + 7 + 2 * last + waits :]
    if last:
        sums_ref, other_ref = before
    prev_ref, term_ref, norm_grad, pad_x, pad_g, parts, gain_parts, x_ref, up_ref, sems = refs
    if last:
        prev_ref[0] = other_ref[...]
        prev_ref = prev_ref.at[1]
    copies = fetching((x_all.at[m], up_all.at[m]), (x_ref, up_ref), sems)
    conv_ref, mixed_ref, scale_ref = conv_ref.at[m], mixed_ref.at[m], scale_ref.at[m]
    frames, features = x_ref.shape
    tap_count = taps_ref.shape[0]
    margin = tap_count // 2
    lead = round_up(margin, 8)
    pad_x[...] = jnp.zeros(pad_x.shape, f32)
    pad_g[...] = jnp.zeros(pad_g.shape, f32)
    scale = scale_ref[...]

    def tiles_sum(values):
        return jnp.sum(values.reshape(frames // 8, 8, LANES), axis=0)

    def gather(c, inner):
        cols = pl.ds(pl.multiple_of(c * LANES, LANES), LANES)
        grad = norm_refs[0][:frames, cols].astype(f32)
        for k in range(1, seqs):
            grad = grad + norm_refs[k][:frames, cols].astype(f32)
        norm_grad[:, cols] = grad
        weighed = grad * mixed_ref[:, cols]
        gain_parts[c] = tiles_sum(weighed * scale)
        return inner + weighed * gain_ref[:, cols]

    inner = lax.fori_loop(0, features // LANES, gather, jnp.zeros((frames, LANES), f32))
    for copy in copies:
        copy.wait()
    pull = scale * scale * scale * (jnp.sum(inner, axis=1, keepdims=True) / features)

    def chunk(c, carry):
        cols = pl.ds(pl.multiple_of(c * LANES, LANES), LANES)
        mixed_grad = (
            up_ref[:, cols].astype(f32)
            + scale * (norm_grad[:, cols] * gain_ref[:, cols])
            - mixed_ref[:, cols] * pull
        )
        conv_grad = mixed_grad * silu_slope(conv_ref[:, cols])
        pad_x[lead : lead + frames, :] = x_ref[:, cols].astype(f32)
        pad_g[lead : lead + frames, :] = conv_grad
        acc = mixed_grad
        for j, rows in shifted(pad_x, [lead + j - margin for j in range(tap_count)], frames):
            parts[8 * j : 8 * j + 8, :] = tiles_sum(conv_grad * rows)
        for j, rows in shifted(pad_g, [lead + margin - j for j in range(tap_count)], frames):
            acc = acc + taps_ref[j, :, cols] * rows
        prev_ref[:, cols] = acc.astype(bf16)
        parts[8 * tap_count :, :] = gain_parts[c]
        sums = parts[pl.ds(0, tap_count + 1, stride=8), :]
        for row in range(1, 8):
            sums = sums + parts[pl.ds(row, tap_count + 1, stride=8), :]
        if last:
            sums = sums + sums_ref[:, cols]
        term_ref[:, cols] = sums.astype(term_ref.dtype)
        return carry

    lax.fori_loop(0, features // LANES, chunk, 0)


def epilogue(m, norm_blocks, x, upstream, saved, taps, gain, before=(), earlier=()):
    _, frames, features = x.shape
    seqs = len(norm_blocks)
    lead = round_up(taps.shape[0] // 2, 8)
    last = bool(before)
    return pl.pallas_call(
        functools.partial(epilogue_body, m, seqs, last, len(earlier)),
        out_shape=(
            jax.ShapeDtypeStruct(x.shape if last else (frames, features), bf16),
            jax.ShapeDtypeStruct((taps.shape[0] + 1, features), bf16 if last else f32),
        ),
        in_specs=whole(seqs) + far(2) + whole(5 + len(before)) + after(len(earlier)),
        out_specs=tuple(whole(2)),
        scratch_shapes=[
            pltpu.VMEM((frames, features), f32),
            pltpu.VMEM((frames + 2 * lead, LANES), f32),
            pltpu.VMEM((frames + 2 * lead, LANES), f32),
            pltpu.VMEM((8 * (taps.shape[0] + 1), LANES), f32),
            pltpu.VMEM((features // LANES, 8, LANES), f32),
        ]
        + [
            pltpu.VMEM((frames, features), bf16),
            pltpu.VMEM((frames, features), bf16),
            pltpu.SemaphoreType.DMA((2,)),
        ],
        compiler_params=params(16),
        cost_estimate=cost(COSTS[11 + m]),
        name="norm_conv_back",
    )(*norm_blocks, x, upstream, *saved, taps, gain, *before, *earlier)


def tree_sum(terms):
    while len(terms) > 1:
        terms = [terms[i] + terms[i + 1] for i in range(0, len(terms), 2)]
    return terms[0]


def last_sum_body(*refs):
    term_refs, taps_ref, gain_ref = refs[:-2], refs[-2], refs[-1]
    tap_count = taps_ref.shape[0]
    total = tree_sum([ref[...].astype(f32) for ref in term_refs])
    for j in range(tap_count):
        taps_ref[j] = total[j : j + 1, :]
    gain_ref[...] = total[tap_count:, :]


def last_sum(terms):
    rows, features = terms[0].shape
    return pl.pallas_call(
        last_sum_body,
        out_shape=(
            jax.ShapeDtypeStruct((rows - 1, 1, features), f32),
            jax.ShapeDtypeStruct((1, features), f32),
        ),
        in_specs=whole(len(terms)),
        out_specs=tuple(whole(2)),
        compiler_params=params(16),
        cost_estimate=cost(COSTS[13]),
        name="last_sum",
    )(*terms)


def to_partner(array, axis, k):
    return lax.ppermute(array, axis, [(i, i ^ k) for i in range(lax.axis_size(axis))])


def from_all(array, axis):
    return [array] + [to_partner(array, axis, k) for k in range(1, lax.axis_size(axis))]


def exchanged(blocks, axis):
    return [blocks[0]] + [to_partner(blocks[k], axis, k) for k in range(1, len(blocks))]


def local(section_input, out_grad, routes, combine, kernel, norm_gain, up_weight, down_weight):
    experts = lax.axis_size("expert")
    seqs = lax.axis_size("dp")
    frames, features = section_input.shape[3:]
    top_count = routes.shape[4]
    capacity = 9 * frames * top_count // (8 * experts)
    taps = kernel.transpose(1, 0, 2)
    up_mat, down_mat = up_weight[0, 0], down_weight[0, 0]
    routes = routes[0, :, 0].transpose(0, 2, 1)
    combine = combine[0, :, 0].transpose(0, 2, 1)
    xs = section_input.reshape(MB, frames, features)
    ups = out_grad.reshape(MB, frames, features)

    sent = first_send(xs, ups, routes, combine, taps, norm_gain)
    pieces = second_send(xs, ups, routes, combine, taps, norm_gain, experts, capacity, sent)
    half = round_up(seqs // 2 * capacity, 8)
    most, last = round_up((seqs - 1) * capacity, 8), round_up(capacity, 8)
    near_places = ((0, capacity), (0, capacity))
    wide_places = ((0, capacity), (2 * capacity, 0))

    first = [sent, to_partner(sent, "dp", 1)]
    near, near_map, pieces = slots(
        first, experts, capacity, frames, near_places, exchanged(pieces, "expert")
    )
    later = passed(to_partner(sent, "dp", 2), near[0])
    first += [later, to_partner(later, "dp", 1)]
    saved = saved_frames(xs, taps, first[1])
    near = exchanged(near, "expert")

    products = functools.partial(
        expert_products,
        parts=experts,
        capacity=capacity,
        up_mat=up_mat,
        down_mat=down_mat,
        total=experts * (2 * half + most + last),
    )
    at = experts * half
    back, kept = products(near, rows=half, first_row=0, before=(), kept=(), earlier=(saved[2],), stage=4)
    pieces = passed(pieces, later)
    later = passed(to_partner(pieces, "dp", 2), back[0])
    second = [pieces, to_partner(pieces, "dp", 1), later, to_partner(later, "dp", 1)]
    wide, wide_map, _ = slots(first[2:], experts, capacity, frames, wide_places, earlier=tuple(near[1:]))
    maps = (near_map, wide_map)
    wide = exchanged(wide, "expert")
    back, kept = products(wide, rows=half, first_row=at, before=back, kept=kept, stage=5)
    first_back = exchanged(back, "expert")
    back, kept = products(second[:-1], rows=most, first_row=2 * at, before=(), kept=kept, stage=6)
    most_back = exchanged(back, "expert")

    _, (own_sum, far_sum, sent) = frame_sums(
        0,
        maps,
        first_back,
        frames,
        ((0, 0, 0), (0, 1, 0), (1, 0, half), (1, 1, half)),
        (((0,), f32), ((2,), f32), ((1, 3), bf16)),
        [back[0]],
    )
    got = to_partner(sent, "dp", 1)
    first_norm = [own_sum, got, to_partner(pair_sum(far_sum, got), "dp", 2)]
    back, kept = products(
        second[-1:], rows=last, first_row=2 * at + experts * most, before=(), kept=kept, stage=7, earlier=(own_sum,)
    )
    last_back = exchanged(back, "expert")
    (all_in, all_grad, all_acted, all_pre), sent = frame_sums(
        1,
        maps,
        most_back,
        frames,
        ((0, 0, 0), (0, 1, 0), (1, 0, 0)),
        (((0,), f32), ((1,), bf16), ((2,), bf16)),
        [],
        kept,
    )
    second_norm = exchanged(sent, "dp")
    over_rows = (((0,), (0,)), ((), ()))
    up_grad = lax.dot_general(all_in, all_pre, over_rows, preferred_element_type=f32).astype(bf16)
    down_grad = lax.dot_general(all_acted, all_grad, over_rows, preferred_element_type=f32).astype(bf16)
    _, sent = frame_sums(1, maps, last_back, frames, ((1, 1, 0),), (((0,), bf16),), [])
    second_norm.append(to_partner(sent[0], "dp", seqs - 1))
    prev, sums = epilogue(0, first_norm, xs, ups, saved, taps, norm_gain, earlier=(up_grad,))
    prev, sums = epilogue(1, second_norm, xs, ups, saved, taps, norm_gain, before=(sums, prev))
    peers = lax.axis_size("pipe")
    handed = lax.ppermute(prev, "pipe", [(i, (i - 1) % peers) for i in range(peers)])
    sums = tree_sum([term.astype(f32) for term in from_all(sums, "expert")]).astype(bf16)
    taps_grad, gain_grad = last_sum(from_all(sums, "dp"))
    return (
        handed[None, :, None],
        taps_grad.transpose(1, 0, 2),
        gain_grad,
        up_grad[None, None],
        down_grad[None, None],
    )


def solution(mesh):
    split = P("pipe", None, ("dp", "expert"), None, None)
    up_split = P("pipe", "expert", None, "dp")
    down_split = P("pipe", "expert", "dp", None)
    return jax.shard_map(
        local,
        mesh=mesh,
        in_specs=(split, split, split, split, P("pipe", None, None), P("pipe", None), up_split, down_split),
        out_specs=(split, P("pipe", None, None), P("pipe", None), up_split, down_split),
        check_vma=False,
    )
```

```python
import functools

import jax
import jax.numpy as jnp
from jax import lax
from jax.experimental import pallas as pl
from jax.experimental.pallas import tpu as pltpu
from jax.sharding import PartitionSpec as P

MB = 2
EPSILON = 1e-06
LANES = 128
TILE = 512
PART = 256
SEND_MIB = 60
EXPERT_MIB = 24
NOWHERE = -512.0
COSTS = (0, 0, 0, 0, 12, 0, 10, 0, 0, 2, 0, 0, 0, 0, 12, 0)
MIB = 1024 * 1024
SMALL = pl.CostEstimate(flops=1, bytes_accessed=1, transcendentals=0)
bf16 = jnp.bfloat16
f32 = jnp.float32


def round_up(value, step):
    return -(-value // step) * step


def params(mib):
    return pltpu.CompilerParams(vmem_limit_bytes=mib * MIB)


def cost(amount):
    return pl.CostEstimate(flops=int(amount * 1.15e9) + 1, bytes_accessed=1, transcendentals=0)


def whole(count):
    return [pl.BlockSpec(memory_space=pltpu.VMEM)] * count


def after(count):
    return [pl.BlockSpec(memory_space=pl.ANY)] * count


def far(count):
    return [pl.BlockSpec(memory_space=pltpu.HBM)] * count


def fetching(sources, targets, sems):
    copies = [
        pltpu.make_async_copy(source, target, sems.at[i])
        for i, (source, target) in enumerate(zip(sources, targets))
    ]
    for copy in copies:
        copy.start()
    return copies


def fetched(sources, targets, sems):
    for copy in fetching(sources, targets, sems):
        copy.wait()


def sigmoid(values):
    return 1.0 / (1.0 + jnp.exp(-values))


def silu_slope(values):
    gate_sig = sigmoid(values)
    return gate_sig * (1.0 + values * (1.0 - gate_sig))


def shifted(pad, starts, frames):
    for residue in range(8):
        group = [(i, start // 8) for i, start in enumerate(starts) if start % 8 == residue]
        if not group:
            continue
        low, high = min(t for _, t in group), max(t for _, t in group)
        first = 8 * low + residue
        block = pad[first : first + 8 * (high - low) + frames, :]
        for i, tile in group:
            yield i, block[8 * (tile - low) : 8 * (tile - low) + frames, :]


def mixed_frames(x_ref, taps_ref, pad, conv_ref, mixed_ref):
    frames, features = x_ref.shape
    tap_count = taps_ref.shape[0]
    margin = tap_count // 2
    lead = round_up(margin, 8)
    pad[...] = jnp.zeros(pad.shape, f32)

    def chunk(c, squares):
        cols = pl.ds(pl.multiple_of(c * LANES, LANES), LANES)
        xs = x_ref[:, cols].astype(f32)
        pad[lead : lead + frames, :] = xs
        acc = jnp.zeros((frames, LANES), f32)
        for j, rows in shifted(pad, [lead + j - margin for j in range(tap_count)], frames):
            acc = acc + taps_ref[j, :, cols] * rows
        mixed = xs + acc * sigmoid(acc)
        if conv_ref is not None:
            conv_ref[:, cols] = acc
        mixed_ref[:, cols] = mixed
        return squares + mixed * mixed

    squares = lax.fori_loop(0, features // LANES, chunk, jnp.zeros((frames, LANES), f32))
    return lax.rsqrt(jnp.sum(squares, axis=1, keepdims=True) / features + EPSILON)


def meta_rows(routes_ref, combine_ref, m):
    own = lax.axis_index("expert").astype(jnp.int32)
    rows = [(routes_ref[m] ^ own).astype(f32)]
    left = combine_ref[m]
    for _ in range(3):
        rows.append(left.astype(bf16).astype(f32))
        left = left - rows[-1]
    return jnp.concatenate(rows, axis=0)


def first_send_body(
    x_all, up_all, routes_all, combine_all, taps_all, gain_all, send_ref, mixed, pad, x_ref, routes_ref,
    combine_ref, taps_ref, gain_ref, sems
):
    frames = x_ref.shape[0]
    fetched(
        (x_all.at[0], up_all.at[0], routes_all, combine_all, taps_all, gain_all),
        (x_ref, send_ref.at[frames : 2 * frames], routes_ref, combine_ref, taps_ref, gain_ref),
        sems,
    )
    scale = mixed_frames(x_ref, taps_ref, pad, None, mixed)
    send_ref[:frames, :] = (mixed[...] * scale * gain_ref[...]).astype(bf16)
    metas = [meta_rows(routes_ref, combine_ref, m) for m in range(MB)]
    send_ref[2 * frames :, :frames] = jnp.concatenate(metas, axis=0).astype(bf16)


def send_scratch(x, routes, combine, taps, gain):
    _, frames, features = x.shape
    return [
        pltpu.VMEM((frames, features), f32),
        pltpu.VMEM((frames + 2 * round_up(taps.shape[0] // 2, 8), LANES), f32),
        pltpu.VMEM((frames, features), bf16),
        pltpu.VMEM(routes.shape, routes.dtype),
        pltpu.VMEM(combine.shape, f32),
        pltpu.VMEM(taps.shape, f32),
        pltpu.VMEM(gain.shape, f32),
        pltpu.SemaphoreType.DMA((6,)),
    ]


def first_send(x, upstream, routes, combine, taps, gain):
    _, frames, features = x.shape
    return pl.pallas_call(
        first_send_body,
        out_shape=jax.ShapeDtypeStruct((2 * frames + 8 * MB, features), bf16),
        in_specs=far(6),
        out_specs=whole(1)[0],
        scratch_shapes=send_scratch(x, routes, combine, taps, gain),
        compiler_params=params(SEND_MIB),
        cost_estimate=cost(COSTS[0]),
        name="first_send",
    )(x, upstream, routes, combine, taps, gain)


def second_send_body(
    experts, capacity, x_all, up_all, routes_all, combine_all, taps_all, gain_all, _, *refs
):
    outs, (mixed, pad, x_ref, routes_ref, combine_ref, taps_ref, gain_ref, sems, joined) = (
        refs[:experts],
        refs[experts:],
    )
    frames, features = x_ref.shape
    fetched(
        (x_all.at[1], up_all.at[1], routes_all, combine_all, taps_all, gain_all),
        (x_ref, joined.at[frames:], routes_ref, combine_ref, taps_ref, gain_ref),
        sems,
    )
    scale = mixed_frames(x_ref, taps_ref, pad, None, mixed)
    joined[:frames, :] = (mixed[...] * scale * gain_ref[...]).astype(bf16)
    slot, weight = slot_map(experts, frames, meta_rows(routes_ref, combine_ref, 1), (0,))
    rows = outs[0].shape[0]
    row_ids = lax.broadcasted_iota(jnp.int32, (rows, frames), 0).astype(f32)
    for e in range(experts):
        normed_row = (row_ids == slot[e : e + 1, :]).astype(f32).astype(bf16)
        chosen = (row_ids - capacity == slot[e : e + 1, :]) & (row_ids >= capacity)
        amount = jnp.sum(jnp.where(chosen, weight[e : e + 1, :], 0.0), axis=1, keepdims=True)
        grad_row = chosen.astype(f32).astype(bf16)
        for first_col in range(0, features, 512):
            cols = slice(first_col, min(first_col + 512, features))
            picked = jnp.dot(grad_row, joined[frames:, cols], preferred_element_type=f32) * amount
            picked = picked + jnp.dot(normed_row, joined[:frames, cols], preferred_element_type=f32)
            outs[e][:, cols] = picked.astype(bf16)


def second_send(x, upstream, routes, combine, taps, gain, experts, capacity, earlier):
    _, frames, features = x.shape
    rows = round_up(2 * capacity, 8)
    return pl.pallas_call(
        functools.partial(second_send_body, experts, capacity),
        out_shape=(jax.ShapeDtypeStruct((rows, features), bf16),) * experts,
        in_specs=far(6) + after(1),
        out_specs=tuple(whole(experts)),
        scratch_shapes=send_scratch(x, routes, combine, taps, gain) + [pltpu.VMEM((2 * frames, features), bf16)],
        compiler_params=params(SEND_MIB),
        cost_estimate=cost(COSTS[14]),
        name="second_send",
    )(x, upstream, routes, combine, taps, gain, earlier)


def saved_body(x_ref, taps_ref, _, conv_ref, mixed_ref, scale_ref, pad):
    for m in range(MB):
        scale_ref[m] = mixed_frames(x_ref.at[m], taps_ref, pad, conv_ref.at[m], mixed_ref.at[m])


def saved_frames(x, taps, earlier):
    lead = round_up(taps.shape[0] // 2, 8)
    return pl.pallas_call(
        saved_body,
        out_shape=(
            jax.ShapeDtypeStruct(x.shape, f32),
            jax.ShapeDtypeStruct(x.shape, f32),
            jax.ShapeDtypeStruct(x.shape[:2] + (1,), f32),
        ),
        in_specs=whole(2) + after(1),
        out_specs=tuple(whole(3)),
        scratch_shapes=[pltpu.VMEM((x.shape[1] + 2 * lead, LANES), f32)],
        compiler_params=params(16),
        cost_estimate=cost(COSTS[1]),
        name="saved_frames",
    )(x, taps, earlier)


def passed_body(*refs):
    pass


def passed(array, earlier):
    return pl.pallas_call(
        passed_body,
        out_shape=jax.ShapeDtypeStruct(array.shape, array.dtype),
        in_specs=after(2),
        out_specs=after(1)[0],
        input_output_aliases={0: 0},
        compiler_params=params(16),
        cost_estimate=SMALL,
        name="passed",
    )(array, earlier)


def slot_map(experts, frames, meta, places):
    total = meta.shape[1]
    padded = round_up(experts, 16)
    named = lax.broadcasted_iota(jnp.int32, (padded, total), 0).astype(f32)
    first, second = meta[0:1, :] == named, meta[1:2, :] == named
    member = first | second
    earlier = lax.broadcasted_iota(jnp.int32, (total, total), 0)
    later = lax.broadcasted_iota(jnp.int32, (total, total), 1)
    before = (earlier < later) & (earlier // frames == later // frames)
    rank = jnp.dot(
        member.astype(f32).astype(bf16),
        before.astype(f32).astype(bf16),
        preferred_element_type=f32,
    )
    seq_of = lax.broadcasted_iota(jnp.int32, (padded, total), 1) // frames
    for k, first_row in enumerate(places):
        rank = jnp.where(seq_of == k, rank + first_row, rank)
    slot = jnp.where(member, rank, NOWHERE)
    first_weight = meta[2:3, :] + meta[4:5, :] + meta[6:7, :]
    second_weight = meta[3:4, :] + meta[5:6, :] + meta[7:8, :]
    weight = jnp.where(first, first_weight, 0.0) + jnp.where(second, second_weight, 0.0)
    return slot, weight


def place(slot, weight, joined, out_ref, first_row, rows):
    row_ids = lax.broadcasted_iota(jnp.int32, (rows, slot.shape[1]), 0).astype(f32)
    chosen = row_ids == slot
    placing = chosen.astype(f32).astype(bf16)
    if weight is not None:
        amount = jnp.sum(jnp.where(chosen, weight, 0.0), axis=1, keepdims=True)
    for first_col in range(0, joined.shape[1], 512):
        cols = slice(first_col, min(first_col + 512, joined.shape[1]))
        picked = jnp.dot(placing, joined[:, cols], preferred_element_type=f32)
        if weight is not None:
            picked = picked * amount
        out_ref[first_row : first_row + rows, cols] = picked.astype(bf16)


def slots_body(experts, frames, places, seqs, waits, *refs):
    block_refs, refs = refs[:seqs], refs[seqs + waits :]
    piece_refs, refs = refs[: len(refs) - experts - 3], refs[len(refs) - experts - 3 :]
    if piece_refs:
        piece_refs, stacked, refs = piece_refs[:-1], piece_refs[-1], refs
        for i, ref in enumerate(piece_refs):
            stacked[i] = ref[...]
    out_refs, (slot_ref, joined, meta) = refs[:experts], refs[experts:]
    total = seqs * frames
    for k in range(seqs):
        here = slice(k * frames, (k + 1) * frames)
        joined[here, :] = block_refs[k][:frames, :]
        joined[total + k * frames : total + (k + 1) * frames, :] = block_refs[k][frames : 2 * frames, :]
        meta[:, here] = block_refs[k][2 * frames :, :frames].astype(f32)
    slot, weight = slot_map(experts, frames, meta[:8, :], places[0])
    slot_ref[0] = slot
    slot_ref[1] = slot_map(experts, frames, meta[8:, :], places[1])[0]
    rows = out_refs[0].shape[0] // 2
    for e in range(experts):
        place(slot[e : e + 1, :], None, joined.at[:total], out_refs[e], 0, rows)
        place(slot[e : e + 1, :], weight[e : e + 1, :], joined.at[total:], out_refs[e], rows, rows)


def slots(blocks, experts, capacity, frames, places, pieces=(), earlier=()):
    features = blocks[0].shape[1]
    seqs = len(blocks)
    rows = round_up(seqs * capacity, 8)
    total = seqs * frames
    together = tuple(jax.ShapeDtypeStruct((len(pieces),) + p.shape, bf16) for p in pieces[:1])
    out = pl.pallas_call(
        functools.partial(slots_body, experts, frames, places, seqs, len(earlier)),
        out_shape=together
        + tuple(jax.ShapeDtypeStruct((2 * rows, features), bf16) for _ in range(experts))
        + (jax.ShapeDtypeStruct((MB, round_up(experts, 16), total), f32),),
        in_specs=whole(seqs) + after(len(earlier)) + whole(len(pieces)),
        out_specs=tuple(whole(len(together) + experts + 1)),
        scratch_shapes=[pltpu.VMEM((2 * total, features), bf16), pltpu.VMEM((8 * MB, total), f32)],
        compiler_params=params(16),
        cost_estimate=cost(COSTS[2 + (not pieces)]),
        name="slots",
    )(*blocks, *earlier, *pieces)
    return out[-1 - experts : -1], out[-1], out[0]


def expert_body(parts, rows, capacity, first_row, counts, *refs):
    cuts = [sum(counts[:i]) for i in range(len(counts) + 1)]
    in_refs, (up_mat, down_mat), before_refs, _, _, slot_refs, kept_far, scratch = (
        refs[cuts[i] : cuts[i + 1]] for i in range(len(counts))
    )
    rows_in, rows_grad, acted, kept, put_sems = scratch
    features, hidden = up_mat.shape
    steps = hidden // TILE
    far_outs = [ref.at[first_row : first_row + parts * rows, :] for ref in kept_far]

    def putting(h):
        cols = pl.ds(pl.multiple_of(h * TILE, TILE), TILE)
        return (
            pltpu.make_async_copy(acted.at[:, cols], far_outs[2].at[:, cols], put_sems.at[0, h]),
            pltpu.make_async_copy(kept.at[:, cols], far_outs[3].at[:, cols], put_sems.at[1, h]),
        )

    row_puts = [
        pltpu.make_async_copy(rows_in, far_outs[0], put_sems.at[2, 0]),
        pltpu.make_async_copy(rows_grad, far_outs[1], put_sems.at[2, 1]),
    ]
    for j in range(parts):
        here = slice(j * rows, (j + 1) * rows)
        if capacity is None:
            rows_in[here, :] = in_refs[j][:rows, :]
            rows_grad[here, :] = in_refs[j][rows:, :]
            continue
        seqs, size = len(in_refs), in_refs[0].shape[1]
        pieces = jnp.concatenate([ref[j] for ref in in_refs], axis=0)
        row = lax.broadcasted_iota(jnp.int32, (rows, seqs * size), 0)
        source = lax.broadcasted_iota(jnp.int32, (rows, seqs * size), 1)
        wanted = (row // capacity) * size + row % capacity
        wanted = jnp.where(row < seqs * capacity, wanted, -2 * size)
        for target, first in ((rows_in, 0), (rows_grad, capacity)):
            moving = (source == wanted + first).astype(f32).astype(bf16)
            target[here, :] = jnp.dot(moving, pieces, preferred_element_type=f32).astype(bf16)
    for copy in row_puts:
        copy.start()

    def forward(h, carry):
        for first in range(0, TILE, PART):
            cols = pl.ds(pl.multiple_of(h * TILE + first, PART), PART)
            pre_act = jnp.dot(rows_in[...], up_mat[:, cols], preferred_element_type=f32)
            act_grad = lax.dot_general(
                rows_grad[...], down_mat[cols, :], (((1,), (1,)), ((), ())), preferred_element_type=f32
            )
            gate_sig = sigmoid(pre_act)
            acted[:, cols] = (pre_act * gate_sig).astype(bf16)
            slope = gate_sig * (1.0 + pre_act * (1.0 - gate_sig))
            kept[:, cols] = (act_grad * slope).astype(bf16)
        for copy in putting(h):
            copy.start()
        return carry

    lax.fori_loop(0, steps, forward, 0)
    own_row = slot_refs[0].shape[0] - rows
    if before_refs:
        for j in range(parts):
            slot_refs[j][:own_row, :] = before_refs[j][...]

    def backward(d, carry):
        for first in range(0, TILE, PART):
            cols = pl.ds(pl.multiple_of(d * TILE + first, PART), PART)
            term = lax.dot_general(
                kept[...], up_mat[cols, :], (((1,), (1,)), ((), ())), preferred_element_type=f32
            )
            for j in range(parts):
                slot_refs[j][own_row:, cols] = term[j * rows : (j + 1) * rows, :].astype(bf16)
        return carry

    lax.fori_loop(0, features // TILE, backward, 0)
    for copy in row_puts:
        copy.wait()
    for h in range(steps):
        for copy in putting(h):
            copy.wait()


def expert_products(blocks, parts, capacity, up_mat, down_mat, rows, total, first_row, before, kept, earlier=(), stage=4):
    features, hidden = up_mat.shape
    steps = hidden // TILE
    mine = parts * rows
    slot_rows = rows + (before[0].shape[0] if before else 0)
    counts = (len(blocks), 2, len(before), len(earlier), len(kept), parts, 4, 5)
    first_kept = sum(counts[:4])
    out = pl.pallas_call(
        functools.partial(
            expert_body, parts, rows, capacity if blocks[0].ndim == 3 else None, first_row, counts
        ),
        out_shape=tuple(jax.ShapeDtypeStruct((slot_rows, features), bf16) for _ in range(parts))
        + (
            pltpu.HBM((total, features), bf16),
            pltpu.HBM((total, features), bf16),
            pltpu.HBM((total, hidden), bf16),
            pltpu.HBM((total, hidden), bf16),
        ),
        in_specs=whole(len(blocks) + 2 + len(before)) + after(len(earlier)) + far(len(kept)),
        out_specs=tuple(whole(parts) + far(4)),
        input_output_aliases={first_kept + i: parts + i for i in range(len(kept))},
        scratch_shapes=[
            pltpu.VMEM((mine, features), bf16),
            pltpu.VMEM((mine, features), bf16),
            pltpu.VMEM((mine, hidden), bf16),
            pltpu.VMEM((mine, hidden), bf16),
            pltpu.SemaphoreType.DMA((3, max(2, steps))),
        ],
        compiler_params=params(EXPERT_MIB),
        cost_estimate=cost(COSTS[stage]),
        name="expert_products",
    )(*blocks, up_mat, down_mat, *before, *earlier, *kept)
    return out[:parts], out[parts:]


def frame_sums_body(m, experts, frames, pieces, groups, *refs):
    map_refs, slot_refs, out_refs, picking = refs[:2], refs[2 : 2 + experts], refs[-1 - len(groups) : -1], refs[-1]
    total = len(pieces) * frames
    rows = slot_refs[0].shape[0]
    same = lax.broadcasted_iota(jnp.int32, (frames, frames), 0) == lax.broadcasted_iota(
        jnp.int32, (frames, frames), 1
    )
    same = same.astype(f32).astype(bf16)
    col_ids = lax.broadcasted_iota(jnp.int32, (frames, rows), 1)
    for i, (half, k, first_row) in enumerate(pieces):
        columns = lax.dot_general(
            same,
            map_refs[half][m, :, k * frames : (k + 1) * frames].astype(bf16),
            (((1,), (1,)), ((), ())),
            preferred_element_type=f32,
        )
        here = (col_ids - first_row).astype(f32)
        for e in range(experts):
            picking[e, i * frames : (i + 1) * frames, :] = (
                (here == columns[:, e : e + 1]).astype(f32).astype(bf16)
            )

    def feature(d, carry):
        cols = pl.ds(pl.multiple_of(d * PART, PART), PART)
        acc = jnp.zeros((total, PART), f32)
        for e in range(experts):
            acc = acc + jnp.dot(picking[e], slot_refs[e][:, cols], preferred_element_type=f32)
        for group, out_ref in zip(groups, out_refs):
            for place, i in enumerate(group):
                out_ref[place * frames : (place + 1) * frames, cols] = acc[
                    i * frames : (i + 1) * frames, :
                ].astype(out_ref.dtype)
        return carry

    lax.fori_loop(0, slot_refs[0].shape[1] // PART, feature, 0)


def frame_sums(m, maps, blocks, frames, pieces, groups, earlier, handed=()):
    rows, features = blocks[0].shape
    first = 2 + len(blocks) + len(earlier)
    out = pl.pallas_call(
        functools.partial(frame_sums_body, m, len(blocks), frames, pieces, tuple(g for g, _ in groups)),
        out_shape=tuple(pltpu.HBM(h.shape, h.dtype) for h in handed)
        + tuple(
            jax.ShapeDtypeStruct((len(group) * frames, features), kind) for group, kind in groups
        ),
        in_specs=whole(2 + len(blocks)) + after(len(earlier)) + far(len(handed)),
        out_specs=tuple(far(len(handed)) + whole(len(groups))),
        input_output_aliases={first + i: i for i in range(len(handed))},
        scratch_shapes=[pltpu.VMEM((len(blocks), len(pieces) * frames, rows), bf16)],
        compiler_params=params(16),
        cost_estimate=cost(COSTS[8 + m + (len(pieces) == 1)]),
        name="frame_sums",
    )(*maps, *blocks, *earlier, *handed)
    return out[: len(handed)], out[len(handed) :]


def pair_sum_body(own_ref, got_ref, out_ref):
    first = got_ref.shape[0] - own_ref.shape[0]
    out_ref[...] = (own_ref[...] + got_ref[first:, :].astype(f32)).astype(bf16)


def pair_sum(own, got):
    return pl.pallas_call(
        pair_sum_body,
        out_shape=jax.ShapeDtypeStruct(own.shape, bf16),
        in_specs=whole(2),
        out_specs=whole(1)[0],
        compiler_params=params(16),
        cost_estimate=cost(COSTS[15]),
        name="pair_sum",
    )(own, got)


def epilogue_body(m, seqs, last, waits, *refs):
    norm_refs = refs[:seqs]
    (x_all, up_all, conv_ref, mixed_ref, scale_ref, taps_ref, gain_ref) = refs[seqs : seqs + 7]
    before, refs = refs[seqs + 7 : seqs + 7 + 2 * last], refs[seqs + 7 + 2 * last + waits :]
    if last:
        sums_ref, other_ref = before
    prev_ref, term_ref, norm_grad, pad_x, pad_g, parts, gain_parts, x_ref, up_ref, sems = refs
    if last:
        prev_ref[0] = other_ref[...]
        prev_ref = prev_ref.at[1]
    copies = fetching((x_all.at[m], up_all.at[m]), (x_ref, up_ref), sems)
    conv_ref, mixed_ref, scale_ref = conv_ref.at[m], mixed_ref.at[m], scale_ref.at[m]
    frames, features = x_ref.shape
    tap_count = taps_ref.shape[0]
    margin = tap_count // 2
    lead = round_up(margin, 8)
    pad_x[...] = jnp.zeros(pad_x.shape, f32)
    pad_g[...] = jnp.zeros(pad_g.shape, f32)
    scale = scale_ref[...]

    def tiles_sum(values):
        return jnp.sum(values.reshape(frames // 8, 8, LANES), axis=0)

    def gather(c, inner):
        cols = pl.ds(pl.multiple_of(c * LANES, LANES), LANES)
        grad = norm_refs[0][:frames, cols].astype(f32)
        for k in range(1, seqs):
            grad = grad + norm_refs[k][:frames, cols].astype(f32)
        norm_grad[:, cols] = grad
        weighed = grad * mixed_ref[:, cols]
        gain_parts[c] = tiles_sum(weighed * scale)
        return inner + weighed * gain_ref[:, cols]

    inner = lax.fori_loop(0, features // LANES, gather, jnp.zeros((frames, LANES), f32))
    for copy in copies:
        copy.wait()
    pull = scale * scale * scale * (jnp.sum(inner, axis=1, keepdims=True) / features)

    def chunk(c, carry):
        cols = pl.ds(pl.multiple_of(c * LANES, LANES), LANES)
        mixed_grad = (
            up_ref[:, cols].astype(f32)
            + scale * (norm_grad[:, cols] * gain_ref[:, cols])
            - mixed_ref[:, cols] * pull
        )
        conv_grad = mixed_grad * silu_slope(conv_ref[:, cols])
        pad_x[lead : lead + frames, :] = x_ref[:, cols].astype(f32)
        pad_g[lead : lead + frames, :] = conv_grad
        acc = mixed_grad
        for j, rows in shifted(pad_x, [lead + j - margin for j in range(tap_count)], frames):
            parts[8 * j : 8 * j + 8, :] = tiles_sum(conv_grad * rows)
        for j, rows in shifted(pad_g, [lead + margin - j for j in range(tap_count)], frames):
            acc = acc + taps_ref[j, :, cols] * rows
        prev_ref[:, cols] = acc.astype(bf16)
        parts[8 * tap_count :, :] = gain_parts[c]
        sums = parts[pl.ds(0, tap_count + 1, stride=8), :]
        for row in range(1, 8):
            sums = sums + parts[pl.ds(row, tap_count + 1, stride=8), :]
        if last:
            sums = sums + sums_ref[:, cols]
        term_ref[:, cols] = sums.astype(term_ref.dtype)
        return carry

    lax.fori_loop(0, features // LANES, chunk, 0)


def epilogue(m, norm_blocks, x, upstream, saved, taps, gain, before=(), earlier=()):
    _, frames, features = x.shape
    seqs = len(norm_blocks)
    lead = round_up(taps.shape[0] // 2, 8)
    last = bool(before)
    return pl.pallas_call(
        functools.partial(epilogue_body, m, seqs, last, len(earlier)),
        out_shape=(
            jax.ShapeDtypeStruct(x.shape if last else (frames, features), bf16),
            jax.ShapeDtypeStruct((taps.shape[0] + 1, features), bf16 if last else f32),
        ),
        in_specs=whole(seqs) + far(2) + whole(5 + len(before)) + after(len(earlier)),
        out_specs=tuple(whole(2)),
        scratch_shapes=[
            pltpu.VMEM((frames, features), f32),
            pltpu.VMEM((frames + 2 * lead, LANES), f32),
            pltpu.VMEM((frames + 2 * lead, LANES), f32),
            pltpu.VMEM((8 * (taps.shape[0] + 1), LANES), f32),
            pltpu.VMEM((features // LANES, 8, LANES), f32),
        ]
        + [
            pltpu.VMEM((frames, features), bf16),
            pltpu.VMEM((frames, features), bf16),
            pltpu.SemaphoreType.DMA((2,)),
        ],
        compiler_params=params(16),
        cost_estimate=cost(COSTS[11 + m]),
        name="norm_conv_back",
    )(*norm_blocks, x, upstream, *saved, taps, gain, *before, *earlier)


def tree_sum(terms):
    while len(terms) > 1:
        terms = [terms[i] + terms[i + 1] for i in range(0, len(terms), 2)]
    return terms[0]


def last_sum_body(*refs):
    term_refs, taps_ref, gain_ref = refs[:-2], refs[-2], refs[-1]
    tap_count = taps_ref.shape[0]
    total = tree_sum([ref[...].astype(f32) for ref in term_refs])
    for j in range(tap_count):
        taps_ref[j] = total[j : j + 1, :]
    gain_ref[...] = total[tap_count:, :]


def last_sum(terms):
    rows, features = terms[0].shape
    return pl.pallas_call(
        last_sum_body,
        out_shape=(
            jax.ShapeDtypeStruct((rows - 1, 1, features), f32),
            jax.ShapeDtypeStruct((1, features), f32),
        ),
        in_specs=whole(len(terms)),
        out_specs=tuple(whole(2)),
        compiler_params=params(16),
        cost_estimate=cost(COSTS[13]),
        name="last_sum",
    )(*terms)


def to_partner(array, axis, k):
    return lax.ppermute(array, axis, [(i, i ^ k) for i in range(lax.axis_size(axis))])


def from_all(array, axis):
    return [array] + [to_partner(array, axis, k) for k in range(1, lax.axis_size(axis))]


def exchanged(blocks, axis):
    return [blocks[0]] + [to_partner(blocks[k], axis, k) for k in range(1, len(blocks))]


def local(section_input, out_grad, routes, combine, kernel, norm_gain, up_weight, down_weight):
    experts = lax.axis_size("expert")
    seqs = lax.axis_size("dp")
    frames, features = section_input.shape[3:]
    top_count = routes.shape[4]
    capacity = 9 * frames * top_count // (8 * experts)
    taps = kernel.transpose(1, 0, 2)
    up_mat, down_mat = up_weight[0, 0], down_weight[0, 0]
    routes = routes[0, :, 0].transpose(0, 2, 1)
    combine = combine[0, :, 0].transpose(0, 2, 1)
    xs = section_input.reshape(MB, frames, features)
    ups = out_grad.reshape(MB, frames, features)

    sent = first_send(xs, ups, routes, combine, taps, norm_gain)
    pieces = second_send(xs, ups, routes, combine, taps, norm_gain, experts, capacity, sent)
    half = round_up(seqs // 2 * capacity, 8)
    most, last = round_up((seqs - 1) * capacity, 8), round_up(capacity, 8)
    near_places = ((0, capacity), (0, capacity))
    wide_places = ((0, capacity), (2 * capacity, 0))

    first = [sent, to_partner(sent, "dp", 1)]
    near, near_map, pieces = slots(
        first, experts, capacity, frames, near_places, exchanged(pieces, "expert")
    )
    later = passed(to_partner(sent, "dp", 2), near[0])
    first += [later, to_partner(later, "dp", 1)]
    saved = saved_frames(xs, taps, first[1])
    near = exchanged(near, "expert")

    products = functools.partial(
        expert_products,
        parts=experts,
        capacity=capacity,
        up_mat=up_mat,
        down_mat=down_mat,
        total=experts * (2 * half + most + last),
    )
    at = experts * half
    back, kept = products(near, rows=half, first_row=0, before=(), kept=(), earlier=(saved[2],), stage=4)
    pieces = passed(pieces, later)
    later = passed(to_partner(pieces, "dp", 2), back[0])
    second = [pieces, to_partner(pieces, "dp", 1), later, to_partner(later, "dp", 1)]
    wide, wide_map, _ = slots(first[2:], experts, capacity, frames, wide_places)
    maps = (near_map, wide_map)
    wide = exchanged(wide, "expert")
    back, kept = products(wide, rows=half, first_row=at, before=back, kept=kept, stage=5)
    first_back = exchanged(back, "expert")
    back, kept = products(second[:-1], rows=most, first_row=2 * at, before=(), kept=kept, stage=6)
    most_back = exchanged(back, "expert")

    _, (own_sum, far_sum, sent) = frame_sums(
        0,
        maps,
        first_back,
        frames,
        ((0, 0, 0), (0, 1, 0), (1, 0, half), (1, 1, half)),
        (((0,), f32), ((2,), f32), ((1, 3), bf16)),
        [back[0]],
    )
    got = to_partner(sent, "dp", 1)
    first_norm = [own_sum, got, to_partner(pair_sum(far_sum, got), "dp", 2)]
    back, kept = products(
        second[-1:], rows=last, first_row=2 * at + experts * most, before=(), kept=kept, stage=7, earlier=(own_sum,)
    )
    last_back = exchanged(back, "expert")
    (all_in, all_grad, all_acted, all_pre), sent = frame_sums(
        1,
        maps,
        most_back,
        frames,
        ((0, 0, 0), (0, 1, 0), (1, 0, 0)),
        (((0,), f32), ((1,), bf16), ((2,), bf16)),
        [],
        kept,
    )
    second_norm = exchanged(sent, "dp")
    over_rows = (((0,), (0,)), ((), ()))
    up_grad = lax.dot_general(all_in, all_pre, over_rows, preferred_element_type=f32).astype(bf16)
    down_grad = lax.dot_general(all_acted, all_grad, over_rows, preferred_element_type=f32).astype(bf16)
    _, sent = frame_sums(1, maps, last_back, frames, ((1, 1, 0),), (((0,), bf16),), [])
    second_norm.append(to_partner(sent[0], "dp", seqs - 1))
    prev, sums = epilogue(0, first_norm, xs, ups, saved, taps, norm_gain)
    prev, sums = epilogue(1, second_norm, xs, ups, saved, taps, norm_gain, before=(sums, prev))
    peers = lax.axis_size("pipe")
    handed = lax.ppermute(prev, "pipe", [(i, (i - 1) % peers) for i in range(peers)])
    sums = tree_sum([term.astype(f32) for term in from_all(sums, "expert")]).astype(bf16)
    taps_grad, gain_grad = last_sum(from_all(sums, "dp"))
    return (
        handed[None, :, None],
        taps_grad.transpose(1, 0, 2),
        gain_grad,
        up_grad[None, None],
        down_grad[None, None],
    )


def solution(mesh):
    split = P("pipe", None, ("dp", "expert"), None, None)
    up_split = P("pipe", "expert", None, "dp")
    down_split = P("pipe", "expert", "dp", None)
    return jax.shard_map(
        local,
        mesh=mesh,
        in_specs=(split, split, split, split, P("pipe", None, None), P("pipe", None), up_split, down_split),
        out_specs=(split, P("pipe", None, None), P("pipe", None), up_split, down_split),
        check_vma=False,
    )
```

```python
import functools

import jax
import jax.numpy as jnp
from jax import lax
from jax.experimental import pallas as pl
from jax.experimental.pallas import tpu as pltpu
from jax.sharding import PartitionSpec as P

MB = 2
EPSILON = 1e-06
LANES = 128
TILE = 512
PART = 256
SEND_MIB = 60
EXPERT_MIB = 24
NOWHERE = -512.0
COSTS = (0, 0, 0, 0, 12, 0, 10, 0, 0, 2, 0, 0, 0, 0, 12, 0)
MIB = 1024 * 1024
SMALL = pl.CostEstimate(flops=1, bytes_accessed=1, transcendentals=0)
bf16 = jnp.bfloat16
f32 = jnp.float32


def round_up(value, step):
    return -(-value // step) * step


def params(mib):
    return pltpu.CompilerParams(vmem_limit_bytes=mib * MIB)


def cost(amount):
    return pl.CostEstimate(flops=int(amount * 1.15e9) + 1, bytes_accessed=1, transcendentals=0)


def whole(count):
    return [pl.BlockSpec(memory_space=pltpu.VMEM)] * count


def after(count):
    return [pl.BlockSpec(memory_space=pl.ANY)] * count


def far(count):
    return [pl.BlockSpec(memory_space=pltpu.HBM)] * count


def fetching(sources, targets, sems):
    copies = [
        pltpu.make_async_copy(source, target, sems.at[i])
        for i, (source, target) in enumerate(zip(sources, targets))
    ]
    for copy in copies:
        copy.start()
    return copies


def fetched(sources, targets, sems):
    for copy in fetching(sources, targets, sems):
        copy.wait()


def sigmoid(values):
    return 1.0 / (1.0 + jnp.exp(-values))


def silu_slope(values):
    gate_sig = sigmoid(values)
    return gate_sig * (1.0 + values * (1.0 - gate_sig))


def shifted(pad, starts, frames):
    for residue in range(8):
        group = [(i, start // 8) for i, start in enumerate(starts) if start % 8 == residue]
        if not group:
            continue
        low, high = min(t for _, t in group), max(t for _, t in group)
        first = 8 * low + residue
        block = pad[first : first + 8 * (high - low) + frames, :]
        for i, tile in group:
            yield i, block[8 * (tile - low) : 8 * (tile - low) + frames, :]


def mixed_frames(x_ref, taps_ref, pad, conv_ref, mixed_ref):
    frames, features = x_ref.shape
    tap_count = taps_ref.shape[0]
    margin = tap_count // 2
    lead = round_up(margin, 8)
    pad[...] = jnp.zeros(pad.shape, f32)

    def chunk(c, squares):
        cols = pl.ds(pl.multiple_of(c * LANES, LANES), LANES)
        xs = x_ref[:, cols].astype(f32)
        pad[lead : lead + frames, :] = xs
        acc = jnp.zeros((frames, LANES), f32)
        for j, rows in shifted(pad, [lead + j - margin for j in range(tap_count)], frames):
            acc = acc + taps_ref[j, :, cols] * rows
        mixed = xs + acc * sigmoid(acc)
        if conv_ref is not None:
            conv_ref[:, cols] = acc
        mixed_ref[:, cols] = mixed
        return squares + mixed * mixed

    squares = lax.fori_loop(0, features // LANES, chunk, jnp.zeros((frames, LANES), f32), unroll=2)
    return lax.rsqrt(jnp.sum(squares, axis=1, keepdims=True) / features + EPSILON)


def meta_rows(routes_ref, combine_ref, m):
    own = lax.axis_index("expert").astype(jnp.int32)
    rows = [(routes_ref[m] ^ own).astype(f32)]
    left = combine_ref[m]
    for _ in range(3):
        rows.append(left.astype(bf16).astype(f32))
        left = left - rows[-1]
    return jnp.concatenate(rows, axis=0)


def first_send_body(
    x_all, up_all, routes_all, combine_all, taps_all, gain_all, send_ref, mixed, pad, x_ref, routes_ref,
    combine_ref, taps_ref, gain_ref, sems
):
    frames = x_ref.shape[0]
    fetched(
        (x_all.at[0], up_all.at[0], routes_all, combine_all, taps_all, gain_all),
        (x_ref, send_ref.at[frames : 2 * frames], routes_ref, combine_ref, taps_ref, gain_ref),
        sems,
    )
    scale = mixed_frames(x_ref, taps_ref, pad, None, mixed)
    send_ref[:frames, :] = (mixed[...] * scale * gain_ref[...]).astype(bf16)
    metas = [meta_rows(routes_ref, combine_ref, m) for m in range(MB)]
    send_ref[2 * frames :, :frames] = jnp.concatenate(metas, axis=0).astype(bf16)


def send_scratch(x, routes, combine, taps, gain):
    _, frames, features = x.shape
    return [
        pltpu.VMEM((frames, features), f32),
        pltpu.VMEM((frames + 2 * round_up(taps.shape[0] // 2, 8), LANES), f32),
        pltpu.VMEM((frames, features), bf16),
        pltpu.VMEM(routes.shape, routes.dtype),
        pltpu.VMEM(combine.shape, f32),
        pltpu.VMEM(taps.shape, f32),
        pltpu.VMEM(gain.shape, f32),
        pltpu.SemaphoreType.DMA((6,)),
    ]


def first_send(x, upstream, routes, combine, taps, gain):
    _, frames, features = x.shape
    return pl.pallas_call(
        first_send_body,
        out_shape=jax.ShapeDtypeStruct((2 * frames + 8 * MB, features), bf16),
        in_specs=far(6),
        out_specs=whole(1)[0],
        scratch_shapes=send_scratch(x, routes, combine, taps, gain),
        compiler_params=params(SEND_MIB),
        cost_estimate=cost(COSTS[0]),
        name="first_send",
    )(x, upstream, routes, combine, taps, gain)


def second_send_body(
    experts, capacity, x_all, up_all, routes_all, combine_all, taps_all, gain_all, _, *refs
):
    outs, (mixed, pad, x_ref, routes_ref, combine_ref, taps_ref, gain_ref, sems, joined) = (
        refs[:experts],
        refs[experts:],
    )
    frames, features = x_ref.shape
    fetched(
        (x_all.at[1], up_all.at[1], routes_all, combine_all, taps_all, gain_all),
        (x_ref, joined.at[frames:], routes_ref, combine_ref, taps_ref, gain_ref),
        sems,
    )
    scale = mixed_frames(x_ref, taps_ref, pad, None, mixed)
    joined[:frames, :] = (mixed[...] * scale * gain_ref[...]).astype(bf16)
    slot, weight = slot_map(experts, frames, meta_rows(routes_ref, combine_ref, 1), (0,))
    rows = outs[0].shape[0]
    row_ids = lax.broadcasted_iota(jnp.int32, (rows, frames), 0).astype(f32)
    for e in range(experts):
        normed_row = (row_ids == slot[e : e + 1, :]).astype(f32).astype(bf16)
        chosen = (row_ids - capacity == slot[e : e + 1, :]) & (row_ids >= capacity)
        amount = jnp.sum(jnp.where(chosen, weight[e : e + 1, :], 0.0), axis=1, keepdims=True)
        grad_row = chosen.astype(f32).astype(bf16)
        for first_col in range(0, features, 512):
            cols = slice(first_col, min(first_col + 512, features))
            picked = jnp.dot(grad_row, joined[frames:, cols], preferred_element_type=f32) * amount
            picked = picked + jnp.dot(normed_row, joined[:frames, cols], preferred_element_type=f32)
            outs[e][:, cols] = picked.astype(bf16)


def second_send(x, upstream, routes, combine, taps, gain, experts, capacity, earlier):
    _, frames, features = x.shape
    rows = round_up(2 * capacity, 8)
    return pl.pallas_call(
        functools.partial(second_send_body, experts, capacity),
        out_shape=(jax.ShapeDtypeStruct((rows, features), bf16),) * experts,
        in_specs=far(6) + after(1),
        out_specs=tuple(whole(experts)),
        scratch_shapes=send_scratch(x, routes, combine, taps, gain) + [pltpu.VMEM((2 * frames, features), bf16)],
        compiler_params=params(SEND_MIB),
        cost_estimate=cost(COSTS[14]),
        name="second_send",
    )(x, upstream, routes, combine, taps, gain, earlier)


def saved_body(x_ref, taps_ref, _, conv_ref, mixed_ref, scale_ref, pad):
    for m in range(MB):
        scale_ref[m] = mixed_frames(x_ref.at[m], taps_ref, pad, conv_ref.at[m], mixed_ref.at[m])


def saved_frames(x, taps, earlier):
    lead = round_up(taps.shape[0] // 2, 8)
    return pl.pallas_call(
        saved_body,
        out_shape=(
            jax.ShapeDtypeStruct(x.shape, f32),
            jax.ShapeDtypeStruct(x.shape, f32),
            jax.ShapeDtypeStruct(x.shape[:2] + (1,), f32),
        ),
        in_specs=whole(2) + after(1),
        out_specs=tuple(whole(3)),
        scratch_shapes=[pltpu.VMEM((x.shape[1] + 2 * lead, LANES), f32)],
        compiler_params=params(16),
        cost_estimate=cost(COSTS[1]),
        name="saved_frames",
    )(x, taps, earlier)


def passed_body(*refs):
    pass


def passed(array, earlier):
    return pl.pallas_call(
        passed_body,
        out_shape=jax.ShapeDtypeStruct(array.shape, array.dtype),
        in_specs=after(2),
        out_specs=after(1)[0],
        input_output_aliases={0: 0},
        compiler_params=params(16),
        cost_estimate=SMALL,
        name="passed",
    )(array, earlier)


def slot_map(experts, frames, meta, places):
    total = meta.shape[1]
    padded = round_up(experts, 16)
    named = lax.broadcasted_iota(jnp.int32, (padded, total), 0).astype(f32)
    first, second = meta[0:1, :] == named, meta[1:2, :] == named
    member = first | second
    earlier = lax.broadcasted_iota(jnp.int32, (total, total), 0)
    later = lax.broadcasted_iota(jnp.int32, (total, total), 1)
    before = (earlier < later) & (earlier // frames == later // frames)
    rank = jnp.dot(
        member.astype(f32).astype(bf16),
        before.astype(f32).astype(bf16),
        preferred_element_type=f32,
    )
    seq_of = lax.broadcasted_iota(jnp.int32, (padded, total), 1) // frames
    for k, first_row in enumerate(places):
        rank = jnp.where(seq_of == k, rank + first_row, rank)
    slot = jnp.where(member, rank, NOWHERE)
    first_weight = meta[2:3, :] + meta[4:5, :] + meta[6:7, :]
    second_weight = meta[3:4, :] + meta[5:6, :] + meta[7:8, :]
    weight = jnp.where(first, first_weight, 0.0) + jnp.where(second, second_weight, 0.0)
    return slot, weight


def place(slot, weight, joined, out_ref, first_row, rows):
    row_ids = lax.broadcasted_iota(jnp.int32, (rows, slot.shape[1]), 0).astype(f32)
    chosen = row_ids == slot
    placing = chosen.astype(f32).astype(bf16)
    if weight is not None:
        amount = jnp.sum(jnp.where(chosen, weight, 0.0), axis=1, keepdims=True)
    for first_col in range(0, joined.shape[1], 512):
        cols = slice(first_col, min(first_col + 512, joined.shape[1]))
        picked = jnp.dot(placing, joined[:, cols], preferred_element_type=f32)
        if weight is not None:
            picked = picked * amount
        out_ref[first_row : first_row + rows, cols] = picked.astype(bf16)


def slots_body(experts, frames, places, seqs, waits, *refs):
    block_refs, refs = refs[:seqs], refs[seqs + waits :]
    piece_refs, refs = refs[: len(refs) - experts - 3], refs[len(refs) - experts - 3 :]
    if piece_refs:
        piece_refs, stacked, refs = piece_refs[:-1], piece_refs[-1], refs
        for i, ref in enumerate(piece_refs):
            stacked[i] = ref[...]
    out_refs, (slot_ref, joined, meta) = refs[:experts], refs[experts:]
    total = seqs * frames
    for k in range(seqs):
        here = slice(k * frames, (k + 1) * frames)
        joined[here, :] = block_refs[k][:frames, :]
        joined[total + k * frames : total + (k + 1) * frames, :] = block_refs[k][frames : 2 * frames, :]
        meta[:, here] = block_refs[k][2 * frames :, :frames].astype(f32)
    slot, weight = slot_map(experts, frames, meta[:8, :], places[0])
    slot_ref[0] = slot
    slot_ref[1] = slot_map(experts, frames, meta[8:, :], places[1])[0]
    rows = out_refs[0].shape[0] // 2
    for e in range(experts):
        place(slot[e : e + 1, :], None, joined.at[:total], out_refs[e], 0, rows)
        place(slot[e : e + 1, :], weight[e : e + 1, :], joined.at[total:], out_refs[e], rows, rows)


def slots(blocks, experts, capacity, frames, places, pieces=(), earlier=()):
    features = blocks[0].shape[1]
    seqs = len(blocks)
    rows = round_up(seqs * capacity, 8)
    total = seqs * frames
    together = tuple(jax.ShapeDtypeStruct((len(pieces),) + p.shape, bf16) for p in pieces[:1])
    out = pl.pallas_call(
        functools.partial(slots_body, experts, frames, places, seqs, len(earlier)),
        out_shape=together
        + tuple(jax.ShapeDtypeStruct((2 * rows, features), bf16) for _ in range(experts))
        + (jax.ShapeDtypeStruct((MB, round_up(experts, 16), total), f32),),
        in_specs=whole(seqs) + after(len(earlier)) + whole(len(pieces)),
        out_specs=tuple(whole(len(together) + experts + 1)),
        scratch_shapes=[pltpu.VMEM((2 * total, features), bf16), pltpu.VMEM((8 * MB, total), f32)],
        compiler_params=params(16),
        cost_estimate=cost(COSTS[2 + (not pieces)]),
        name="slots",
    )(*blocks, *earlier, *pieces)
    return out[-1 - experts : -1], out[-1], out[0]


def expert_body(parts, rows, capacity, first_row, counts, *refs):
    cuts = [sum(counts[:i]) for i in range(len(counts) + 1)]
    in_refs, (up_mat, down_mat), before_refs, _, _, slot_refs, kept_far, scratch = (
        refs[cuts[i] : cuts[i + 1]] for i in range(len(counts))
    )
    rows_in, rows_grad, acted, kept, put_sems = scratch
    features, hidden = up_mat.shape
    steps = hidden // TILE
    far_outs = [ref.at[first_row : first_row + parts * rows, :] for ref in kept_far]

    def putting(h):
        cols = pl.ds(pl.multiple_of(h * TILE, TILE), TILE)
        return (
            pltpu.make_async_copy(acted.at[:, cols], far_outs[2].at[:, cols], put_sems.at[0, h]),
            pltpu.make_async_copy(kept.at[:, cols], far_outs[3].at[:, cols], put_sems.at[1, h]),
        )

    row_puts = [
        pltpu.make_async_copy(rows_in, far_outs[0], put_sems.at[2, 0]),
        pltpu.make_async_copy(rows_grad, far_outs[1], put_sems.at[2, 1]),
    ]
    for j in range(parts):
        here = slice(j * rows, (j + 1) * rows)
        if capacity is None:
            rows_in[here, :] = in_refs[j][:rows, :]
            rows_grad[here, :] = in_refs[j][rows:, :]
            continue
        seqs, size = len(in_refs), in_refs[0].shape[1]
        pieces = jnp.concatenate([ref[j] for ref in in_refs], axis=0)
        row = lax.broadcasted_iota(jnp.int32, (rows, seqs * size), 0)
        source = lax.broadcasted_iota(jnp.int32, (rows, seqs * size), 1)
        wanted = (row // capacity) * size + row % capacity
        wanted = jnp.where(row < seqs * capacity, wanted, -2 * size)
        for target, first in ((rows_in, 0), (rows_grad, capacity)):
            moving = (source == wanted + first).astype(f32).astype(bf16)
            target[here, :] = jnp.dot(moving, pieces, preferred_element_type=f32).astype(bf16)
    for copy in row_puts:
        copy.start()

    def forward(h, carry):
        for first in range(0, TILE, PART):
            cols = pl.ds(pl.multiple_of(h * TILE + first, PART), PART)
            pre_act = jnp.dot(rows_in[...], up_mat[:, cols], preferred_element_type=f32)
            act_grad = lax.dot_general(
                rows_grad[...], down_mat[cols, :], (((1,), (1,)), ((), ())), preferred_element_type=f32
            )
            gate_sig = sigmoid(pre_act)
            acted[:, cols] = (pre_act * gate_sig).astype(bf16)
            slope = gate_sig * (1.0 + pre_act * (1.0 - gate_sig))
            kept[:, cols] = (act_grad * slope).astype(bf16)
        for copy in putting(h):
            copy.start()
        return carry

    lax.fori_loop(0, steps, forward, 0)
    own_row = slot_refs[0].shape[0] - rows
    if before_refs:
        for j in range(parts):
            slot_refs[j][:own_row, :] = before_refs[j][...]

    def backward(d, carry):
        for first in range(0, TILE, PART):
            cols = pl.ds(pl.multiple_of(d * TILE + first, PART), PART)
            term = lax.dot_general(
                kept[...], up_mat[cols, :], (((1,), (1,)), ((), ())), preferred_element_type=f32
            )
            for j in range(parts):
                slot_refs[j][own_row:, cols] = term[j * rows : (j + 1) * rows, :].astype(bf16)
        return carry

    lax.fori_loop(0, features // TILE, backward, 0)
    for copy in row_puts:
        copy.wait()
    for h in range(steps):
        for copy in putting(h):
            copy.wait()


def expert_products(blocks, parts, capacity, up_mat, down_mat, rows, total, first_row, before, kept, earlier=(), stage=4):
    features, hidden = up_mat.shape
    steps = hidden // TILE
    mine = parts * rows
    slot_rows = rows + (before[0].shape[0] if before else 0)
    counts = (len(blocks), 2, len(before), len(earlier), len(kept), parts, 4, 5)
    first_kept = sum(counts[:4])
    out = pl.pallas_call(
        functools.partial(
            expert_body, parts, rows, capacity if blocks[0].ndim == 3 else None, first_row, counts
        ),
        out_shape=tuple(jax.ShapeDtypeStruct((slot_rows, features), bf16) for _ in range(parts))
        + (
            pltpu.HBM((total, features), bf16),
            pltpu.HBM((total, features), bf16),
            pltpu.HBM((total, hidden), bf16),
            pltpu.HBM((total, hidden), bf16),
        ),
        in_specs=whole(len(blocks) + 2 + len(before)) + after(len(earlier)) + far(len(kept)),
        out_specs=tuple(whole(parts) + far(4)),
        input_output_aliases={first_kept + i: parts + i for i in range(len(kept))},
        scratch_shapes=[
            pltpu.VMEM((mine, features), bf16),
            pltpu.VMEM((mine, features), bf16),
            pltpu.VMEM((mine, hidden), bf16),
            pltpu.VMEM((mine, hidden), bf16),
            pltpu.SemaphoreType.DMA((3, max(2, steps))),
        ],
        compiler_params=params(EXPERT_MIB),
        cost_estimate=cost(COSTS[stage]),
        name="expert_products",
    )(*blocks, up_mat, down_mat, *before, *earlier, *kept)
    return out[:parts], out[parts:]


def frame_sums_body(m, experts, frames, pieces, groups, *refs):
    map_refs, slot_refs, out_refs, picking = refs[:2], refs[2 : 2 + experts], refs[-1 - len(groups) : -1], refs[-1]
    total = len(pieces) * frames
    rows = slot_refs[0].shape[0]
    same = lax.broadcasted_iota(jnp.int32, (frames, frames), 0) == lax.broadcasted_iota(
        jnp.int32, (frames, frames), 1
    )
    same = same.astype(f32).astype(bf16)
    col_ids = lax.broadcasted_iota(jnp.int32, (frames, rows), 1)
    for i, (half, k, first_row) in enumerate(pieces):
        columns = lax.dot_general(
            same,
            map_refs[half][m, :, k * frames : (k + 1) * frames].astype(bf16),
            (((1,), (1,)), ((), ())),
            preferred_element_type=f32,
        )
        here = (col_ids - first_row).astype(f32)
        for e in range(experts):
            picking[e, i * frames : (i + 1) * frames, :] = (
                (here == columns[:, e : e + 1]).astype(f32).astype(bf16)
            )

    def feature(d, carry):
        cols = pl.ds(pl.multiple_of(d * PART, PART), PART)
        acc = jnp.zeros((total, PART), f32)
        for e in range(experts):
            acc = acc + jnp.dot(picking[e], slot_refs[e][:, cols], preferred_element_type=f32)
        for group, out_ref in zip(groups, out_refs):
            for place, i in enumerate(group):
                out_ref[place * frames : (place + 1) * frames, cols] = acc[
                    i * frames : (i + 1) * frames, :
                ].astype(out_ref.dtype)
        return carry

    lax.fori_loop(0, slot_refs[0].shape[1] // PART, feature, 0)


def frame_sums(m, maps, blocks, frames, pieces, groups, earlier, handed=()):
    rows, features = blocks[0].shape
    first = 2 + len(blocks) + len(earlier)
    out = pl.pallas_call(
        functools.partial(frame_sums_body, m, len(blocks), frames, pieces, tuple(g for g, _ in groups)),
        out_shape=tuple(pltpu.HBM(h.shape, h.dtype) for h in handed)
        + tuple(
            jax.ShapeDtypeStruct((len(group) * frames, features), kind) for group, kind in groups
        ),
        in_specs=whole(2 + len(blocks)) + after(len(earlier)) + far(len(handed)),
        out_specs=tuple(far(len(handed)) + whole(len(groups))),
        input_output_aliases={first + i: i for i in range(len(handed))},
        scratch_shapes=[pltpu.VMEM((len(blocks), len(pieces) * frames, rows), bf16)],
        compiler_params=params(16),
        cost_estimate=cost(COSTS[8 + m + (len(pieces) == 1)]),
        name="frame_sums",
    )(*maps, *blocks, *earlier, *handed)
    return out[: len(handed)], out[len(handed) :]


def pair_sum_body(own_ref, got_ref, out_ref):
    first = got_ref.shape[0] - own_ref.shape[0]
    out_ref[...] = (own_ref[...] + got_ref[first:, :].astype(f32)).astype(bf16)


def pair_sum(own, got):
    return pl.pallas_call(
        pair_sum_body,
        out_shape=jax.ShapeDtypeStruct(own.shape, bf16),
        in_specs=whole(2),
        out_specs=whole(1)[0],
        compiler_params=params(16),
        cost_estimate=cost(COSTS[15]),
        name="pair_sum",
    )(own, got)


def epilogue_body(m, seqs, last, waits, *refs):
    norm_refs = refs[:seqs]
    (x_all, up_all, conv_ref, mixed_ref, scale_ref, taps_ref, gain_ref) = refs[seqs : seqs + 7]
    before, refs = refs[seqs + 7 : seqs + 7 + 2 * last], refs[seqs + 7 + 2 * last + waits :]
    if last:
        sums_ref, other_ref = before
    prev_ref, term_ref, norm_grad, pad_x, pad_g, parts, gain_parts, x_ref, up_ref, sems = refs
    if last:
        prev_ref[0] = other_ref[...]
        prev_ref = prev_ref.at[1]
    copies = fetching((x_all.at[m], up_all.at[m]), (x_ref, up_ref), sems)
    conv_ref, mixed_ref, scale_ref = conv_ref.at[m], mixed_ref.at[m], scale_ref.at[m]
    frames, features = x_ref.shape
    tap_count = taps_ref.shape[0]
    margin = tap_count // 2
    lead = round_up(margin, 8)
    pad_x[...] = jnp.zeros(pad_x.shape, f32)
    pad_g[...] = jnp.zeros(pad_g.shape, f32)
    scale = scale_ref[...]

    def tiles_sum(values):
        return jnp.sum(values.reshape(frames // 8, 8, LANES), axis=0)

    def gather(c, inner):
        cols = pl.ds(pl.multiple_of(c * LANES, LANES), LANES)
        grad = norm_refs[0][:frames, cols].astype(f32)
        for k in range(1, seqs):
            grad = grad + norm_refs[k][:frames, cols].astype(f32)
        norm_grad[:, cols] = grad
        weighed = grad * mixed_ref[:, cols]
        gain_parts[c] = tiles_sum(weighed * scale)
        return inner + weighed * gain_ref[:, cols]

    inner = lax.fori_loop(0, features // LANES, gather, jnp.zeros((frames, LANES), f32))
    for copy in copies:
        copy.wait()
    pull = scale * scale * scale * (jnp.sum(inner, axis=1, keepdims=True) / features)

    def chunk(c, carry):
        cols = pl.ds(pl.multiple_of(c * LANES, LANES), LANES)
        mixed_grad = (
            up_ref[:, cols].astype(f32)
            + scale * (norm_grad[:, cols] * gain_ref[:, cols])
            - mixed_ref[:, cols] * pull
        )
        conv_grad = mixed_grad * silu_slope(conv_ref[:, cols])
        pad_x[lead : lead + frames, :] = x_ref[:, cols].astype(f32)
        pad_g[lead : lead + frames, :] = conv_grad
        acc = mixed_grad
        for j, rows in shifted(pad_x, [lead + j - margin for j in range(tap_count)], frames):
            parts[8 * j : 8 * j + 8, :] = tiles_sum(conv_grad * rows)
        for j, rows in shifted(pad_g, [lead + margin - j for j in range(tap_count)], frames):
            acc = acc + taps_ref[j, :, cols] * rows
        prev_ref[:, cols] = acc.astype(bf16)
        parts[8 * tap_count :, :] = gain_parts[c]
        sums = parts[pl.ds(0, tap_count + 1, stride=8), :]
        for row in range(1, 8):
            sums = sums + parts[pl.ds(row, tap_count + 1, stride=8), :]
        if last:
            sums = sums + sums_ref[:, cols]
        term_ref[:, cols] = sums.astype(term_ref.dtype)
        return carry

    lax.fori_loop(0, features // LANES, chunk, 0, unroll=2)


def epilogue(m, norm_blocks, x, upstream, saved, taps, gain, before=(), earlier=()):
    _, frames, features = x.shape
    seqs = len(norm_blocks)
    lead = round_up(taps.shape[0] // 2, 8)
    last = bool(before)
    return pl.pallas_call(
        functools.partial(epilogue_body, m, seqs, last, len(earlier)),
        out_shape=(
            jax.ShapeDtypeStruct(x.shape if last else (frames, features), bf16),
            jax.ShapeDtypeStruct((taps.shape[0] + 1, features), bf16 if last else f32),
        ),
        in_specs=whole(seqs) + far(2) + whole(5 + len(before)) + after(len(earlier)),
        out_specs=tuple(whole(2)),
        scratch_shapes=[
            pltpu.VMEM((frames, features), f32),
            pltpu.VMEM((frames + 2 * lead, LANES), f32),
            pltpu.VMEM((frames + 2 * lead, LANES), f32),
            pltpu.VMEM((8 * (taps.shape[0] + 1), LANES), f32),
            pltpu.VMEM((features // LANES, 8, LANES), f32),
        ]
        + [
            pltpu.VMEM((frames, features), bf16),
            pltpu.VMEM((frames, features), bf16),
            pltpu.SemaphoreType.DMA((2,)),
        ],
        compiler_params=params(16),
        cost_estimate=cost(COSTS[11 + m]),
        name="norm_conv_back",
    )(*norm_blocks, x, upstream, *saved, taps, gain, *before, *earlier)


def tree_sum(terms):
    while len(terms) > 1:
        terms = [terms[i] + terms[i + 1] for i in range(0, len(terms), 2)]
    return terms[0]


def last_sum_body(*refs):
    term_refs, handed_ref, (taps_ref, gain_ref, out_ref, sem) = refs[:-5], refs[-5], refs[-4:]
    copy = pltpu.make_async_copy(handed_ref, out_ref, sem)
    copy.start()
    tap_count = taps_ref.shape[0]
    total = tree_sum([ref[...].astype(f32) for ref in term_refs])
    for j in range(tap_count):
        taps_ref[j] = total[j : j + 1, :]
    gain_ref[...] = total[tap_count:, :]
    copy.wait()


def last_sum(terms, handed):
    rows, features = terms[0].shape
    return pl.pallas_call(
        last_sum_body,
        out_shape=(
            jax.ShapeDtypeStruct((rows - 1, 1, features), f32),
            jax.ShapeDtypeStruct((1, features), f32),
            pltpu.HBM(handed.shape, handed.dtype),
        ),
        in_specs=whole(len(terms)) + after(1),
        out_specs=tuple(whole(2) + far(1)),
        scratch_shapes=[pltpu.SemaphoreType.DMA],
        compiler_params=params(16),
        cost_estimate=cost(COSTS[13]),
        name="last_sum",
    )(*terms, handed)


def to_partner(array, axis, k):
    return lax.ppermute(array, axis, [(i, i ^ k) for i in range(lax.axis_size(axis))])


def from_all(array, axis):
    return [array] + [to_partner(array, axis, k) for k in range(1, lax.axis_size(axis))]


def exchanged(blocks, axis):
    return [blocks[0]] + [to_partner(blocks[k], axis, k) for k in range(1, len(blocks))]


def local(section_input, out_grad, routes, combine, kernel, norm_gain, up_weight, down_weight):
    experts = lax.axis_size("expert")
    seqs = lax.axis_size("dp")
    frames, features = section_input.shape[3:]
    top_count = routes.shape[4]
    capacity = 9 * frames * top_count // (8 * experts)
    taps = kernel.transpose(1, 0, 2)
    up_mat, down_mat = up_weight[0, 0], down_weight[0, 0]
    routes = routes[0, :, 0].transpose(0, 2, 1)
    combine = combine[0, :, 0].transpose(0, 2, 1)
    xs = section_input.reshape(MB, frames, features)
    ups = out_grad.reshape(MB, frames, features)

    sent = first_send(xs, ups, routes, combine, taps, norm_gain)
    pieces = second_send(xs, ups, routes, combine, taps, norm_gain, experts, capacity, sent)
    half = round_up(seqs // 2 * capacity, 8)
    most, last = round_up((seqs - 1) * capacity, 8), round_up(capacity, 8)
    near_places = ((0, capacity), (0, capacity))
    wide_places = ((0, capacity), (2 * capacity, 0))

    first = [sent, to_partner(sent, "dp", 1)]
    near, near_map, pieces = slots(
        first, experts, capacity, frames, near_places, exchanged(pieces, "expert")
    )
    later = passed(to_partner(sent, "dp", 2), near[0])
    first += [later, to_partner(later, "dp", 1)]
    saved = saved_frames(xs, taps, first[1])
    near = exchanged(near, "expert")

    products = functools.partial(
        expert_products,
        parts=experts,
        capacity=capacity,
        up_mat=up_mat,
        down_mat=down_mat,
        total=experts * (2 * half + most + last),
    )
    at = experts * half
    back, kept = products(near, rows=half, first_row=0, before=(), kept=(), earlier=(saved[2],), stage=4)
    pieces = passed(pieces, later)
    later = passed(to_partner(pieces, "dp", 2), back[0])
    second = [pieces, to_partner(pieces, "dp", 1), later, to_partner(later, "dp", 1)]
    wide, wide_map, _ = slots(first[2:], experts, capacity, frames, wide_places)
    maps = (near_map, wide_map)
    wide = exchanged(wide, "expert")
    back, kept = products(wide, rows=half, first_row=at, before=back, kept=kept, stage=5)
    first_back = exchanged(back, "expert")
    back, kept = products(second[:-1], rows=most, first_row=2 * at, before=(), kept=kept, stage=6)
    most_back = exchanged(back, "expert")

    _, (own_sum, far_sum, sent) = frame_sums(
        0,
        maps,
        first_back,
        frames,
        ((0, 0, 0), (0, 1, 0), (1, 0, half), (1, 1, half)),
        (((0,), f32), ((2,), f32), ((1, 3), bf16)),
        [back[0]],
    )
    got = to_partner(sent, "dp", 1)
    first_norm = [own_sum, got, to_partner(pair_sum(far_sum, got), "dp", 2)]
    back, kept = products(
        second[-1:], rows=last, first_row=2 * at + experts * most, before=(), kept=kept, stage=7, earlier=(own_sum,)
    )
    last_back = exchanged(back, "expert")
    (all_in, all_grad, all_acted, all_pre), sent = frame_sums(
        1,
        maps,
        most_back,
        frames,
        ((0, 0, 0), (0, 1, 0), (1, 0, 0)),
        (((0,), f32), ((1,), bf16), ((2,), bf16)),
        [],
        kept,
    )
    second_norm = exchanged(sent, "dp")
    over_rows = (((0,), (0,)), ((), ()))
    up_grad = lax.dot_general(all_in, all_pre, over_rows, preferred_element_type=f32).astype(bf16)
    down_grad = lax.dot_general(all_acted, all_grad, over_rows, preferred_element_type=f32).astype(bf16)
    _, sent = frame_sums(1, maps, last_back, frames, ((1, 1, 0),), (((0,), bf16),), [])
    second_norm.append(to_partner(sent[0], "dp", seqs - 1))
    prev, sums = epilogue(0, first_norm, xs, ups, saved, taps, norm_gain)
    prev, sums = epilogue(1, second_norm, xs, ups, saved, taps, norm_gain, before=(sums, prev))
    peers = lax.axis_size("pipe")
    handed = lax.ppermute(prev, "pipe", [(i, (i - 1) % peers) for i in range(peers)])
    sums = tree_sum([term.astype(f32) for term in from_all(sums, "dp")]).astype(bf16)
    taps_grad, gain_grad, handed = last_sum(from_all(sums, "expert"), handed)
    return (
        handed[None, :, None],
        taps_grad.transpose(1, 0, 2),
        gain_grad,
        up_grad[None, None],
        down_grad[None, None],
    )


def solution(mesh):
    split = P("pipe", None, ("dp", "expert"), None, None)
    up_split = P("pipe", "expert", None, "dp")
    down_split = P("pipe", "expert", "dp", None)
    return jax.shard_map(
        local,
        mesh=mesh,
        in_specs=(split, split, split, split, P("pipe", None, None), P("pipe", None), up_split, down_split),
        out_specs=(split, P("pipe", None, None), P("pipe", None), up_split, down_split),
        check_vma=False,
    )
```

```python
import functools

import jax
import jax.numpy as jnp
from jax import lax
from jax.experimental import pallas as pl
from jax.experimental.pallas import tpu as pltpu
from jax.sharding import PartitionSpec as P

MB = 2
EPSILON = 1e-06
LANES = 128
TILE = 512
PART = 256
SEND_MIB = 60
EXPERT_MIB = 24
NOWHERE = -512.0
COSTS = (0, 0, 0, 0, 12, 0, 10, 0, 0, 2, 0, 0, 0, 0, 12, 0)
MIB = 1024 * 1024
SMALL = pl.CostEstimate(flops=1, bytes_accessed=1, transcendentals=0)
bf16 = jnp.bfloat16
f32 = jnp.float32


def round_up(value, step):
    return -(-value // step) * step


def params(mib):
    return pltpu.CompilerParams(vmem_limit_bytes=mib * MIB)


def cost(amount):
    return pl.CostEstimate(flops=int(amount * 1.15e9) + 1, bytes_accessed=1, transcendentals=0)


def whole(count):
    return [pl.BlockSpec(memory_space=pltpu.VMEM)] * count


def after(count):
    return [pl.BlockSpec(memory_space=pl.ANY)] * count


def far(count):
    return [pl.BlockSpec(memory_space=pltpu.HBM)] * count


def fetching(sources, targets, sems):
    copies = [
        pltpu.make_async_copy(source, target, sems.at[i])
        for i, (source, target) in enumerate(zip(sources, targets))
    ]
    for copy in copies:
        copy.start()
    return copies


def fetched(sources, targets, sems):
    for copy in fetching(sources, targets, sems):
        copy.wait()


def sigmoid(values):
    return 1.0 / (1.0 + jnp.exp(-values))


def silu_slope(values):
    gate_sig = sigmoid(values)
    return gate_sig * (1.0 + values * (1.0 - gate_sig))


def shifted(pad, starts, frames):
    for residue in range(8):
        group = [(i, start // 8) for i, start in enumerate(starts) if start % 8 == residue]
        if not group:
            continue
        low, high = min(t for _, t in group), max(t for _, t in group)
        first = 8 * low + residue
        block = pad[first : first + 8 * (high - low) + frames, :]
        for i, tile in group:
            yield i, block[8 * (tile - low) : 8 * (tile - low) + frames, :]


def mixed_frames(x_ref, taps_ref, pad, conv_ref, mixed_ref):
    frames, features = x_ref.shape
    tap_count = taps_ref.shape[0]
    margin = tap_count // 2
    lead = round_up(margin, 8)
    pad[...] = jnp.zeros(pad.shape, f32)

    def chunk(c, squares):
        cols = pl.ds(pl.multiple_of(c * LANES, LANES), LANES)
        xs = x_ref[:, cols].astype(f32)
        pad[lead : lead + frames, :] = xs
        acc = jnp.zeros((frames, LANES), f32)
        for j, rows in shifted(pad, [lead + j - margin for j in range(tap_count)], frames):
            acc = acc + taps_ref[j, :, cols] * rows
        mixed = xs + acc * sigmoid(acc)
        if conv_ref is not None:
            conv_ref[:, cols] = acc
        mixed_ref[:, cols] = mixed
        return squares + mixed * mixed

    squares = lax.fori_loop(0, features // LANES, chunk, jnp.zeros((frames, LANES), f32), unroll=4)
    return lax.rsqrt(jnp.sum(squares, axis=1, keepdims=True) / features + EPSILON)


def meta_rows(routes_ref, combine_ref, m):
    own = lax.axis_index("expert").astype(jnp.int32)
    rows = [(routes_ref[m] ^ own).astype(f32)]
    left = combine_ref[m]
    for _ in range(3):
        rows.append(left.astype(bf16).astype(f32))
        left = left - rows[-1]
    return jnp.concatenate(rows, axis=0)


def first_send_body(
    x_all, up_all, routes_all, combine_all, taps_all, gain_all, send_ref, mixed, pad, x_ref, routes_ref,
    combine_ref, taps_ref, gain_ref, sems
):
    frames = x_ref.shape[0]
    fetched(
        (x_all.at[0], up_all.at[0], routes_all, combine_all, taps_all, gain_all),
        (x_ref, send_ref.at[frames : 2 * frames], routes_ref, combine_ref, taps_ref, gain_ref),
        sems,
    )
    scale = mixed_frames(x_ref, taps_ref, pad, None, mixed)
    send_ref[:frames, :] = (mixed[...] * scale * gain_ref[...]).astype(bf16)
    metas = [meta_rows(routes_ref, combine_ref, m) for m in range(MB)]
    send_ref[2 * frames :, :frames] = jnp.concatenate(metas, axis=0).astype(bf16)


def send_scratch(x, routes, combine, taps, gain):
    _, frames, features = x.shape
    return [
        pltpu.VMEM((frames, features), f32),
        pltpu.VMEM((frames + 2 * round_up(taps.shape[0] // 2, 8), LANES), f32),
        pltpu.VMEM((frames, features), bf16),
        pltpu.VMEM(routes.shape, routes.dtype),
        pltpu.VMEM(combine.shape, f32),
        pltpu.VMEM(taps.shape, f32),
        pltpu.VMEM(gain.shape, f32),
        pltpu.SemaphoreType.DMA((6,)),
    ]


def first_send(x, upstream, routes, combine, taps, gain):
    _, frames, features = x.shape
    return pl.pallas_call(
        first_send_body,
        out_shape=jax.ShapeDtypeStruct((2 * frames + 8 * MB, features), bf16),
        in_specs=far(6),
        out_specs=whole(1)[0],
        scratch_shapes=send_scratch(x, routes, combine, taps, gain),
        compiler_params=params(SEND_MIB),
        cost_estimate=cost(COSTS[0]),
        name="first_send",
    )(x, upstream, routes, combine, taps, gain)


def second_send_body(
    experts, capacity, x_all, up_all, routes_all, combine_all, taps_all, gain_all, _, *refs
):
    outs, (mixed, pad, x_ref, routes_ref, combine_ref, taps_ref, gain_ref, sems, joined) = (
        refs[:experts],
        refs[experts:],
    )
    frames, features = x_ref.shape
    fetched(
        (x_all.at[1], up_all.at[1], routes_all, combine_all, taps_all, gain_all),
        (x_ref, joined.at[frames:], routes_ref, combine_ref, taps_ref, gain_ref),
        sems,
    )
    scale = mixed_frames(x_ref, taps_ref, pad, None, mixed)
    joined[:frames, :] = (mixed[...] * scale * gain_ref[...]).astype(bf16)
    slot, weight = slot_map(experts, frames, meta_rows(routes_ref, combine_ref, 1), (0,))
    rows = outs[0].shape[0]
    row_ids = lax.broadcasted_iota(jnp.int32, (rows, frames), 0).astype(f32)
    for e in range(experts):
        normed_row = (row_ids == slot[e : e + 1, :]).astype(f32).astype(bf16)
        chosen = (row_ids - capacity == slot[e : e + 1, :]) & (row_ids >= capacity)
        amount = jnp.sum(jnp.where(chosen, weight[e : e + 1, :], 0.0), axis=1, keepdims=True)
        grad_row = chosen.astype(f32).astype(bf16)
        for first_col in range(0, features, 512):
            cols = slice(first_col, min(first_col + 512, features))
            picked = jnp.dot(grad_row, joined[frames:, cols], preferred_element_type=f32) * amount
            picked = picked + jnp.dot(normed_row, joined[:frames, cols], preferred_element_type=f32)
            outs[e][:, cols] = picked.astype(bf16)


def second_send(x, upstream, routes, combine, taps, gain, experts, capacity, earlier):
    _, frames, features = x.shape
    rows = round_up(2 * capacity, 8)
    return pl.pallas_call(
        functools.partial(second_send_body, experts, capacity),
        out_shape=(jax.ShapeDtypeStruct((rows, features), bf16),) * experts,
        in_specs=far(6) + after(1),
        out_specs=tuple(whole(experts)),
        scratch_shapes=send_scratch(x, routes, combine, taps, gain) + [pltpu.VMEM((2 * frames, features), bf16)],
        compiler_params=params(SEND_MIB),
        cost_estimate=cost(COSTS[14]),
        name="second_send",
    )(x, upstream, routes, combine, taps, gain, earlier)


def saved_body(x_ref, taps_ref, _, conv_ref, mixed_ref, scale_ref, pad):
    for m in range(MB):
        scale_ref[m] = mixed_frames(x_ref.at[m], taps_ref, pad, conv_ref.at[m], mixed_ref.at[m])


def saved_frames(x, taps, earlier):
    lead = round_up(taps.shape[0] // 2, 8)
    return pl.pallas_call(
        saved_body,
        out_shape=(
            jax.ShapeDtypeStruct(x.shape, f32),
            jax.ShapeDtypeStruct(x.shape, f32),
            jax.ShapeDtypeStruct(x.shape[:2] + (1,), f32),
        ),
        in_specs=whole(2) + after(1),
        out_specs=tuple(whole(3)),
        scratch_shapes=[pltpu.VMEM((x.shape[1] + 2 * lead, LANES), f32)],
        compiler_params=params(16),
        cost_estimate=cost(COSTS[1]),
        name="saved_frames",
    )(x, taps, earlier)


def passed_body(*refs):
    pass


def passed(array, earlier):
    return pl.pallas_call(
        passed_body,
        out_shape=jax.ShapeDtypeStruct(array.shape, array.dtype),
        in_specs=after(2),
        out_specs=after(1)[0],
        input_output_aliases={0: 0},
        compiler_params=params(16),
        cost_estimate=SMALL,
        name="passed",
    )(array, earlier)


def slot_map(experts, frames, meta, places):
    total = meta.shape[1]
    padded = round_up(experts, 16)
    named = lax.broadcasted_iota(jnp.int32, (padded, total), 0).astype(f32)
    first, second = meta[0:1, :] == named, meta[1:2, :] == named
    member = first | second
    earlier = lax.broadcasted_iota(jnp.int32, (total, total), 0)
    later = lax.broadcasted_iota(jnp.int32, (total, total), 1)
    before = (earlier < later) & (earlier // frames == later // frames)
    rank = jnp.dot(
        member.astype(f32).astype(bf16),
        before.astype(f32).astype(bf16),
        preferred_element_type=f32,
    )
    seq_of = lax.broadcasted_iota(jnp.int32, (padded, total), 1) // frames
    for k, first_row in enumerate(places):
        rank = jnp.where(seq_of == k, rank + first_row, rank)
    slot = jnp.where(member, rank, NOWHERE)
    first_weight = meta[2:3, :] + meta[4:5, :] + meta[6:7, :]
    second_weight = meta[3:4, :] + meta[5:6, :] + meta[7:8, :]
    weight = jnp.where(first, first_weight, 0.0) + jnp.where(second, second_weight, 0.0)
    return slot, weight


def place(slot, weight, joined, out_ref, first_row, rows):
    row_ids = lax.broadcasted_iota(jnp.int32, (rows, slot.shape[1]), 0).astype(f32)
    chosen = row_ids == slot
    placing = chosen.astype(f32).astype(bf16)
    if weight is not None:
        amount = jnp.sum(jnp.where(chosen, weight, 0.0), axis=1, keepdims=True)
    for first_col in range(0, joined.shape[1], 512):
        cols = slice(first_col, min(first_col + 512, joined.shape[1]))
        picked = jnp.dot(placing, joined[:, cols], preferred_element_type=f32)
        if weight is not None:
            picked = picked * amount
        out_ref[first_row : first_row + rows, cols] = picked.astype(bf16)


def slots_body(experts, frames, places, seqs, waits, *refs):
    block_refs, refs = refs[:seqs], refs[seqs + waits :]
    piece_refs, refs = refs[: len(refs) - experts - 3], refs[len(refs) - experts - 3 :]
    if piece_refs:
        piece_refs, stacked, refs = piece_refs[:-1], piece_refs[-1], refs
        for i, ref in enumerate(piece_refs):
            stacked[i] = ref[...]
    out_refs, (slot_ref, joined, meta) = refs[:experts], refs[experts:]
    total = seqs * frames
    for k in range(seqs):
        here = slice(k * frames, (k + 1) * frames)
        joined[here, :] = block_refs[k][:frames, :]
        joined[total + k * frames : total + (k + 1) * frames, :] = block_refs[k][frames : 2 * frames, :]
        meta[:, here] = block_refs[k][2 * frames :, :frames].astype(f32)
    slot, weight = slot_map(experts, frames, meta[:8, :], places[0])
    slot_ref[0] = slot
    slot_ref[1] = slot_map(experts, frames, meta[8:, :], places[1])[0]
    rows = out_refs[0].shape[0] // 2
    for e in range(experts):
        place(slot[e : e + 1, :], None, joined.at[:total], out_refs[e], 0, rows)
        place(slot[e : e + 1, :], weight[e : e + 1, :], joined.at[total:], out_refs[e], rows, rows)


def slots(blocks, experts, capacity, frames, places, pieces=(), earlier=()):
    features = blocks[0].shape[1]
    seqs = len(blocks)
    rows = round_up(seqs * capacity, 8)
    total = seqs * frames
    together = tuple(jax.ShapeDtypeStruct((len(pieces),) + p.shape, bf16) for p in pieces[:1])
    out = pl.pallas_call(
        functools.partial(slots_body, experts, frames, places, seqs, len(earlier)),
        out_shape=together
        + tuple(jax.ShapeDtypeStruct((2 * rows, features), bf16) for _ in range(experts))
        + (jax.ShapeDtypeStruct((MB, round_up(experts, 16), total), f32),),
        in_specs=whole(seqs) + after(len(earlier)) + whole(len(pieces)),
        out_specs=tuple(whole(len(together) + experts + 1)),
        scratch_shapes=[pltpu.VMEM((2 * total, features), bf16), pltpu.VMEM((8 * MB, total), f32)],
        compiler_params=params(16),
        cost_estimate=cost(COSTS[2 + (not pieces)]),
        name="slots",
    )(*blocks, *earlier, *pieces)
    return out[-1 - experts : -1], out[-1], out[0]


def expert_body(parts, rows, capacity, first_row, counts, *refs):
    cuts = [sum(counts[:i]) for i in range(len(counts) + 1)]
    in_refs, (up_mat, down_mat), before_refs, _, _, slot_refs, kept_far, scratch = (
        refs[cuts[i] : cuts[i + 1]] for i in range(len(counts))
    )
    rows_in, rows_grad, acted, kept, put_sems = scratch
    features, hidden = up_mat.shape
    steps = hidden // TILE
    far_outs = [ref.at[first_row : first_row + parts * rows, :] for ref in kept_far]

    def putting(h):
        cols = pl.ds(pl.multiple_of(h * TILE, TILE), TILE)
        return (
            pltpu.make_async_copy(acted.at[:, cols], far_outs[2].at[:, cols], put_sems.at[0, h]),
            pltpu.make_async_copy(kept.at[:, cols], far_outs[3].at[:, cols], put_sems.at[1, h]),
        )

    row_puts = [
        pltpu.make_async_copy(rows_in, far_outs[0], put_sems.at[2, 0]),
        pltpu.make_async_copy(rows_grad, far_outs[1], put_sems.at[2, 1]),
    ]
    for j in range(parts):
        here = slice(j * rows, (j + 1) * rows)
        if capacity is None:
            rows_in[here, :] = in_refs[j][:rows, :]
            rows_grad[here, :] = in_refs[j][rows:, :]
            continue
        seqs, size = len(in_refs), in_refs[0].shape[1]
        pieces = jnp.concatenate([ref[j] for ref in in_refs], axis=0)
        row = lax.broadcasted_iota(jnp.int32, (rows, seqs * size), 0)
        source = lax.broadcasted_iota(jnp.int32, (rows, seqs * size), 1)
        wanted = (row // capacity) * size + row % capacity
        wanted = jnp.where(row < seqs * capacity, wanted, -2 * size)
        for target, first in ((rows_in, 0), (rows_grad, capacity)):
            moving = (source == wanted + first).astype(f32).astype(bf16)
            target[here, :] = jnp.dot(moving, pieces, preferred_element_type=f32).astype(bf16)
    for copy in row_puts:
        copy.start()

    def forward(h, carry):
        for first in range(0, TILE, PART):
            cols = pl.ds(pl.multiple_of(h * TILE + first, PART), PART)
            pre_act = jnp.dot(rows_in[...], up_mat[:, cols], preferred_element_type=f32)
            act_grad = lax.dot_general(
                rows_grad[...], down_mat[cols, :], (((1,), (1,)), ((), ())), preferred_element_type=f32
            )
            gate_sig = sigmoid(pre_act)
            acted[:, cols] = (pre_act * gate_sig).astype(bf16)
            slope = gate_sig * (1.0 + pre_act * (1.0 - gate_sig))
            kept[:, cols] = (act_grad * slope).astype(bf16)
        for copy in putting(h):
            copy.start()
        return carry

    lax.fori_loop(0, steps, forward, 0)
    own_row = slot_refs[0].shape[0] - rows
    if before_refs:
        for j in range(parts):
            slot_refs[j][:own_row, :] = before_refs[j][...]

    def backward(d, carry):
        for first in range(0, TILE, PART):
            cols = pl.ds(pl.multiple_of(d * TILE + first, PART), PART)
            term = lax.dot_general(
                kept[...], up_mat[cols, :], (((1,), (1,)), ((), ())), preferred_element_type=f32
            )
            for j in range(parts):
                slot_refs[j][own_row:, cols] = term[j * rows : (j + 1) * rows, :].astype(bf16)
        return carry

    lax.fori_loop(0, features // TILE, backward, 0)
    for copy in row_puts:
        copy.wait()
    for h in range(steps):
        for copy in putting(h):
            copy.wait()


def expert_products(blocks, parts, capacity, up_mat, down_mat, rows, total, first_row, before, kept, earlier=(), stage=4):
    features, hidden = up_mat.shape
    steps = hidden // TILE
    mine = parts * rows
    slot_rows = rows + (before[0].shape[0] if before else 0)
    counts = (len(blocks), 2, len(before), len(earlier), len(kept), parts, 4, 5)
    first_kept = sum(counts[:4])
    out = pl.pallas_call(
        functools.partial(
            expert_body, parts, rows, capacity if blocks[0].ndim == 3 else None, first_row, counts
        ),
        out_shape=tuple(jax.ShapeDtypeStruct((slot_rows, features), bf16) for _ in range(parts))
        + (
            pltpu.HBM((total, features), bf16),
            pltpu.HBM((total, features), bf16),
            pltpu.HBM((total, hidden), bf16),
            pltpu.HBM((total, hidden), bf16),
        ),
        in_specs=whole(len(blocks) + 2 + len(before)) + after(len(earlier)) + far(len(kept)),
        out_specs=tuple(whole(parts) + far(4)),
        input_output_aliases={first_kept + i: parts + i for i in range(len(kept))},
        scratch_shapes=[
            pltpu.VMEM((mine, features), bf16),
            pltpu.VMEM((mine, features), bf16),
            pltpu.VMEM((mine, hidden), bf16),
            pltpu.VMEM((mine, hidden), bf16),
            pltpu.SemaphoreType.DMA((3, max(2, steps))),
        ],
        compiler_params=params(EXPERT_MIB),
        cost_estimate=cost(COSTS[stage]),
        name="expert_products",
    )(*blocks, up_mat, down_mat, *before, *earlier, *kept)
    return out[:parts], out[parts:]


def frame_sums_body(m, experts, frames, pieces, groups, *refs):
    map_refs, slot_refs, out_refs, picking = refs[:2], refs[2 : 2 + experts], refs[-1 - len(groups) : -1], refs[-1]
    total = len(pieces) * frames
    rows = slot_refs[0].shape[0]
    same = lax.broadcasted_iota(jnp.int32, (frames, frames), 0) == lax.broadcasted_iota(
        jnp.int32, (frames, frames), 1
    )
    same = same.astype(f32).astype(bf16)
    col_ids = lax.broadcasted_iota(jnp.int32, (frames, rows), 1)
    for i, (half, k, first_row) in enumerate(pieces):
        columns = lax.dot_general(
            same,
            map_refs[half][m, :, k * frames : (k + 1) * frames].astype(bf16),
            (((1,), (1,)), ((), ())),
            preferred_element_type=f32,
        )
        here = (col_ids - first_row).astype(f32)
        for e in range(experts):
            picking[e, i * frames : (i + 1) * frames, :] = (
                (here == columns[:, e : e + 1]).astype(f32).astype(bf16)
            )

    def feature(d, carry):
        cols = pl.ds(pl.multiple_of(d * PART, PART), PART)
        acc = jnp.zeros((total, PART), f32)
        for e in range(experts):
            acc = acc + jnp.dot(picking[e], slot_refs[e][:, cols], preferred_element_type=f32)
        for group, out_ref in zip(groups, out_refs):
            for place, i in enumerate(group):
                out_ref[place * frames : (place + 1) * frames, cols] = acc[
                    i * frames : (i + 1) * frames, :
                ].astype(out_ref.dtype)
        return carry

    lax.fori_loop(0, slot_refs[0].shape[1] // PART, feature, 0)


def frame_sums(m, maps, blocks, frames, pieces, groups, earlier, handed=()):
    rows, features = blocks[0].shape
    first = 2 + len(blocks) + len(earlier)
    out = pl.pallas_call(
        functools.partial(frame_sums_body, m, len(blocks), frames, pieces, tuple(g for g, _ in groups)),
        out_shape=tuple(pltpu.HBM(h.shape, h.dtype) for h in handed)
        + tuple(
            jax.ShapeDtypeStruct((len(group) * frames, features), kind) for group, kind in groups
        ),
        in_specs=whole(2 + len(blocks)) + after(len(earlier)) + far(len(handed)),
        out_specs=tuple(far(len(handed)) + whole(len(groups))),
        input_output_aliases={first + i: i for i in range(len(handed))},
        scratch_shapes=[pltpu.VMEM((len(blocks), len(pieces) * frames, rows), bf16)],
        compiler_params=params(16),
        cost_estimate=cost(COSTS[8 + m + (len(pieces) == 1)]),
        name="frame_sums",
    )(*maps, *blocks, *earlier, *handed)
    return out[: len(handed)], out[len(handed) :]


def pair_sum_body(own_ref, got_ref, out_ref):
    first = got_ref.shape[0] - own_ref.shape[0]
    out_ref[...] = (own_ref[...] + got_ref[first:, :].astype(f32)).astype(bf16)


def pair_sum(own, got):
    return pl.pallas_call(
        pair_sum_body,
        out_shape=jax.ShapeDtypeStruct(own.shape, bf16),
        in_specs=whole(2),
        out_specs=whole(1)[0],
        compiler_params=params(16),
        cost_estimate=cost(COSTS[15]),
        name="pair_sum",
    )(own, got)


def epilogue_body(m, seqs, last, waits, *refs):
    norm_refs = refs[:seqs]
    (x_all, up_all, conv_ref, mixed_ref, scale_ref, taps_ref, gain_ref) = refs[seqs : seqs + 7]
    before, refs = refs[seqs + 7 : seqs + 7 + 2 * last], refs[seqs + 7 + 2 * last + waits :]
    if last:
        sums_ref, other_ref = before
    prev_ref, term_ref, norm_grad, pad_x, pad_g, parts, gain_parts, x_ref, up_ref, sems = refs
    if last:
        prev_ref[0] = other_ref[...]
        prev_ref = prev_ref.at[1]
    copies = fetching((x_all.at[m], up_all.at[m]), (x_ref, up_ref), sems)
    conv_ref, mixed_ref, scale_ref = conv_ref.at[m], mixed_ref.at[m], scale_ref.at[m]
    frames, features = x_ref.shape
    tap_count = taps_ref.shape[0]
    margin = tap_count // 2
    lead = round_up(margin, 8)
    pad_x[...] = jnp.zeros(pad_x.shape, f32)
    pad_g[...] = jnp.zeros(pad_g.shape, f32)
    scale = scale_ref[...]

    def tiles_sum(values):
        return jnp.sum(values.reshape(frames // 8, 8, LANES), axis=0)

    def gather(c, inner):
        cols = pl.ds(pl.multiple_of(c * LANES, LANES), LANES)
        grad = norm_refs[0][:frames, cols].astype(f32)
        for k in range(1, seqs):
            grad = grad + norm_refs[k][:frames, cols].astype(f32)
        norm_grad[:, cols] = grad
        weighed = grad * mixed_ref[:, cols]
        gain_parts[c] = tiles_sum(weighed * scale)
        return inner + weighed * gain_ref[:, cols]

    inner = lax.fori_loop(0, features // LANES, gather, jnp.zeros((frames, LANES), f32), unroll=4)
    for copy in copies:
        copy.wait()
    pull = scale * scale * scale * (jnp.sum(inner, axis=1, keepdims=True) / features)

    def chunk(c, carry):
        cols = pl.ds(pl.multiple_of(c * LANES, LANES), LANES)
        mixed_grad = (
            up_ref[:, cols].astype(f32)
            + scale * (norm_grad[:, cols] * gain_ref[:, cols])
            - mixed_ref[:, cols] * pull
        )
        conv_grad = mixed_grad * silu_slope(conv_ref[:, cols])
        pad_x[lead : lead + frames, :] = x_ref[:, cols].astype(f32)
        pad_g[lead : lead + frames, :] = conv_grad
        acc = mixed_grad
        for j, rows in shifted(pad_x, [lead + j - margin for j in range(tap_count)], frames):
            parts[8 * j : 8 * j + 8, :] = tiles_sum(conv_grad * rows)
        for j, rows in shifted(pad_g, [lead + margin - j for j in range(tap_count)], frames):
            acc = acc + taps_ref[j, :, cols] * rows
        prev_ref[:, cols] = acc.astype(bf16)
        parts[8 * tap_count :, :] = gain_parts[c]
        sums = parts[pl.ds(0, tap_count + 1, stride=8), :]
        for row in range(1, 8):
            sums = sums + parts[pl.ds(row, tap_count + 1, stride=8), :]
        if last:
            sums = sums + sums_ref[:, cols]
        term_ref[:, cols] = sums.astype(term_ref.dtype)
        return carry

    lax.fori_loop(0, features // LANES, chunk, 0, unroll=4)


def epilogue(m, norm_blocks, x, upstream, saved, taps, gain, before=(), earlier=()):
    _, frames, features = x.shape
    seqs = len(norm_blocks)
    lead = round_up(taps.shape[0] // 2, 8)
    last = bool(before)
    return pl.pallas_call(
        functools.partial(epilogue_body, m, seqs, last, len(earlier)),
        out_shape=(
            jax.ShapeDtypeStruct(x.shape if last else (frames, features), bf16),
            jax.ShapeDtypeStruct((taps.shape[0] + 1, features), bf16 if last else f32),
        ),
        in_specs=whole(seqs) + far(2) + whole(5 + len(before)) + after(len(earlier)),
        out_specs=tuple(whole(2)),
        scratch_shapes=[
            pltpu.VMEM((frames, features), f32),
            pltpu.VMEM((frames + 2 * lead, LANES), f32),
            pltpu.VMEM((frames + 2 * lead, LANES), f32),
            pltpu.VMEM((8 * (taps.shape[0] + 1), LANES), f32),
            pltpu.VMEM((features // LANES, 8, LANES), f32),
        ]
        + [
            pltpu.VMEM((frames, features), bf16),
            pltpu.VMEM((frames, features), bf16),
            pltpu.SemaphoreType.DMA((2,)),
        ],
        compiler_params=params(16),
        cost_estimate=cost(COSTS[11 + m]),
        name="norm_conv_back",
    )(*norm_blocks, x, upstream, *saved, taps, gain, *before, *earlier)


def tree_sum(terms):
    while len(terms) > 1:
        terms = [terms[i] + terms[i + 1] for i in range(0, len(terms), 2)]
    return terms[0]


def last_sum_body(*refs):
    term_refs, handed_ref, (taps_ref, gain_ref, out_ref, sem) = refs[:-5], refs[-5], refs[-4:]
    copy = pltpu.make_async_copy(handed_ref, out_ref, sem)
    copy.start()
    tap_count = taps_ref.shape[0]
    total = tree_sum([ref[...].astype(f32) for ref in term_refs])
    for j in range(tap_count):
        taps_ref[j] = total[j : j + 1, :]
    gain_ref[...] = total[tap_count:, :]
    copy.wait()


def last_sum(terms, handed):
    rows, features = terms[0].shape
    return pl.pallas_call(
        last_sum_body,
        out_shape=(
            jax.ShapeDtypeStruct((rows - 1, 1, features), f32),
            jax.ShapeDtypeStruct((1, features), f32),
            pltpu.HBM(handed.shape, handed.dtype),
        ),
        in_specs=whole(len(terms)) + after(1),
        out_specs=tuple(whole(2) + far(1)),
        scratch_shapes=[pltpu.SemaphoreType.DMA],
        compiler_params=params(16),
        cost_estimate=cost(COSTS[13]),
        name="last_sum",
    )(*terms, handed)


def to_partner(array, axis, k):
    return lax.ppermute(array, axis, [(i, i ^ k) for i in range(lax.axis_size(axis))])


def from_all(array, axis):
    return [array] + [to_partner(array, axis, k) for k in range(1, lax.axis_size(axis))]


def exchanged(blocks, axis):
    return [blocks[0]] + [to_partner(blocks[k], axis, k) for k in range(1, len(blocks))]


def local(section_input, out_grad, routes, combine, kernel, norm_gain, up_weight, down_weight):
    experts = lax.axis_size("expert")
    seqs = lax.axis_size("dp")
    frames, features = section_input.shape[3:]
    top_count = routes.shape[4]
    capacity = 9 * frames * top_count // (8 * experts)
    taps = kernel.transpose(1, 0, 2)
    up_mat, down_mat = up_weight[0, 0], down_weight[0, 0]
    routes = routes[0, :, 0].transpose(0, 2, 1)
    combine = combine[0, :, 0].transpose(0, 2, 1)
    xs = section_input.reshape(MB, frames, features)
    ups = out_grad.reshape(MB, frames, features)

    sent = first_send(xs, ups, routes, combine, taps, norm_gain)
    pieces = second_send(xs, ups, routes, combine, taps, norm_gain, experts, capacity, sent)
    half = round_up(seqs // 2 * capacity, 8)
    most, last = round_up((seqs - 1) * capacity, 8), round_up(capacity, 8)
    near_places = ((0, capacity), (0, capacity))
    wide_places = ((0, capacity), (2 * capacity, 0))

    first = [sent, to_partner(sent, "dp", 1)]
    near, near_map, pieces = slots(
        first, experts, capacity, frames, near_places, exchanged(pieces, "expert")
    )
    later = passed(to_partner(sent, "dp", 2), near[0])
    first += [later, to_partner(later, "dp", 1)]
    saved = saved_frames(xs, taps, first[1])
    near = exchanged(near, "expert")

    products = functools.partial(
        expert_products,
        parts=experts,
        capacity=capacity,
        up_mat=up_mat,
        down_mat=down_mat,
        total=experts * (2 * half + most + last),
    )
    at = experts * half
    back, kept = products(near, rows=half, first_row=0, before=(), kept=(), earlier=(saved[2],), stage=4)
    pieces = passed(pieces, later)
    later = passed(to_partner(pieces, "dp", 2), back[0])
    second = [pieces, to_partner(pieces, "dp", 1), later, to_partner(later, "dp", 1)]
    wide, wide_map, _ = slots(first[2:], experts, capacity, frames, wide_places)
    maps = (near_map, wide_map)
    wide = exchanged(wide, "expert")
    back, kept = products(wide, rows=half, first_row=at, before=back, kept=kept, stage=5)
    first_back = exchanged(back, "expert")
    back, kept = products(second[:-1], rows=most, first_row=2 * at, before=(), kept=kept, stage=6)
    most_back = exchanged(back, "expert")

    _, (own_sum, far_sum, sent) = frame_sums(
        0,
        maps,
        first_back,
        frames,
        ((0, 0, 0), (0, 1, 0), (1, 0, half), (1, 1, half)),
        (((0,), f32), ((2,), f32), ((1, 3), bf16)),
        [back[0]],
    )
    got = to_partner(sent, "dp", 1)
    first_norm = [own_sum, got, to_partner(pair_sum(far_sum, got), "dp", 2)]
    back, kept = products(
        second[-1:], rows=last, first_row=2 * at + experts * most, before=(), kept=kept, stage=7, earlier=(own_sum,)
    )
    last_back = exchanged(back, "expert")
    (all_in, all_grad, all_acted, all_pre), sent = frame_sums(
        1,
        maps,
        most_back,
        frames,
        ((0, 0, 0), (0, 1, 0), (1, 0, 0)),
        (((0,), f32), ((1,), bf16), ((2,), bf16)),
        [],
        kept,
    )
    second_norm = exchanged(sent, "dp")
    over_rows = (((0,), (0,)), ((), ()))
    up_grad = lax.dot_general(all_in, all_pre, over_rows, preferred_element_type=f32).astype(bf16)
    down_grad = lax.dot_general(all_acted, all_grad, over_rows, preferred_element_type=f32).astype(bf16)
    _, sent = frame_sums(1, maps, last_back, frames, ((1, 1, 0),), (((0,), bf16),), [])
    second_norm.append(to_partner(sent[0], "dp", seqs - 1))
    prev, sums = epilogue(0, first_norm, xs, ups, saved, taps, norm_gain)
    prev, sums = epilogue(1, second_norm, xs, ups, saved, taps, norm_gain, before=(sums, prev))
    peers = lax.axis_size("pipe")
    handed = lax.ppermute(prev, "pipe", [(i, (i - 1) % peers) for i in range(peers)])
    sums = tree_sum([term.astype(f32) for term in from_all(sums, "dp")]).astype(bf16)
    taps_grad, gain_grad, handed = last_sum(from_all(sums, "expert"), handed)
    return (
        handed[None, :, None],
        taps_grad.transpose(1, 0, 2),
        gain_grad,
        up_grad[None, None],
        down_grad[None, None],
    )


def solution(mesh):
    split = P("pipe", None, ("dp", "expert"), None, None)
    up_split = P("pipe", "expert", None, "dp")
    down_split = P("pipe", "expert", "dp", None)
    return jax.shard_map(
        local,
        mesh=mesh,
        in_specs=(split, split, split, split, P("pipe", None, None), P("pipe", None), up_split, down_split),
        out_specs=(split, P("pipe", None, None), P("pipe", None), up_split, down_split),
        check_vma=False,
    )
```
